32 devices in a mesh: dp: 16 (over z, x, core), grp: 2 (over y).
Axes of the slice: x: 2, y: 2, z: 4, core: 2. Of those that a mesh axis runs over, the one named last changes fastest.
Arguments:
- pixels: bfloat16 [1024, 16, 16, 768], P('dp', 'grp'), may hold values from -2.5 to 2.5
- frame_bounds: int32 [1024, 2], P('dp'), may hold values from 96 to 256, as said below
- clip_frames: int32 [256], replicated, may hold values from 1 to 17, 1024 in all
- codes: int32 [1024, 16, 16], P('dp', 'grp'), may hold values from 0 to 63999
- projections: float32 [2, 768, 256], P(None, 'dp'), may hold values from -0.21875 to 0.21875
- blocks: float32 [4, 256, 256], P(None, 'dp'), may hold values from -0.375 to 0.375
- fsq_maps: float32 [2, 256, 6], P(None, 'dp'), may hold values from -0.6 to 0.6
- gains: float32 [2, 256], P(None, 'dp'), may hold values from 0.5 to 1.5
- disc_first: float32 [48, 64], P(None, 'dp'), may hold values from -0.875 to 0.875
- disc_mid: float32 [2048, 128], P('dp'), may hold values from -0.25 to 0.25
- disc_last: float32 [128, 256], P(None, 'dp'), may hold values from -1 to 1
- disc_head: float32 [256], P('dp'), may hold values from -0.25 to 0.25
- moment_projections: float32 [2, 768, 256], P(None, 'dp'), may hold values from -7.8125e-07 to 7.8125e-07
- moment_blocks: float32 [4, 256, 256], P(None, 'dp'), may hold values from -7.8125e-07 to 7.8125e-07
- moment_fsq_maps: float32 [2, 256, 6], P(None, 'dp'), may hold values from -2.2097087e-05 to 2.2097087e-05
- moment_gains: float32 [2, 256], P(None, 'dp'), may hold values from -1.171875e-05 to 1.171875e-05
- moment_disc_first: float32 [48, 64], P(None, 'dp'), may hold values from -0.0015 to 0.0015
- moment_disc_mid: float32 [2048, 128], P('dp'), may hold values from -0.0015 to 0.0015
- moment_disc_last: float32 [128, 256], P(None, 'dp'), may hold values from -0.0015 to 0.0015
- moment_disc_head: float32 [256], P('dp'), may hold values from -0.006 to 0.006
- square_projections: float32 [2, 768, 256], P(None, 'dp'), may hold values from 3.8146973e-13 to 1.5258789e-12
- square_blocks: float32 [4, 256, 256], P(None, 'dp'), may hold values from 3.8146973e-13 to 1.5258789e-12
- square_fsq_maps: float32 [2, 256, 6], P(None, 'dp'), may hold values from 5.859375e-11 to 9.765625e-10
- square_gains: float32 [2, 256], P(None, 'dp'), may hold values from 9.155274e-11 to 3.0517577e-10
- square_disc_first: float32 [48, 64], P(None, 'dp'), may hold values from 3e-07 to 5e-06
- square_disc_mid: float32 [2048, 128], P('dp'), may hold values from 3e-07 to 5e-06
- square_disc_last: float32 [128, 256], P(None, 'dp'), may hold values from 3e-07 to 5e-06
- square_disc_head: float32 [256], P('dp'), may hold values from 5e-06 to 8e-05
Outputs:
- new_moment_projections: float32 [2, 768, 256], P(None, 'dp')
- new_moment_blocks: float32 [4, 256, 256], P(None, 'dp')
- new_moment_fsq_maps: float32 [2, 256, 6], P(None, 'dp')
- new_moment_gains: float32 [2, 256], P(None, 'dp')
- new_moment_disc_first: float32 [48, 64], P(None, 'dp')
- new_moment_disc_mid: float32 [2048, 128], P('dp')
- new_moment_disc_last: float32 [128, 256], P(None, 'dp')
- new_moment_disc_head: float32 [256], P('dp')
- new_square_projections: float32 [2, 768, 256], P(None, 'dp')
- new_square_blocks: float32 [4, 256, 256], P(None, 'dp')
- new_square_fsq_maps: float32 [2, 256, 6], P(None, 'dp')
- new_square_gains: float32 [2, 256], P(None, 'dp')
- new_square_disc_first: float32 [48, 64], P(None, 'dp')
- new_square_disc_mid: float32 [2048, 128], P('dp')
- new_square_disc_last: float32 [128, 256], P(None, 'dp')
- new_square_disc_head: float32 [256], P('dp')
- new_projections: float32 [2, 768, 256], P(None, 'dp')
- new_blocks: float32 [4, 256, 256], P(None, 'dp')
- new_fsq_maps: float32 [2, 256, 6], P(None, 'dp')
- new_gains: float32 [2, 256], P(None, 'dp')
- new_disc_first: float32 [48, 64], P(None, 'dp')
- new_disc_mid: float32 [2048, 128], P('dp')
- new_disc_last: float32 [128, 256], P(None, 'dp')
- new_disc_head: float32 [256], P('dp')
- loss_terms: float32 [2], replicated
- adversarial_sums: float32 [2], replicated
- perplexity: float32 [], replicated
The draws below stay inside these ranges and needn't reach their ends.
Inputs may be any that keep to these rules, and one draw needn't show every extreme that they name: `frame_bounds`: height and width bounds of a valid top-left rectangle; some frame has both at 256.
All inputs are finite; a program needn't handle non-finite values.
Results may differ from the reference program's by a relative error of at most 0.0019.
The reference program's roundings to bfloat16 on the way count: a program that leaves them out, or rounds other values in their place, can miss the bound.
Values may be sent and summed in bfloat16 or wider, within the bound.
No kernel may reach another device: no remote copies, remote signals or barrier semaphores. Data moves between devices by JAX's collectives and lax.ppermute only.
A program may use at most 896 MiB of HBM per device.

```python
import math
import jax
import jax.numpy as jnp
import numpy as np
from jax import lax

C = 256
PIX = 768
DA = 64
DB = 128
DC = 256
CODES = 64000
STEP = 10
FRAMES = 1024
CLIPS = 256


def draw_frame_bounds(key, part):
    height_key, width_key = jax.random.split(jax.random.fold_in(key, 7))
    frame_index = jnp.arange(FRAMES, dtype=jnp.int32)
    final_frame = max(FRAMES - 1, 1)
    height = jnp.minimum(256, 192 + jax.random.randint(height_key, (FRAMES,), 0, 64) + 64 * frame_index // final_frame)
    width = jnp.minimum(256, 96 + jax.random.randint(width_key, (FRAMES,), 0, 32) + 176 * frame_index // final_frame)
    return jnp.stack([height, width], axis=1).astype(jnp.int32)


def draw_disc_head(key, part):
    key = jax.random.fold_in(key, 11)
    size_key, order_key = jax.random.split(key)
    groups = DC // 16
    negative = (groups * 5 + 7) // 8
    order = jax.random.permutation(order_key, groups)
    signs = jnp.where(order < negative, -1.0, 1.0).astype(jnp.float32)
    sizes = jax.random.uniform(size_key, (DC,), jnp.float32, 2.0, 4.0) * DC ** (-0.5)
    return (jnp.repeat(signs, 16) * sizes).astype(jnp.float32)


def with_ends(entries, own_key, smallest, largest):
    extent = entries.shape
    index_at = [jax.random.randint(jax.random.fold_in(own_key, axis), (), 0, extent[axis]) for axis in range(len(extent))]
    entries = entries.at[tuple(index_at)].set(smallest)
    longest = extent.index(max(extent))
    index_at[longest] = (index_at[longest] + 1) % extent[longest]
    return entries.at[tuple(index_at)].set(largest)


def shard_levels(stream_key, extent, pieces, low, top_value):
    loudness = 1.0
    for axis_at, blocks in pieces:
        draws = jax.random.uniform(jax.random.fold_in(jax.random.fold_in(stream_key, 6), axis_at), (blocks,), jnp.float32, low / len(pieces), top_value / len(pieces))
        loudness = loudness * jnp.repeat(jnp.exp(draws), extent[axis_at] // blocks).reshape((-1,) + (1,) * (len(extent) - 1 - axis_at))
    return loudness


def rank_table(number_of, skew):
    weights = [(1 << 20) // math.isqrt(rank ** skew) + 1 for rank in range(1, number_of + 1)]
    spread = 1 + sum(weights) // (1 << 30)
    return np.cumsum(np.array([max(1, weight // spread) for weight in weights]))


def ranked_ids(key, extent, number_of, skew):
    listing = rank_table(number_of, skew)
    lot = jax.random.randint(jax.random.fold_in(key, 1), extent, 0, int(listing[number_of - 1]))
    standing = jnp.searchsorted(jnp.asarray(listing, jnp.int32), lot, side="right")
    return jax.random.permutation(jax.random.fold_in(key, 2), number_of)[standing].astype(jnp.int32)


def profile(number_of, total, most, slope):
    loads = [(1 << 20) // math.isqrt(grade ** slope) + 1 for grade in range(2, number_of + 1)]
    rest, holding = total - most - (number_of - 1), [1] * (number_of - 1)
    while rest > 0:
        candidates = [i for i in range(number_of - 1) if holding[i] < most]
        mass, remaining = sum([loads[i] for i in candidates]), rest
        for i in candidates:
            more = min(most - holding[i], max(1, remaining * loads[i] // mass), rest)
            holding[i] = holding[i] + more
            rest = rest - more
    return np.array([most] + holding)


def ragged_sizes(rng, count, total, reach, slope):
    if count == 2:
        one = jax.random.randint(rng, (), max(1, total - reach), min(reach, total - 1) + 1)
        return jnp.stack([one, total - one])
    lengths = jnp.asarray(profile(count, total, reach, slope), jnp.int32)
    twos = (count - 1) // 2
    donor, taker = lengths[1:1 + 2 * twos:2], lengths[2:2 + 2 * twos:2]
    slack = jnp.minimum(donor - 1, reach - taker)
    passed = jax.random.randint(jax.random.fold_in(rng, 1), (twos,), 0, 1 << 20) % (slack + 1)
    lengths = lengths.at[1:1 + 2 * twos:2].set(donor - passed).at[2:2 + 2 * twos:2].set(taker + passed)
    return lengths[jax.random.permutation(jax.random.fold_in(rng, 2), count)]


def centred(rng, extent, scale, most, cuts=(), held_as=jnp.bfloat16):
    loudness = shard_levels(rng, extent, cuts, -0.22, 0.18) if cuts else 1.0
    result = jax.random.normal(rng, extent, jnp.float32) * scale * loudness
    return jnp.minimum(jnp.maximum(result, -most), most).astype(held_as)


def setup_inputs(seed: int = 0) -> dict:
    streams_of = jax.random.split(jax.random.key(seed), 29)
    return {
        "pixels": centred(streams_of[0], (FRAMES, 16, 16, PIX), 0.4, 2.5, ((0, 16), (1, 2))),
        "frame_bounds": draw_frame_bounds(jax.random.fold_in(streams_of[28], 71), 0),
        "clip_frames": ragged_sizes(streams_of[2], CLIPS, FRAMES, 17, 2).astype(jnp.int32),
        "codes": with_ends(ranked_ids(streams_of[3], (FRAMES, 16, 16), CODES, 2), jax.random.fold_in(streams_of[3], 3), 0, CODES - 1).astype(jnp.int32),
        "projections": centred(streams_of[4], (2, PIX, C), PIX ** -0.5, 0.21875, ((1, 16),), jnp.float32),
        "blocks": centred(streams_of[5], (4, C, C), C ** -0.5, 0.375, ((1, 16),), jnp.float32),
        "fsq_maps": centred(streams_of[6], (2, C, 6), 0.1, 0.6, ((1, 16),), jnp.float32),
        "gains": jnp.clip(1.0 + 0.1 * jax.random.normal(streams_of[7], (2, C), jnp.float32), 0.5, 1.5),
        "disc_first": centred(streams_of[8], (48, DA), 48 ** -0.5, 0.875, ((1, 16),), jnp.float32),
        "disc_mid": centred(streams_of[9], (32 * DA, DB), (8 * DA) ** -0.5, 0.25, ((0, 16),), jnp.float32),
        "disc_last": centred(streams_of[10], (DB, DC), (DB // 4) ** -0.5, 1.0, ((1, 16),), jnp.float32),
        "disc_head": draw_disc_head(jax.random.fold_in(streams_of[28], 71), 0),
        "moment_projections": centred(streams_of[12], (2, PIX, C), (0.00007 * (FRAMES * 256) ** -0.5), 7.81249980263965e-07, ((1, 16),), jnp.float32),
        "moment_blocks": centred(streams_of[13], (4, C, C), (0.00007 * (FRAMES * 256) ** -0.5), 7.81249980263965e-07, ((1, 16),), jnp.float32),
        "moment_fsq_maps": centred(streams_of[14], (2, C, 6), (0.00008 * (FRAMES * 256) ** -0.25), 2.209708691225387e-05, ((1, 16),), jnp.float32),
        "moment_gains": centred(streams_of[15], (2, C), (0.001 * (FRAMES * 256) ** -0.5), 1.1718750101863407e-05, ((1, 16),), jnp.float32),
        "moment_disc_first": centred(streams_of[16], (48, DA), 0.00025, 0.0015, ((1, 16),), jnp.float32),
        "moment_disc_mid": centred(streams_of[17], (32 * DA, DB), 0.00025, 0.0015, ((0, 16),), jnp.float32),
        "moment_disc_last": centred(streams_of[18], (DB, DC), 0.00025, 0.0015, ((1, 16),), jnp.float32),
        "moment_disc_head": centred(streams_of[19], (DC,), 0.001, 0.006, ((0, 16),), jnp.float32),
        "square_projections": jnp.clip(jnp.exp(math.log(1.5258789240815696e-12) - 1.3862944 * jax.random.uniform(streams_of[20], (2, PIX, C), jnp.float32) ** shard_levels(streams_of[20], (2, PIX, C), ((1, 16),), -0.2, 0.2)), 3.814697310203924e-13, 1.5258789240815696e-12),
        "square_blocks": jnp.clip(jnp.exp(math.log(1.5258789240815696e-12) - 1.3862944 * jax.random.uniform(streams_of[21], (4, C, C), jnp.float32) ** shard_levels(streams_of[21], (4, C, C), ((1, 16),), -0.2, 0.2)), 3.814697310203924e-13, 1.5258789240815696e-12),
        "square_fsq_maps": jnp.clip(jnp.exp(math.log(9.765624975344167e-10) - 2.8134107 * jax.random.uniform(streams_of[22], (2, C, 6), jnp.float32) ** shard_levels(streams_of[22], (2, C, 6), ((1, 16),), -0.2, 0.2)), 5.859374790917471e-11, 9.765624975344167e-10),
        "square_gains": jnp.clip(jnp.exp(math.log(3.051757735406113e-10) - 1.2039727 * jax.random.uniform(streams_of[23], (2, C), jnp.float32) ** shard_levels(streams_of[23], (2, C), ((1, 16),), -0.2, 0.2)), 9.155273761329852e-11, 3.051757735406113e-10),
        "square_disc_first": jnp.clip(jnp.exp(math.log(4.999999873689376e-06) - 2.8134107 * jax.random.uniform(streams_of[24], (48, DA), jnp.float32) ** shard_levels(streams_of[24], (48, DA), ((1, 16),), -0.2, 0.2)), 3.000000106112566e-07, 4.999999873689376e-06),
        "square_disc_mid": jnp.clip(jnp.exp(math.log(4.999999873689376e-06) - 2.8134107 * jax.random.uniform(streams_of[25], (32 * DA, DB), jnp.float32) ** shard_levels(streams_of[25], (32 * DA, DB), ((0, 16),), -0.2, 0.2)), 3.000000106112566e-07, 4.999999873689376e-06),
        "square_disc_last": jnp.clip(jnp.exp(math.log(4.999999873689376e-06) - 2.8134107 * jax.random.uniform(streams_of[26], (DB, DC), jnp.float32) ** shard_levels(streams_of[26], (DB, DC), ((1, 16),), -0.2, 0.2)), 3.000000106112566e-07, 4.999999873689376e-06),
        "square_disc_head": jnp.clip(jnp.exp(math.log(7.999999797903001e-05) - 2.7725887 * jax.random.uniform(streams_of[27], (DC,), jnp.float32) ** shard_levels(streams_of[27], (DC,), ((0, 16),), -0.2, 0.2)), 4.999999873689376e-06, 7.999999797903001e-05),
    }


HIGHEST = lax.Precision.HIGHEST
EPS_NORM = 1e-06
BETA_ONE = 0.9
BETA_TWO = 0.95
ADAM_EPS = 1e-08
DECAY = 0.1
RATE_MATRIX = 0.04
RATE_GAIN = 0.25
GEN_WEIGHT = 0.02
HALVES = (3.5, 3.5, 3.5, 2.0, 2.0, 2.0)
LEVELS = (8, 8, 8, 5, 5, 5)

@jax.custom_vjp
def low(v):
    return lax.optimization_barrier(v.astype(jnp.bfloat16)).astype(jnp.float32)

@jax.custom_vjp
def low_back(v):
    return v

def low_keep(v):
    return (low(v), None)

def low_pass(kept, grad):
    return (grad,)

def back_keep(v):
    return (v, None)

def back_low(kept, grad):
    return (low(grad),)
low.defvjp(low_keep, low_pass)
low_back.defvjp(back_keep, back_low)

def mat_mul(operand, weights):
    return low_back(jnp.dot(operand, weights, precision=HIGHEST))

def frame_weights(bounds, clip_frames, first_frame):
    clip_ends = jnp.cumsum(clip_frames)
    frame_index = first_frame + jnp.arange(bounds.shape[0], dtype=jnp.int32)
    clip_of = lax.optimization_barrier(jnp.sum((clip_ends[None, :] <= frame_index[:, None]).astype(jnp.int32), axis=1))
    picked = lax.optimization_barrier(jnp.sum(jnp.where(clip_of[:, None] == jnp.arange(clip_frames.shape[0], dtype=jnp.int32)[None, :], clip_frames[None, :], 0), axis=1))
    return 1.0 / picked.astype(jnp.float32)

def pixel_mask(bounds, row_start, band_rows, width):
    places = jnp.arange(width, dtype=jnp.int32)
    subpatch = places // 48
    within = places % 48
    down = subpatch // 4 * 4 + within // 12
    across = subpatch % 4 * 4 + within % 12 // 3
    pixel_rows = (row_start + jnp.arange(band_rows, dtype=jnp.int32))[:, None] * 16 + down[None, :]
    pixel_cols = jnp.arange(16, dtype=jnp.int32)[:, None] * 16 + across[None, :]
    inside = (pixel_rows[None, :, None, :] < bounds[:, 0][:, None, None, None]) & (pixel_cols[None, None, :, :] < bounds[:, 1][:, None, None, None])
    return inside.astype(jnp.float32)

def code_values(codes):
    parts = []
    remains = codes
    for levels, halves in zip(LEVELS, HALVES):
        parts.append(((remains % levels).astype(jnp.float32) - halves) / halves)
        remains = remains // levels
    return jnp.stack(parts, axis=-1)

def block(stream, gain_row, first_mat, second_mat):
    normal = stream * lax.rsqrt(lax.optimization_barrier(jnp.mean(stream * stream, axis=-1, keepdims=True)) + EPS_NORM)
    acted = low(jax.nn.silu(mat_mul(low(normal * gain_row), first_mat)))
    return stream + mat_mul(acted, second_mat)

def encode(pixel_rows, weights):
    project, matrices, fsq_pair, gain_pair = weights
    stream = mat_mul(pixel_rows, project[0])
    middle = block(stream, gain_pair[0], matrices[0], matrices[1])
    return (middle, mat_mul(low(middle), fsq_pair[0]))

def autoencode(pixel_rows, coded, fixed_tanh, weights):
    project, matrices, fsq_pair, gain_pair = weights
    middle, latent = encode(pixel_rows, weights)
    values = low(coded + jnp.tanh(latent) - fixed_tanh)
    start = mat_mul(values, fsq_pair[1].T)
    output = block(start, gain_pair[1], matrices[2], matrices[3])
    return mat_mul(low(output), project[1].T)

def judge(inputs, weights):
    first_conv, mid_conv, last_conv, head_map = weights
    frames = inputs.shape[0]
    pre_one = mat_mul(inputs.reshape(-1, 48), first_conv).reshape(frames, 16, 16, -1)
    act_one = low(jax.nn.silu(pre_one))
    below = low_back(jnp.concatenate([act_one[:, 1:], jnp.zeros_like(act_one[:, :1])], axis=1))
    joined = jnp.concatenate([act_one, below], axis=-1).reshape(frames * 256, -1)
    act_two = low(jax.nn.silu(mat_mul(joined, mid_conv)))
    act_three = low(jax.nn.silu(mat_mul(act_two, last_conv)))
    return jnp.dot(act_three, head_map, precision=HIGHEST)

def adamw(master, moment, square, grad, rate, decay):
    new_moment = BETA_ONE * moment + (1.0 - BETA_ONE) * grad
    new_square = BETA_TWO * square + (1.0 - BETA_TWO) * grad * grad
    update = new_moment / (1.0 - BETA_ONE ** STEP) / (jnp.sqrt(new_square / (1.0 - BETA_TWO ** STEP)) + ADAM_EPS)
    return (new_moment, new_square, master - rate * (update + decay * master))

def reference(pixels, frame_bounds, clip_frames, codes, projections, blocks, fsq_maps, gains, disc_first, disc_mid, disc_last, disc_head, moment_projections, moment_blocks, moment_fsq_maps, moment_gains, moment_disc_first, moment_disc_mid, moment_disc_last, moment_disc_head, square_projections, square_blocks, square_fsq_maps, square_gains, square_disc_first, square_disc_mid, square_disc_last, square_disc_head):
    masters = (projections, blocks, fsq_maps, gains, disc_first, disc_mid, disc_last, disc_head)
    moments = (moment_projections, moment_blocks, moment_fsq_maps, moment_gains, moment_disc_first, moment_disc_mid, moment_disc_last, moment_disc_head)
    squares = (square_projections, square_blocks, square_fsq_maps, square_gains, square_disc_first, square_disc_mid, square_disc_last, square_disc_head)
    frames = pixels.shape[0]
    width = pixels.shape[-1]
    weighting = frame_weights(frame_bounds, clip_frames, 0)
    weight_mask = pixel_mask(frame_bounds, 0, 16, width) * weighting[:, None, None, None]
    total_weight = jnp.sum(weight_mask)
    mask_rows = weight_mask.reshape(frames * 256, width)
    pixel_rows = pixels.astype(jnp.float32).reshape(frames * 256, width)
    coded = code_values(codes).reshape(frames * 256, 6)
    count_all = jnp.float32(frames * 256)
    lowered = tuple((low(weight) for weight in masters[:4]))
    fixed_tanh = jnp.tanh(encode(pixel_rows, lowered)[1])

    def auto_loss(auto_weights, judge_weights):
        auto_weights = tuple((low(weight) for weight in auto_weights))
        judge_weights = tuple((low(weight) for weight in judge_weights))
        recon = autoencode(pixel_rows, coded, fixed_tanh, auto_weights)
        fake = low(recon)
        scores = judge(fake.reshape(frames, 16, 16, width), judge_weights)
        diff = recon - pixel_rows
        l1_sum = jnp.sum(mask_rows * jnp.sqrt(diff * diff + 1.0))
        gen_sum = jnp.sum(-scores)
        return (l1_sum / total_weight + GEN_WEIGHT * gen_sum / count_all, (fake, l1_sum, gen_sum))
    loss_auto, pull_auto, (fake, l1_sum, gen_sum) = jax.vjp(auto_loss, masters[:4], masters[4:], has_aux=True)
    grads_auto = pull_auto(jnp.ones_like(loss_auto))[0]

    def judge_loss(judge_weights):
        judge_weights = tuple((low(weight) for weight in judge_weights))
        real_scores = judge(pixel_rows.reshape(frames, 16, 16, width), judge_weights)
        fake_scores = judge(fake.reshape(frames, 16, 16, width), judge_weights)
        disc_sum = jnp.sum(jax.nn.softplus(1.0 - real_scores)) + jnp.sum(jax.nn.softplus(1.0 + fake_scores))
        return (disc_sum / count_all, disc_sum)
    loss_judge, pull_judge, disc_sum = jax.vjp(judge_loss, masters[4:], has_aux=True)
    grads_judge = pull_judge(jnp.ones_like(loss_judge))[0]
    grads = tuple(grads_auto) + tuple(grads_judge)
    results = [adamw(masters[number], moments[number], squares[number], grads[number], RATE_GAIN if number == 3 else RATE_MATRIX, 0.0 if number == 3 else DECAY) for number in range(8)]
    counts = jax.ops.segment_sum(jnp.ones((codes.size,), jnp.float32), codes.reshape(-1).astype(jnp.int32), num_segments=CODES)
    shares = counts / jnp.sum(counts)
    perplexity = jnp.exp(-jnp.sum(jax.scipy.special.xlogy(shares, shares)))
    loss_terms = jnp.stack([l1_sum, total_weight])
    adversarial_sums = jnp.stack([gen_sum, disc_sum])
    return (results[0][0], results[1][0], results[2][0], results[3][0], results[4][0], results[5][0], results[6][0], results[7][0], results[0][1], results[1][1], results[2][1], results[3][1], results[4][1], results[5][1], results[6][1], results[7][1], results[0][2], results[1][2], results[2][2], results[3][2], results[4][2], results[5][2], results[6][2], results[7][2], loss_terms, adversarial_sums, perplexity)
```

```python
import jax
import jax.numpy as jnp
import numpy as np
from jax import lax
from jax.experimental import pallas as pl
from jax.experimental.pallas import tpu as pltpu
from jax.sharding import PartitionSpec as P

CODES = 64000
STEP = 10
EPS_NORM = 1e-06
BETA_ONE = 0.9
BETA_TWO = 0.95
ADAM_EPS = 1e-08
DECAY = 0.1
RATE_MATRIX = 0.04
RATE_GAIN = 0.25
GEN_WEIGHT = 0.02
HALVES = (3.5, 3.5, 3.5, 2.0, 2.0, 2.0)
LEVELS = (8, 8, 8, 5, 5, 5)

F32 = jnp.float32
BF16 = jnp.bfloat16
VMEM_LIMIT = 60 * 2**20
MAX_LANES = 512


def nn(left, right):
    return jnp.dot(left, right, preferred_element_type=F32)


def nt(left, right):
    return lax.dot_general(left, right, (((1,), (1,)), ((), ())), preferred_element_type=F32)


def low(value):
    return value.astype(BF16)


def wide(columns, lanes):
    return jnp.concatenate([columns] * (lanes // 128), axis=1)


def fold(value):
    total = value[:, :128]
    for start in range(128, value.shape[1], 128):
        total = total + value[:, start : start + 128]
    return total


def silu_parts(half):
    turned = jnp.tanh(half)
    acted = half + half * turned
    return acted, (1.0 + turned) + (acted - acted * turned)


def norm_parts(stream):
    scaling = lax.rsqrt(jnp.mean(stream * stream, axis=0, keepdims=True) + EPS_NORM)
    return scaling, stream * scaling


def softplus(value):
    return jnp.maximum(value, 0.0) + jnp.log1p(jnp.exp(-jnp.abs(value)))


def block_forward(stream, gain, first_half_t, second_t):
    scaling, normal = norm_parts(stream)
    normed = low(normal * gain)
    acted, slope = silu_parts(nn(first_half_t, normed))
    acted = low(acted)
    return stream + nn(second_t, acted), (scaling, normal, normed, acted, slope)


def block_backward(grad_out, saved, gain, first, second_half, grad_first, grad_second, grad_gain):
    scaling, normal, normed, acted, slope = saved
    grad_low = low(grad_out)
    grad_second[...] += nt(acted, grad_low)
    grad_inside = low(nn(second_half, grad_low) * slope)
    grad_first[...] += nt(normed, grad_inside)
    grad_normed = nn(first, grad_inside)
    along = grad_normed * normal
    grad_gain[...] += fold(along)
    mean = jnp.mean(along * gain, axis=0, keepdims=True)
    return grad_out + scaling * (grad_normed * gain - normal * mean)


def judge_middle(stash_q, fresh_p, wlt_half, wl_half, head_half, head_rows, count_all, active, kind):
    lanes = fresh_p.shape[1]
    acted_two, slope_two = silu_parts(fresh_p[:128] + stash_q)
    acted_two = low(acted_two)
    acted_three, slope_three = silu_parts(nn(wlt_half, acted_two))
    acted_three = low(acted_three)
    score = nn(head_rows, acted_three)[:1]
    shaped = wide(head_half, lanes) * slope_three
    if kind == "real":
        grad_score = -jax.nn.sigmoid(1.0 - score) * (active / count_all)
        grad_three = low(grad_score * shaped)
        grad_two = (low(nn(wl_half, grad_three) * slope_two),)
        losses = (softplus(1.0 - score),)
    else:
        pull = jax.nn.sigmoid(1.0 + score)
        grad_score = pull * (active / count_all)
        grad_three = low(grad_score * shaped)
        grad_three_gen = low((-GEN_WEIGHT / count_all * active) * shaped)
        grad_two_gen = nn(wl_half, grad_three_gen) * slope_two
        grad_two = (low(grad_two_gen * (pull * (-1.0 / GEN_WEIGHT))), low(grad_two_gen))
        losses = (softplus(1.0 + score), -score)
    return acted_two, acted_three, grad_score, grad_three, grad_two, losses


def make_kernel(kind, band, lanes, chunks, count_all):
    frames_in = lanes // 16
    fake = kind == "fake"

    def kernel(*refs):
        refs = list(refs)

        def take(number):
            taken = refs[:number]
            del refs[:number]
            return taken

        places, reals = take(2)
        xa_ref, xb_ref, xbelow_ref, xabove_ref = take(4)
        bdt_ref, wm_ref, wl_ref, headw_ref, headr_ref = take(5)
        if fake:
            codes_ref, lane_ref, consts_ref, spots_ref = take(4)
            proj_ref, blocks_ref, fsq_ref, fsqt_ref, gains_ref, bd_ref = take(6)
            gproj_ref, gblocks_ref, gfsq_ref, ggains_ref = take(4)
        gwm_ref, gwl_ref, gw1_ref, ghead_ref, loss_ref = take(5)
        wmt_s, wmh_s, wlt_s, wlh_s, q_s = take(5)
        kinds = 2 if fake else 1
        g2_s = take(kinds)
        if fake:
            projt_s, blockt_s, blockh_s, gradlow_s = take(4)
            names = ("xt", "fake", "gl1", "act", "slope", "normal", "scaling", "normed", "acted", "bslope", "outlow", "values")
        else:
            names = ("xt", "act", "slope")
        stash_a = dict(zip(names, take(len(names))))
        stash_b = dict(zip(names, take(len(names))))
        chunk, step = pl.program_id(0), pl.program_id(1)
        last_step = band // 2
        row_start, has_below, has_above = places[0], places[1], places[2]
        inv_total = reals[0]
        has_above_f = has_above.astype(F32)

        @pl.when((chunk == 0) & (step == 0))
        def prepare():
            half = jnp.asarray(0.5, BF16)
            for part in range(4):
                rows = pl.ds(part * 256, 256)
                wmh_s[rows, :] = wm_ref[rows, :] * half
                wmt_s[:, rows] = (wm_ref[rows, :] * half).T
            wlt_s[...] = (wl_ref[...] * half).T
            wlh_s[...] = wl_ref[...] * half
            for ref in (gwm_ref, gwl_ref, gw1_ref, ghead_ref, loss_ref):
                ref[...] = jnp.zeros_like(ref)
            if fake:
                projt_s[0] = proj_ref[0].T
                projt_s[1] = proj_ref[1].T
                for number in range(4):
                    scale = jnp.asarray(0.5 if number % 2 == 0 else 1.0, BF16)
                    blockt_s[number] = (blocks_ref[number] * scale).T
                    if number % 2 == 1:
                        blockh_s[number // 2] = blocks_ref[number] * half
                for ref in (gproj_ref, gblocks_ref, gfsq_ref, ggains_ref):
                    ref[...] = jnp.zeros_like(ref)

        def front(row, x, stash, lite=False):
            xt = x.reshape(lanes, 768).T
            if not lite:
                stash["xt"][...] = xt
            if fake:
                consts = consts_ref[...]
                code = codes_ref[pl.ds(row + 1, 1), :]
                turn = jnp.floor((code + 0.5) * wide(consts[0:16], lanes))
                level = wide(consts[16:32], lanes)
                digit = turn - level * jnp.floor((turn + 0.5) * wide(consts[32:48], lanes))
                values = low((digit - wide(consts[48:64], lanes)) * wide(consts[64:80], lanes))
                gain = wide(gains_ref[1], lanes)
                start = nn(fsq_ref[1], values)
                output, saved = block_forward(start, gain, blockt_s[2], blockt_s[3])
                outlow = low(output)
                if not lite:
                    stash["values"][...] = values
                    stash["outlow"][...] = outlow
                    for name, item in zip(("scaling", "normal", "normed", "acted", "bslope"), saved):
                        stash[name][...] = item
                    lane = lax.broadcasted_iota(jnp.int32, (1, lanes), 1)
                    column = (lane % 16).astype(F32)
                    place = (row_start + row).astype(F32)
                    high = lane_ref[0:1, :] - 16.0 * place
                    broad = lane_ref[1:2, :] - 16.0 * column
                    valid = jnp.where(row >= 0, 1.0, 0.0)
                    weight = lane_ref[2:3, :] * valid
                    weight_share = weight * inv_total
                    l1_sum = jnp.zeros((1, lanes), F32)
            parts = []
            for group in range(4):
                rows = pl.ds(group * 192, 192)
                if fake:
                    recon = nn(proj_ref[1, rows, :], outlow)
                    inputs = low(recon)
                    if not lite:
                        stash["fake"][rows, :] = inputs
                        diff = recon - xt[group * 192 : group * 192 + 192].astype(F32)
                        square = diff * diff + 1.0
                        inverse = lax.rsqrt(square)
                        inside = (wide(spots_ref[0, rows, :], lanes) < high) & (
                            wide(spots_ref[1, rows, :], lanes) < broad
                        )
                        l1_sum = l1_sum + jnp.sum(jnp.where(inside, square * inverse, 0.0), axis=0, keepdims=True)
                        stash["gl1"][rows, :] = jnp.where(inside, diff * inverse, 0.0) * weight_share
                else:
                    inputs = xt[group * 192 : group * 192 + 192]
                acted, slope = silu_parts(nn(bdt_ref[...], inputs))
                acted = low(acted)
                wide_rows = pl.ds(group * 256, 256)
                if not lite:
                    stash["act"][wide_rows, :] = acted
                    stash["slope"][wide_rows, :] = slope
                parts.append(acted)
            joined = jnp.concatenate(parts, axis=0)
            if lite:
                q_s[...] = nn(wmt_s[128:256, :], joined)
                return
            fresh = nn(wmt_s[...], joined)
            active = jnp.where(row >= 0, 1.0, has_above_f)
            counted = jnp.where(row >= 0, 1.0, 0.0)
            acted_two, acted_three, grad_score, grad_three, grad_two, losses = judge_middle(
                q_s[...], fresh, wlt_s[...], wlh_s[...], headw_ref[...], headr_ref[...], count_all, active, kind
            )
            q_s[...] = fresh[128:]
            for number, item in enumerate(losses):
                loss_ref[number : number + 1, :] += item * counted
            if fake:
                loss_ref[2:3, :] += l1_sum * weight
            gwl_ref[...] += nt(acted_two * counted.astype(BF16), grad_three)
            ghead_ref[...] += fold(acted_three.astype(F32) * (grad_score * counted))
            for ref, item in zip(g2_s, grad_two):
                ref[128:256, :] = item

        def finish(stash):
            for group in range(4):
                rows, wide_rows = pl.ds(group * 192, 192), pl.ds(group * 256, 256)
                slope = stash["slope"][wide_rows, :]
                small = low(nn(wmh_s[wide_rows, :], g2_s[0][...]) * slope)
                inputs = stash["fake" if fake else "xt"][rows, :]
                gw1_ref[...] += nt(inputs, small)
                gwm_ref[wide_rows, :] += nt(stash["act"][wide_rows, :], g2_s[0][...])
                if fake:
                    small_gen = low(nn(wmh_s[wide_rows, :], g2_s[1][...]) * slope)
                    grad_recon = low(stash["gl1"][rows, :] + nn(bd_ref[...], small_gen))
                    gradlow_s[rows, :] = grad_recon
                    gproj_ref[1, rows, :] += nt(grad_recon, stash["outlow"][...])
            if fake:
                gain = wide(gains_ref[1], lanes)
                saved = tuple(stash[name][...] for name in ("scaling", "normal", "normed", "acted", "bslope"))
                grad_start = block_backward(
                    nn(projt_s[1], gradlow_s[...]), saved, gain, blocks_ref[2], blockh_s[1],
                    gblocks_ref.at[2], gblocks_ref.at[3], ggains_ref.at[1],
                )
                start_low = low(grad_start)
                gfsq_ref[1] += nt(start_low, stash["values"][...])
                grad_values = nn(fsqt_ref[1], start_low)
                gain = wide(gains_ref[0], lanes)
                stream = nn(projt_s[0], stash["xt"][...])
                middle, saved = block_forward(stream, gain, blockt_s[0], blockt_s[1])
                middle_low = low(middle)
                tangent = jnp.tanh(nn(fsqt_ref[0], middle_low))
                grad_latent = low(grad_values * (1.0 - tangent * tangent))
                gfsq_ref[0] += nt(middle_low, grad_latent)
                grad_stream = block_backward(
                    nn(fsq_ref[0], grad_latent), saved, gain, blocks_ref[0], blockh_s[0],
                    gblocks_ref.at[0], gblocks_ref.at[1], ggains_ref.at[0],
                )
                gproj_ref[0] += nt(stash["xt"][...], low(grad_stream))
            for ref in g2_s:
                ref[0:128, :] = ref[128:256, :]

        @pl.when((step == 0) & (has_below > 0))
        def below():
            front(jnp.int32(band), xbelow_ref[...], None, lite=True)

        @pl.when((step == 0) & (has_below == 0))
        def edge():
            q_s[...] = jnp.zeros_like(q_s)

        @pl.when(step == 0)
        def first():
            front(jnp.int32(band - 1), xa_ref[...], stash_a)
            for ref in g2_s:
                ref[0:128, :] = ref[128:256, :]

        @pl.when(step > 0)
        def main():
            front(band - 2 * step, xa_ref[...], stash_b)
            finish(stash_a)
            x = jnp.where(step == last_step, xabove_ref[...], xb_ref[...].reshape(frames_in, 16, 768))
            front(band - 2 * step - 1, x, stash_a)
            finish(stash_b)

    return kernel


def run_kernel(kind, pixels, halos, places, reals, judge, extra, weights, count_all):
    frames, band = pixels.shape[:2]
    lanes = min(MAX_LANES, frames * 16)
    chunks = frames * 16 // lanes
    frames_in = lanes // 16
    fake = kind == "fake"
    smem = pl.BlockSpec(memory_space=pltpu.SMEM)

    def whole(array):
        return pl.BlockSpec(array.shape, lambda c, s: (0,) * array.ndim)

    def row_spec(first):
        if first:
            return lambda c, s: (c, jnp.where(s == 0, band - 1, band - 2 * s), 0, 0)
        return lambda c, s: (c, jnp.maximum(band - 1 - 2 * s, 0), 0, 0)

    block = (frames_in, 1, 16, 768)
    halo_spec = pl.BlockSpec((frames_in, 16, 768), lambda c, s: (c, 0, 0))
    operands = [places, reals, pixels, pixels, *halos, *judge]
    specs = [smem, smem, pl.BlockSpec(block, row_spec(True)), pl.BlockSpec(block, row_spec(False)), halo_spec, halo_spec]
    specs += [whole(item) for item in judge]
    if fake:
        codes, lane_info, consts, spots = extra
        operands += [codes, lane_info, consts, spots, *weights]
        specs += [
            pl.BlockSpec((codes.shape[0], lanes), lambda c, s: (0, c)),
            pl.BlockSpec((lane_info.shape[0], lanes), lambda c, s: (0, c)),
            whole(consts),
            whole(spots),
        ]
        specs += [whole(item) for item in weights]
    outs = []
    if fake:
        outs += [(2, 768, 256), (4, 256, 256), (2, 256, 16), (2, 256, 128)]
    outs += [(1024, 256), (128, 256), (192, 256), (256, 128), (8, lanes)]
    outs = [jax.ShapeDtypeStruct(shape, F32) for shape in outs]
    scratch = [
        pltpu.VMEM((256, 1024), BF16),
        pltpu.VMEM((1024, 256), BF16),
        pltpu.VMEM((256, 128), BF16),
        pltpu.VMEM((128, 256), BF16),
        pltpu.VMEM((128, lanes), F32),
    ]
    scratch += [pltpu.VMEM((256, lanes), BF16)] * (2 if fake else 1)
    if fake:
        scratch += [
            pltpu.VMEM((2, 256, 768), BF16),
            pltpu.VMEM((4, 256, 256), BF16),
            pltpu.VMEM((2, 256, 256), BF16),
            pltpu.VMEM((768, lanes), BF16),
        ]
        stash = [
            ((768, lanes), BF16),
            ((768, lanes), BF16),
            ((768, lanes), F32),
            ((1024, lanes), BF16),
            ((1024, lanes), F32),
            ((256, lanes), F32),
            ((1, lanes), F32),
            ((256, lanes), BF16),
            ((256, lanes), BF16),
            ((256, lanes), F32),
            ((256, lanes), BF16),
            ((16, lanes), BF16),
        ]
    else:
        stash = [((768, lanes), BF16), ((1024, lanes), BF16), ((1024, lanes), F32)]
    scratch += [pltpu.VMEM(*item) for item in stash] * 2
    return pl.pallas_call(
        make_kernel(kind, band, lanes, chunks, count_all),
        grid=(chunks, band // 2 + 1),
        in_specs=specs,
        out_specs=[pl.BlockSpec(item.shape, lambda c, s, n=len(item.shape): (0,) * n) for item in outs],
        out_shape=outs,
        scratch_shapes=scratch,
        compiler_params=pltpu.CompilerParams(
            vmem_limit_bytes=VMEM_LIMIT, dimension_semantics=("arbitrary", "arbitrary")
        ),
        name="judge_" + kind,
    )(*operands)


def count_kernel(codes_ref, counts_ref):
    @pl.when(pl.program_id(0) == 0)
    def clear():
        counts_ref[...] = jnp.zeros_like(counts_ref)

    code = codes_ref[0]
    upper = jnp.floor(code * (1.0 / 256.0))
    lower = code - 256.0 * upper
    bins = lax.broadcasted_iota(jnp.int32, (256, code.shape[1]), 0).astype(F32)
    one, zero = jnp.asarray(1.0, F32), jnp.asarray(0.0, F32)
    counts_ref[...] += nt(low(jnp.where(bins == upper, one, zero)), low(jnp.where(bins == lower, one, zero)))


def count_codes(codes):
    parts = codes.size // 1024
    return pl.pallas_call(
        count_kernel,
        grid=(parts,),
        in_specs=[pl.BlockSpec((1, 1, 1024), lambda s: (s, 0, 0))],
        out_specs=pl.BlockSpec((256, 256), lambda s: (0, 0)),
        out_shape=jax.ShapeDtypeStruct((256, 256), F32),
        name="count",
    )(codes.astype(F32).reshape(parts, 1, 1024))


def passed_along(x, axis, by):
    size = lax.axis_size(axis)
    pairs = [(i, i + by) for i in range(size) if 0 <= i + by < size]
    return lax.ppermute(x, axis, pairs)


def frame_weights(bounds, clip_frames, first_frame):
    clip_ends = jnp.cumsum(clip_frames)
    frame_index = first_frame + jnp.arange(bounds.shape[0], dtype=jnp.int32)
    clip_of = jnp.sum((clip_ends[None, :] <= frame_index[:, None]).astype(jnp.int32), axis=1)
    picked = jnp.sum(
        jnp.where(
            clip_of[:, None] == jnp.arange(clip_frames.shape[0], dtype=jnp.int32)[None, :],
            clip_frames[None, :],
            0,
        ),
        axis=1,
    )
    return 1.0 / picked.astype(F32)


def adamw(master, moment, square, grad, rate, decay):
    new_moment = BETA_ONE * moment + (1.0 - BETA_ONE) * grad
    new_square = BETA_TWO * square + (1.0 - BETA_TWO) * grad * grad
    update = (
        new_moment
        / (1.0 - BETA_ONE**STEP)
        / (jnp.sqrt(new_square / (1.0 - BETA_TWO**STEP)) + ADAM_EPS)
    )
    return (new_moment, new_square, master - rate * (update + decay * master))


def constants():
    products = np.cumprod((1,) + LEVELS)[:6]
    rows = np.zeros((5, 16), np.float32)
    rows[1] = 1.0
    rows[2] = 1.0
    rows[0, :6] = 1.0 / products
    rows[1, :6] = LEVELS
    rows[2, :6] = 1.0 / np.array(LEVELS)
    rows[3, :6] = HALVES
    rows[4, :6] = 1.0 / np.array(HALVES)
    consts = np.broadcast_to(rows.reshape(80, 1), (80, 128)).astype(np.float32)
    places = np.arange(768)
    down = places // 48 // 4 * 4 + places % 48 // 12
    across = places // 48 % 4 * 4 + places % 48 % 12 // 3
    spots = np.broadcast_to(np.stack([down, across])[:, :, None], (2, 768, 128)).astype(np.float32)
    return jnp.asarray(consts), jnp.asarray(spots)


def on_device(pixels, frame_bounds, clip_frames, codes, *states):
    masters, moments, squares = states[:8], states[8:16], states[16:24]
    frames, band = pixels.shape[:2]
    grp, bands = lax.axis_index("grp"), lax.axis_size("grp")
    parts = lax.axis_size("dp")
    count_all = float(frames * parts * 256)
    halos = (passed_along(pixels[:, 0], "grp", -1), passed_along(pixels[:, band - 1], "grp", 1))
    code_halos = (passed_along(codes[:, 0], "grp", -1), passed_along(codes[:, band - 1], "grp", 1))
    weighting = frame_weights(frame_bounds, clip_frames, lax.axis_index("dp") * frames)
    own_total = jnp.sum(
        weighting * (3 * frame_bounds[:, 0] * frame_bounds[:, 1]).astype(F32)
    )
    total_weight = lax.psum(own_total, "dp")
    counts = lax.psum(count_codes(codes), ("dp", "grp"))

    shards = [low(weight) for weight in masters]
    axes = (1, 1, 1, 1, 1, 0, 1, 0)
    project, matrices, fsq_pair, gain_pair, first_conv, mid_conv, last_conv, head_map = (
        lax.all_gather(shard, "dp", axis=axis, tiled=True) for shard, axis in zip(shards, axes)
    )
    half = jnp.asarray(0.5, BF16)
    eye = jnp.eye(4, dtype=BF16)
    bd = jnp.kron(eye, first_conv)
    bdt = bd.T * half
    wm = jnp.concatenate([mid_conv[:1024], mid_conv[1024:]], axis=1)
    headw = jnp.broadcast_to(head_map.astype(F32)[:, None] * 0.5, (256, 128))
    headr = jnp.concatenate([head_map[None, :], jnp.zeros((15, 256), BF16)], axis=0)
    judge = (bdt, wm, last_conv, headw, headr)
    fsq = jnp.pad(fsq_pair, ((0, 0), (0, 0), (0, 10)))
    fsqt = fsq.transpose(0, 2, 1)
    gains = jnp.broadcast_to(gain_pair.astype(F32)[:, :, None], (2, 256, 128))
    weights = (project, matrices, fsq, fsqt, gains, bd)

    places = jnp.stack([grp * band, (grp < bands - 1).astype(jnp.int32), (grp > 0).astype(jnp.int32)]).astype(jnp.int32)
    reals = jnp.stack([1.0 / total_weight, total_weight])
    all_codes = jnp.concatenate([code_halos[1][:, None], codes, code_halos[0][:, None]], axis=1)
    code_rows = all_codes.transpose(1, 0, 2).reshape(band + 2, frames * 16).astype(F32)
    lane_info = jnp.repeat(
        jnp.stack([frame_bounds[:, 0].astype(F32), frame_bounds[:, 1].astype(F32), weighting] + [weighting] * 5), 16, axis=1
    )
    consts, spots = constants()
    extra = (code_rows, lane_info, consts, spots)

    fake_outs = run_kernel("fake", pixels, halos, places, reals, judge, extra, weights, count_all)
    real_outs = run_kernel("real", pixels, halos, places, reals, judge, None, None, count_all)
    gproj, gblocks, gfsq, ggains = fake_outs[:4]
    gwm, gwl, gw1, ghead = (left + right for left, right in zip(fake_outs[4:8], real_outs[:4]))
    first_grad = sum(gw1[48 * n : 48 * n + 48, 64 * n : 64 * n + 64] for n in range(4))
    grads = (
        gproj,
        gblocks,
        gfsq[:, :, :6],
        jnp.sum(ggains, axis=-1),
        first_grad,
        jnp.concatenate([gwm[:, :128], gwm[:, 128:]], axis=0),
        gwl,
        jnp.sum(ghead, axis=-1),
    )
    losses = jnp.stack(
        [jnp.sum(fake_outs[8][2]), jnp.sum(fake_outs[8][1]), jnp.sum(fake_outs[8][0]) + jnp.sum(real_outs[4][0])]
    )
    pieces = []
    for grad, axis in zip(grads, axes):
        shape = grad.shape
        split = grad.reshape(shape[:axis] + (parts, shape[axis] // parts) + shape[axis + 1 :])
        pieces.append(jnp.moveaxis(split, axis, 0).reshape(parts, -1))
    sizes = [piece.shape[1] for piece in pieces]
    packed = jnp.concatenate(pieces, axis=1)
    padding = -packed.shape[1] % 1024
    packed = jnp.pad(packed, ((0, 0), (0, padding)))
    summed = lax.psum_scatter(packed, "dp", scatter_dimension=0, tiled=True)
    summed = lax.psum(summed, "grp").reshape(-1)
    totals, place = [], 0
    for master, size in zip(masters, sizes):
        totals.append(summed[place : place + size].reshape(master.shape))
        place += size
    losses = lax.psum(losses, ("dp", "grp"))
    results = [
        adamw(
            masters[number],
            moments[number],
            squares[number],
            totals[number],
            RATE_GAIN if number == 3 else RATE_MATRIX,
            0.0 if number == 3 else DECAY,
        )
        for number in range(8)
    ]
    shares_all = counts / jnp.sum(counts)
    perplexity = jnp.exp(-jnp.sum(jax.scipy.special.xlogy(shares_all, shares_all)))
    loss_terms = jnp.stack([losses[0], total_weight])
    adversarial_sums = jnp.stack([losses[1], losses[2]])
    return (
        *(result[0] for result in results),
        *(result[1] for result in results),
        *(result[2] for result in results),
        loss_terms,
        adversarial_sums,
        perplexity,
    )


def solution(mesh):
    states = (
        P(None, "dp", None),
        P(None, "dp", None),
        P(None, "dp", None),
        P(None, "dp"),
        P(None, "dp"),
        P("dp", None),
        P(None, "dp"),
        P("dp"),
    )
    return jax.shard_map(
        on_device,
        mesh=mesh,
        in_specs=(P("dp", "grp", None, None), P("dp", None), P(), P("dp", "grp", None)) + states * 3,
        out_specs=states * 3 + (P(), P(), P()),
        check_vma=False,
    )
```

```python
import jax
import jax.numpy as jnp
import numpy as np
from jax import lax
from jax.experimental import pallas as pl
from jax.experimental.pallas import tpu as pltpu
from jax.sharding import PartitionSpec as P

STEP = 10
EPS_NORM = 1e-06
BETA_ONE = 0.9
BETA_TWO = 0.95
ADAM_EPS = 1e-08
DECAY = 0.1
RATE_MATRIX = 0.04
RATE_GAIN = 0.25
GEN_WEIGHT = 0.02
HALVES = (3.5, 3.5, 3.5, 2.0, 2.0, 2.0)
LEVELS = (8, 8, 8, 5, 5, 5)

F32 = jnp.float32
BF16 = jnp.bfloat16
VMEM_LIMIT = 60 * 2**20
FAKE_LANES = 512
REAL_LANES = 1024
SLABS = 16
VALUES = (0, 8, 4, 12, 2, 10, 6, 14)
AUTO_ROWS = 160
SLAB_ROWS = 240
AXES = (1, 1, 1, 1, 1, 0, 1, 0)
HIGHEST = lax.Precision.HIGHEST


def nn(left, right):
    return jnp.dot(left, right, preferred_element_type=F32)


def nt(left, right):
    return lax.dot_general(left, right, (((1,), (1,)), ((), ())), preferred_element_type=F32)


def low(value):
    return value.astype(BF16)


def wide(columns, lanes):
    return jnp.concatenate([columns] * (lanes // 128), axis=1)


def fold(value):
    total = value[:, :128]
    for start in range(128, value.shape[1], 128):
        total = total + value[:, start : start + 128]
    return total


def silu_parts(half):
    turned = jnp.tanh(half)
    upper = 1.0 + turned
    acted = half * upper
    return acted, upper + acted * (1.0 - turned)


def norm_parts(stream):
    scaling = lax.rsqrt(jnp.mean(stream * stream, axis=0, keepdims=True) + EPS_NORM)
    return scaling, stream * scaling


def softplus(value):
    return jnp.maximum(value, 0.0) + jnp.log1p(jnp.exp(-jnp.abs(value)))


def cost(flops, moved):
    return pl.CostEstimate(flops=int(flops), bytes_accessed=int(moved), transcendentals=0)


def aligned(index, size):
    return pl.ds(pl.multiple_of(index * size, size), size)


def interleave(*pieces):
    pieces = list(pieces)
    while pieces:
        for piece in list(pieces):
            try:
                next(piece)
            except StopIteration:
                pieces.remove(piece)


def slab_owners(me, slabs):
    for core, array in enumerate(slabs):
        for place, value in enumerate(VALUES):
            yield me ^ value ^ core, array.at[place]


def unpack_judge(me, slabs, pair_s, misc_s, first_row):
    for owner, slab in slab_owners(me, slabs):
        rows = pl.ds(pl.multiple_of(lax.rem(owner, 8) * 128, 128), 64)
        more = pl.ds(pl.multiple_of(lax.rem(owner, 8) * 128 + 64, 64), 64)
        side = owner // 8
        pair_s[side, rows, :] = slab[first_row : first_row + 64, 0:128]
        pair_s[side, more, :] = slab[first_row : first_row + 64, 128:256]
        misc_s[aligned(owner, 16), :] = slab[first_row + 64 : first_row + 80, :]


def slab_targets(me):
    for core in range(2):
        for place, value in enumerate(VALUES):
            yield me ^ value ^ core, core, place


def scalar_rows(scalars, split):
    row = lax.broadcasted_iota(jnp.int32, (16, 128), 0)
    if not split:
        return jnp.where(row == 0, scalars, 0.0)
    upper = low(scalars).astype(F32)
    rest = scalars - upper
    middle = low(rest).astype(F32)
    return jnp.where(row == 0, upper, jnp.where(row == 1, middle, jnp.where(row == 2, rest - middle, 0.0)))


def prepare_judge(pair_s, misc_s, judge):
    wmt_s, wmh_s, wlt_s, wlh_s, headw_s, headr_s, bdt_s, bd_s = judge
    half = jnp.asarray(0.5, BF16)
    for side in range(2):
        columns = pl.ds(side * 128, 128)
        for part in range(4):
            rows = pl.ds(part * 256, 256)
            block = pair_s[side, rows, :] * half
            wmh_s[rows, columns] = block
            wmt_s[columns, rows] = block.T
    last_t = misc_s[:, 0:128]
    wlt_s[...] = last_t * half
    wlh_s[...] = last_t.T * half
    turned = misc_s[:, 128:256].T
    headr_s[...] = turned[32:48, :]
    headw_s[...] = jnp.broadcast_to(misc_s[:, 128:256].astype(F32)[:, 32:33] * 0.5, headw_s.shape)
    row = lax.broadcasted_iota(jnp.int32, (256, 256), 0) % 64
    column = lax.broadcasted_iota(jnp.int32, (256, 256), 1)
    pick = low(jnp.where(column == row // 4 * 16 + row % 4, 1.0, 0.0))
    picked = low(nn(pick, misc_s[...]))
    lane = lax.broadcasted_iota(jnp.int32, (256, 192), 0)
    place = lax.broadcasted_iota(jnp.int32, (256, 192), 1)
    spread = low(jnp.where(lane == 176 + place % 48, 1.0, 0.0))
    diagonal = (lane // 64) == (place // 48)
    band_t = jnp.where(diagonal, nn(picked, spread), 0.0)
    bdt_s[...] = low(band_t * 0.5)
    if bd_s is not None:
        bd_s[...] = low(band_t).T


def judge_scratch(fake):
    shapes = [((256, 1024), BF16), ((1024, 256), BF16), ((256, 128), BF16), ((128, 256), BF16)]
    shapes += [((256, 128), F32), ((16, 256), BF16), ((256, 192), BF16)]
    if fake:
        shapes += [((192, 256), BF16)]
    return shapes


def judge_middle(fresh, q_s, judge, count_all, active, counted, kind, gwl_ref, ghead_ref, loss_ref, new_g2, extra_loss=None):
    _, _, wlt_s, wlh_s, headw_s, headr_s = judge[:6]
    lanes = fresh.shape[1]
    acted_two, slope_two = silu_parts(fresh[:128] + q_s[...])
    q_s[...] = fresh[128:]
    acted_two = low(acted_two)
    yield
    acted_three, slope_three = silu_parts(nn(wlt_s[...], acted_two))
    acted_three = low(acted_three)
    yield
    score = nn(headr_s[...], acted_three)[:1]
    shaped = wide(headw_s[...], lanes) * slope_three
    if kind == "real":
        grad_score = -jax.nn.sigmoid(1.0 - score) * (active / count_all)
        grad_three = low(grad_score * shaped)
        loss_ref[0:1, :] += softplus(1.0 - score) * counted
        yield
        new_g2[0][...] = low(nn(wlh_s[...], grad_three) * slope_two)
    else:
        pull = jax.nn.sigmoid(1.0 + score)
        grad_score = pull * (active / count_all)
        grad_three = low(grad_score * shaped)
        grad_three_gen = low((-GEN_WEIGHT / count_all * active) * shaped)
        loss_ref[0:1, :] += softplus(1.0 + score) * counted
        loss_ref[1:2, :] -= score * counted
        yield
        grad_two_gen = nn(wlh_s[...], grad_three_gen) * slope_two
        new_g2[0][...] = low(grad_two_gen * (pull * (-1.0 / GEN_WEIGHT)))
        new_g2[1][...] = low(grad_two_gen)
    yield
    gwl_ref[...] += nt(acted_two * counted.astype(BF16), grad_three)
    ghead_ref[...] += fold(acted_three.astype(F32) * (grad_score * counted))
    yield


def real_kernel(band, lanes, chunks, count_all):
    rows_n = band + 1
    total = chunks * rows_n

    def kernel(*refs):
        refs = list(refs)

        def take(number):
            taken = refs[:number]
            del refs[:number]
            return taken

        (places,) = take(1)
        slabs = take(2)
        xf, xe, xbelow, xabove = take(4)
        start_refs = take(4)
        (fake_loss,) = take(1)
        send_ref, keep_ref = take(2)
        judge = take(7) + [None]
        pair_s, misc_s = take(2)
        gwm_ref, gwl_ref, gw1_ref, ghead_ref = take(4)
        q_s, g2, g2_new, act_s, slope_s, small = take(6)
        first_s, lastt_s, loss_ref = take(3)
        wmt_s, wmh_s, bdt_s = judge[0], judge[1], judge[6]
        stage = pl.program_id(0)
        has_below, has_above, me = places[1], places[2].astype(F32), places[3]
        step = lax.rem(stage, rows_n)
        row = band - 1 - step
        slot = lax.rem(stage, 2)
        back_ok = (stage >= 2) & (lax.rem(stage - 2, rows_n) != band)
        front_ok = stage < total
        act, slope = act_s.at[slot], slope_s.at[slot]
        halo = row < 0
        active = jnp.where(halo, has_above, 1.0)
        counted = jnp.where(halo, 0.0, 1.0)

        @pl.when(stage == 0)
        def prepare():
            unpack_judge(me, slabs, pair_s, misc_s, 0)
            prepare_judge(pair_s, misc_s, judge)
            for ref, start in zip((gwm_ref, gwl_ref, gw1_ref, ghead_ref), start_refs):
                ref[...] = start[...]
            loss_ref[...] = jnp.zeros_like(loss_ref)

        @pl.when(front_ok & (step == 0) & (has_below > 0))
        def below():
            joined = jnp.zeros((128, lanes), F32)
            for group in range(4):
                acted, _ = silu_parts(nn(bdt_s[...], xbelow[192 * group : 192 * group + 192, :]))
                joined = joined + nn(wmt_s[128:256, 256 * group : 256 * group + 256], low(acted))
            q_s[...] = joined

        @pl.when(front_ok & (step == 0) & (has_below == 0))
        def edge():
            q_s[...] = jnp.zeros_like(q_s)

        def back_small():
            for group in range(4):
                rows = slice(256 * group, 256 * group + 256)
                for start in range(0, lanes, 256):
                    part = slice(start, start + 256)
                    small[rows, part] = low(nn(wmh_s[rows, :], g2[:, part]) * slope[rows, part])
                yield

        def back_middle():
            for group in range(4):
                rows = slice(256 * group, 256 * group + 256)
                gwm_ref[rows, :] += nt(act[rows, :], g2[...])
                yield

        def back_first():
            for group in range(4):
                gw1_ref[...] += nt(xe[0, 192 * group : 192 * group + 192, :], small[256 * group : 256 * group + 256, :])
                yield

        def front_first():
            for group in range(4):
                for start in range(0, lanes, 256):
                    part = slice(start, start + 256)
                    rows = slice(192 * group, 192 * group + 192)
                    x = jnp.where(halo, xabove[rows, part], xf[0, rows, part])
                    acted, slope_new = silu_parts(nn(bdt_s[...], x))
                    act[256 * group : 256 * group + 256, part] = low(acted)
                    slope[256 * group : 256 * group + 256, part] = slope_new
                yield

        def front_middle():
            fresh = nn(wmt_s[...], act[...])
            yield
            yield from judge_middle(
                fresh, q_s, judge, count_all, active, counted, "real", gwl_ref, ghead_ref, loss_ref, (g2_new,)
            )

        def shift():
            g2[0:128, :] = g2[128:256, :]
            g2[128:256, :] = g2_new[...]

        @pl.when(front_ok & back_ok)
        def both():
            interleave(back_small())
            interleave(back_middle(), front_first())
            interleave(front_middle(), back_first())
            shift()

        @pl.when(front_ok & jnp.logical_not(back_ok))
        def front_only():
            interleave(front_first())
            interleave(front_middle())
            shift()

        @pl.when(jnp.logical_not(front_ok) & back_ok)
        def back_only():
            interleave(back_small())
            interleave(back_first(), back_middle())

        @pl.when(stage == total)
        def write():
            turned = gw1_ref[...].T
            lane = lax.broadcasted_iota(jnp.int32, (64, 192), 1)
            summed = jnp.zeros((64, 192), F32)
            for block in range(4):
                summed = summed + jnp.where(lane // 48 == block, turned[64 * block : 64 * block + 64, :], 0.0)
            place = lax.broadcasted_iota(jnp.int32, (192, 128), 0) % 48
            folding = jnp.where(place == lax.broadcasted_iota(jnp.int32, (192, 128), 1), 1.0, 0.0)
            first = jnp.dot(summed, folding, precision=HIGHEST, preferred_element_type=F32)
            for owner in range(SLABS):
                first_s[16 * owner : 16 * owner + 16, :] = jnp.zeros((16, 128), F32)
                first_s[16 * owner : 16 * owner + 4, :] = first[4 * owner : 4 * owner + 4, :]
            lastt_s[...] = gwl_ref[...].T
            scalars = jnp.zeros((1, 128), F32)
            sums = (jnp.sum(fake_loss[2:3, :]), jnp.sum(fake_loss[1:2, :]), jnp.sum(fake_loss[0:1, :]) + jnp.sum(loss_ref[0:1, :]))
            for number, item in enumerate(sums):
                scalars = jnp.where(lax.broadcasted_iota(jnp.int32, (1, 128), 1) == number, item, scalars)
            for owner, core, chip in slab_targets(me):
                side, rows = owner // 8, lax.rem(owner, 8) * 128
                upper = pl.ds(pl.multiple_of(rows, 64), 64)
                lower = pl.ds(pl.multiple_of(rows + 64, 64), 64)
                own = aligned(owner, 16)
                left = jnp.where(side == 0, gwm_ref[upper, 0:128], gwm_ref[upper, 128:256])
                right = jnp.where(side == 0, gwm_ref[lower, 0:128], gwm_ref[lower, 128:256])
                target = (keep_ref, send_ref)[core]
                target[chip, 0:64, 0:128] = left
                target[chip, 0:64, 128:256] = right
                target[chip, 64:80, 0:128] = ghead_ref[own, :]
                target[chip, 64:80, 128:256] = lastt_s[own, :]
                target[chip, 80:96, 0:128] = first_s[own, :]
                target[chip, 80:96, 128:256] = scalar_rows(scalars, False)

    return kernel


def run_real(xt, halos, places, slabs, starts, count_all):
    band, _, positions = xt.shape
    lanes = min(REAL_LANES, positions)
    chunks = positions // lanes
    rows_n = band + 1
    total = chunks * rows_n

    def front_row(t):
        t = jnp.minimum(t, total - 1)
        return (jnp.maximum(band - 1 - lax.rem(t, rows_n), 0), 0, t // rows_n)

    def back_row(t):
        t = jnp.maximum(t - 2, 0)
        return (jnp.maximum(band - 1 - lax.rem(t, rows_n), 0), 0, t // rows_n)

    def halo_row(t):
        return (0, jnp.minimum(t, total - 1) // rows_n)

    specs = [pl.BlockSpec(memory_space=pltpu.SMEM)]
    specs += [pl.BlockSpec((SLABS // 2, 80, 256), lambda t: (0, 2, 0))] * 2
    specs += [pl.BlockSpec((1, 768, lanes), front_row), pl.BlockSpec((1, 768, lanes), back_row)]
    specs += [pl.BlockSpec((768, lanes), halo_row)] * 2
    specs += [pl.BlockSpec(item.shape, lambda t: (0, 0)) for item in starts]
    outs = [
        jax.ShapeDtypeStruct((SLABS // 2, 96, 256), F32),
        jax.ShapeDtypeStruct((SLABS // 2, 96, 256), F32),
    ]
    scratch = judge_scratch(False) + [((2, 1024, 128), BF16), ((256, 256), BF16)]
    scratch += [((1024, 256), F32), ((128, 256), F32), ((192, 256), F32), ((256, 128), F32)]
    scratch += [((128, lanes), F32), ((256, lanes), BF16), ((128, lanes), BF16)]
    scratch += [((2, 1024, lanes), BF16), ((2, 1024, lanes), F32), ((1024, lanes), BF16)]
    scratch += [((256, 128), F32), ((256, 128), F32), ((8, lanes), F32)]
    return pl.pallas_call(
        real_kernel(band, lanes, chunks, count_all),
        grid=(total + 1,),
        in_specs=specs,
        out_specs=[pl.BlockSpec(item.shape, lambda t, n=len(item.shape): (0,) * n) for item in outs],
        out_shape=outs,
        scratch_shapes=[pltpu.VMEM(*item) for item in scratch],
        compiler_params=pltpu.CompilerParams(vmem_limit_bytes=VMEM_LIMIT),
        cost_estimate=cost(5.4e6 * band * positions, 3072 * band * positions),
        name="judge_real",
    )(places, *slabs, xt, xt, *halos, *starts)


def block_forward(stream, gain, first_half_t, second_t):
    scaling, normal = norm_parts(stream)
    normed = low(normal * gain)
    acted, slope = silu_parts(nn(first_half_t, normed))
    acted = low(acted)
    return stream + nn(second_t, acted), (scaling, normal, normed, acted, slope)


def block_backward(grad_out, saved, gain, first, second_half, grad_first, grad_second, grad_gain):
    scaling, normal, normed, acted, slope = saved
    grad_low = low(grad_out)
    grad_second[...] += nt(acted, grad_low)
    grad_inside = low(nn(second_half, grad_low) * slope)
    grad_first[...] += nt(normed, grad_inside)
    grad_normed = nn(first, grad_inside)
    along = grad_normed * normal
    grad_gain[...] += fold(along)
    mean = jnp.mean(along * gain, axis=0, keepdims=True)
    return grad_out + scaling * (grad_normed * gain - normal * mean)


def fake_kernel(band, lanes, chunks, count_all):
    names = ("fake", "gl1", "act", "slope", "normal", "scaling", "normed", "acted", "bslope", "outlow", "values")

    def kernel(*refs):
        refs = list(refs)

        def take(number):
            taken = refs[:number]
            del refs[:number]
            return taken

        (places,) = take(1)
        slabs = take(2)
        xc_ref, xa_ref, xb_ref, codes_ref, lane_ref, consts_ref, spots_ref = take(7)
        send_ref, keep_ref, gwm_ref, gwl_ref, gw1_ref, ghead_ref, loss_ref = take(7)
        judge = take(8)
        pair_s, misc_s = take(2)
        proj_s, projt_s, block_s, blockt_s, blockh_s, fsq_s, fsqt_s, gains_s, total_s = take(9)
        gproj_ref, gblocks_ref, gfsq_ref, ggains_ref = take(4)
        q_s, g2_disc, g2_gen, new_disc, new_gen, small_s, smallgen_s, gradlow_s = take(8)
        stash_a = dict(zip(names, take(len(names))))
        stash_b = dict(zip(names, take(len(names))))
        wmt_s, wmh_s, bdt_s, bd_s = judge[0], judge[1], judge[6], judge[7]
        chunk, step = pl.program_id(0), pl.program_id(1)
        last_step = band // 2
        row_start, has_below, me = places[0], places[1], places[3]
        has_above = places[2].astype(F32)

        @pl.when((chunk == 0) & (step == 0))
        def prepare():
            unpack_judge(me, slabs, pair_s, misc_s, AUTO_ROWS)
            prepare_judge(pair_s, misc_s, judge)
            for owner, slab in slab_owners(me, slabs):
                rows, some = aligned(owner, 48), aligned(owner, 16)
                proj_s[0, rows, :] = slab[0:48, :]
                proj_s[1, rows, :] = slab[48:96, :]
                for index in range(4):
                    block_s[index, some, :] = slab[96 + 16 * index : 112 + 16 * index, :]
            projt_s[0] = proj_s[0].T
            projt_s[1] = proj_s[1].T
            for index in range(4):
                scale = jnp.asarray(0.5 if index % 2 == 0 else 1.0, BF16)
                blockt_s[index] = (block_s[index] * scale).T
                if index % 2 == 1:
                    blockh_s[index // 2] = block_s[index] * jnp.asarray(0.5, BF16)
            tail = misc_s[:, 128:256]
            turned = tail.T
            fsqt_s[0] = turned[0:16, :]
            fsqt_s[1] = turned[16:32, :]
            for index in range(2):
                fsq_s[index] = fsqt_s[index].T
                gains_s[index] = jnp.broadcast_to(tail.astype(F32)[:, 33 + index : 34 + index], (256, 128))
            lane = lax.broadcasted_iota(jnp.int32, (256, 128), 1)
            held = (lane >= 96) & (lane < 99)
            total_s[...] = jnp.broadcast_to(jnp.sum(jnp.where(held, tail.astype(F32), 0.0)), (8, 128))
            for ref in (gwm_ref, gwl_ref, gw1_ref, ghead_ref, loss_ref, gproj_ref, gblocks_ref, gfsq_ref, ggains_ref):
                ref[...] = jnp.zeros_like(ref)

        def latent_values(row):
            consts = consts_ref[...]
            code = codes_ref[pl.ds(row + 1, 1), :]
            turn = jnp.floor((code + 0.5) * wide(consts[0:16], lanes))
            level = wide(consts[16:32], lanes)
            digit = turn - level * jnp.floor((turn + 0.5) * wide(consts[32:48], lanes))
            return low((digit - wide(consts[48:64], lanes)) * wide(consts[64:80], lanes))

        def front(row, x_ref, stash):
            values = latent_values(row)
            stash["values"][...] = values
            gain = wide(gains_s[1], lanes)
            output, saved = block_forward(nn(fsq_s[1], values), gain, blockt_s[2], blockt_s[3])
            outlow = low(output)
            stash["outlow"][...] = outlow
            for name, item in zip(("scaling", "normal", "normed", "acted", "bslope"), saved):
                stash[name][...] = item
            lane = lax.broadcasted_iota(jnp.int32, (1, lanes), 1)
            column = (lane % 16).astype(F32)
            place = (row_start + row).astype(F32)
            high = lane_ref[0:1, :] - 16.0 * place
            broad = lane_ref[1:2, :] - 16.0 * column
            counted = jnp.where(row >= 0, 1.0, 0.0)
            active = jnp.where(row >= 0, 1.0, has_above)
            weight = lane_ref[2:3, :] * counted
            weight_share = weight / wide(total_s[0:1, :], lanes)
            l1_sum = jnp.zeros((1, lanes), F32)
            for group in range(4):
                rows = pl.ds(group * 192, 192)
                recon = nn(proj_s[1, rows, :], outlow)
                stash["fake"][rows, :] = low(recon)
                diff = recon - x_ref[0, rows, :].astype(F32)
                square = diff * diff + 1.0
                inverse = lax.rsqrt(square)
                inside = (wide(spots_ref[0, rows, :], lanes) < high) & (wide(spots_ref[1, rows, :], lanes) < broad)
                l1_sum = l1_sum + jnp.sum(jnp.where(inside, square * inverse, 0.0), axis=0, keepdims=True)
                stash["gl1"][rows, :] = jnp.where(inside, diff * inverse, 0.0) * weight_share
            loss_ref[2:3, :] += l1_sum * weight
            for group in range(4):
                rows, wide_rows = pl.ds(group * 192, 192), pl.ds(group * 256, 256)
                acted, slope = silu_parts(nn(bdt_s[...], stash["fake"][rows, :]))
                stash["act"][wide_rows, :] = low(acted)
                stash["slope"][wide_rows, :] = slope
            fresh = nn(wmt_s[...], stash["act"][...])
            for _ in judge_middle(
                fresh, q_s, judge, count_all, active, counted, "fake", gwl_ref, ghead_ref, loss_ref, (new_disc, new_gen)
            ):
                pass
            g2_disc[128:256, :] = new_disc[...]
            g2_gen[128:256, :] = new_gen[...]

        def below():
            values = latent_values(jnp.int32(band))
            output, _ = block_forward(nn(fsq_s[1], values), wide(gains_s[1], lanes), blockt_s[2], blockt_s[3])
            outlow = low(output)
            joined = jnp.zeros((128, lanes), F32)
            for group in range(4):
                recon = low(nn(proj_s[1, pl.ds(group * 192, 192), :], outlow))
                acted, _ = silu_parts(nn(bdt_s[...], recon))
                joined = joined + nn(wmt_s[128:256, 256 * group : 256 * group + 256], low(acted))
            q_s[...] = joined

        def finish(x_ref, stash):
            for group in range(4):
                wide_rows = pl.ds(group * 256, 256)
                slope = stash["slope"][wide_rows, :]
                smallgen_s[wide_rows, :] = low(nn(wmh_s[wide_rows, :], g2_gen[...]) * slope)
                small_s[wide_rows, :] = low(nn(wmh_s[wide_rows, :], g2_disc[...]) * slope)
            for group in range(4):
                rows, wide_rows = pl.ds(group * 192, 192), pl.ds(group * 256, 256)
                gradlow_s[rows, :] = low(stash["gl1"][rows, :] + nn(bd_s[...], smallgen_s[wide_rows, :]))
            gain = wide(gains_s[1], lanes)
            saved = tuple(stash[name][...] for name in ("scaling", "normal", "normed", "acted", "bslope"))
            grad_output = nn(projt_s[1], gradlow_s[...])
            for group in range(4):
                rows, wide_rows = pl.ds(group * 192, 192), pl.ds(group * 256, 256)
                gw1_ref[...] += nt(stash["fake"][rows, :], small_s[wide_rows, :])
                gwm_ref[wide_rows, :] += nt(stash["act"][wide_rows, :], g2_disc[...])
                gproj_ref[1, rows, :] += nt(gradlow_s[rows, :], stash["outlow"][...])
            grad_start = block_backward(
                grad_output, saved, gain, block_s[2], blockh_s[1],
                gblocks_ref.at[2], gblocks_ref.at[3], ggains_ref.at[1],
            )
            start_low = low(grad_start)
            gfsq_ref[1] += nt(start_low, stash["values"][...])
            grad_values = nn(fsqt_s[1], start_low)
            gain = wide(gains_s[0], lanes)
            stream = nn(projt_s[0], x_ref[0])
            middle, saved = block_forward(stream, gain, blockt_s[0], blockt_s[1])
            middle_low = low(middle)
            tangent = jnp.tanh(nn(fsqt_s[0], middle_low))
            grad_latent = low(grad_values * (1.0 - tangent * tangent))
            gfsq_ref[0] += nt(middle_low, grad_latent)
            grad_stream = block_backward(
                nn(fsq_s[0], grad_latent), saved, gain, block_s[0], blockh_s[0],
                gblocks_ref.at[0], gblocks_ref.at[1], ggains_ref.at[0],
            )
            gproj_ref[0] += nt(x_ref[0], low(grad_stream))
            for ref in (g2_disc, g2_gen):
                ref[0:128, :] = ref[128:256, :]

        @pl.when((step == 0) & (has_below > 0))
        def halo():
            below()

        @pl.when((step == 0) & (has_below == 0))
        def edge():
            q_s[...] = jnp.zeros_like(q_s)

        @pl.when(step == 0)
        def first():
            front(jnp.int32(band - 1), xa_ref, stash_a)
            for ref in (g2_disc, g2_gen):
                ref[0:128, :] = ref[128:256, :]

        @pl.when(step > 0)
        def main():
            front(band - 2 * step, xa_ref, stash_b)
            finish(xc_ref, stash_a)
            front(band - 2 * step - 1, xb_ref, stash_a)
            finish(xa_ref, stash_b)

        @pl.when((chunk == chunks - 1) & (step == last_step))
        def write():
            loss_ref[3:4, 0:128] = total_s[0:1, :]
            for owner, core, chip in slab_targets(me):
                rows, own = aligned(owner, 48), aligned(owner, 16)
                target = (keep_ref, send_ref)[core]
                target[chip, 0:48, :] = gproj_ref[0, rows, :]
                target[chip, 48:96, :] = gproj_ref[1, rows, :]
                for index in range(4):
                    target[chip, 96 + 16 * index : 112 + 16 * index, :] = gblocks_ref[index, own, :]
                target[chip, 160:192, :] = jnp.zeros((32, 256), F32)
                target[chip, 160:176, 0:16] = gfsq_ref[0, own, :]
                target[chip, 160:176, 128:144] = gfsq_ref[1, own, :]
                target[chip, 176:192, 0:128] = ggains_ref[0, own, :]
                target[chip, 176:192, 128:256] = ggains_ref[1, own, :]

    return kernel


def run_fake(xt, places, slabs, extra, count_all):
    band, _, positions = xt.shape
    lanes = min(FAKE_LANES, positions)
    chunks = positions // lanes
    codes, lane_info, consts, spots = extra

    def whole(array):
        return pl.BlockSpec(array.shape, lambda c, s: (0,) * array.ndim)

    def row_spec(shift):
        def index(c, s):
            row = jnp.where(s == 0, band - 1, band - 2 * s + shift)
            return (jnp.maximum(row, 0), 0, c)

        return pl.BlockSpec((1, 768, lanes), index)

    specs = [pl.BlockSpec(memory_space=pltpu.SMEM)]
    specs += [whole(item) for item in slabs]
    specs += [row_spec(1), row_spec(0), row_spec(-1)]
    specs += [
        pl.BlockSpec((codes.shape[0], lanes), lambda c, s: (0, c)),
        pl.BlockSpec((lane_info.shape[0], lanes), lambda c, s: (0, c)),
        whole(consts),
        whole(spots),
    ]
    outs = [
        jax.ShapeDtypeStruct((SLABS // 2, 192, 256), F32),
        jax.ShapeDtypeStruct((SLABS // 2, 192, 256), F32),
        *(jax.ShapeDtypeStruct(shape, F32) for shape in [(1024, 256), (128, 256), (192, 256), (256, 128), (8, lanes)]),
    ]
    scratch = judge_scratch(True) + [((2, 1024, 128), BF16), ((256, 256), BF16)]
    scratch += [((2, 768, 256), BF16), ((2, 256, 768), BF16), ((4, 256, 256), BF16), ((4, 256, 256), BF16)]
    scratch += [((2, 256, 256), BF16), ((2, 256, 16), BF16), ((2, 16, 256), BF16), ((2, 256, 128), F32), ((8, 128), F32)]
    scratch += [((2, 768, 256), F32), ((4, 256, 256), F32), ((2, 256, 16), F32), ((2, 256, 128), F32)]
    scratch += [((128, lanes), F32)] + [((256, lanes), BF16)] * 2 + [((128, lanes), BF16)] * 2
    scratch += [((1024, lanes), BF16)] * 2 + [((768, lanes), BF16)]
    scratch += [
        ((768, lanes), BF16),
        ((768, lanes), F32),
        ((1024, lanes), BF16),
        ((1024, lanes), F32),
        ((256, lanes), F32),
        ((1, lanes), F32),
        ((256, lanes), BF16),
        ((256, lanes), BF16),
        ((256, lanes), F32),
        ((256, lanes), BF16),
        ((16, lanes), BF16),
    ] * 2
    return pl.pallas_call(
        fake_kernel(band, lanes, chunks, count_all),
        grid=(chunks, band // 2 + 1),
        in_specs=specs,
        out_specs=[pl.BlockSpec(item.shape, lambda c, s, n=len(item.shape): (0,) * n) for item in outs],
        out_shape=outs,
        scratch_shapes=[pltpu.VMEM(*item) for item in scratch],
        compiler_params=pltpu.CompilerParams(vmem_limit_bytes=VMEM_LIMIT),
        cost_estimate=cost(1.6e7 * band * positions, 3072 * band * positions),
        name="judge_fake",
    )(places, *slabs, xt, xt, xt, codes, lane_info, consts, spots)


def turn_kernel(pixels_ref, turned_ref):
    frames = pixels_ref.shape[0]
    turned_ref[0] = pixels_ref[...].reshape(frames * 16, 768).T


def turn_pixels(pixels):
    frames, band = pixels.shape[:2]
    part = min(frames, 32)
    return pl.pallas_call(
        turn_kernel,
        grid=(band, frames // part),
        in_specs=[pl.BlockSpec((part, 1, 16, 768), lambda r, c: (c, r, 0, 0))],
        out_specs=pl.BlockSpec((1, 768, part * 16), lambda r, c: (r, 0, c)),
        out_shape=jax.ShapeDtypeStruct((band, 768, frames * 16), BF16),
        compiler_params=pltpu.CompilerParams(vmem_limit_bytes=VMEM_LIMIT),
        cost_estimate=cost(0, 4 * pixels.size),
        name="turn",
    )(pixels)


def count_kernel(codes_ref, counts_ref):
    @pl.when(pl.program_id(0) == 0)
    def clear():
        counts_ref[...] = jnp.zeros_like(counts_ref)

    code = codes_ref[0]
    upper = jnp.floor(code * (1.0 / 256.0))
    lower = code - 256.0 * upper
    bins = lax.broadcasted_iota(jnp.int32, (256, code.shape[1]), 0).astype(F32)
    one, zero = jnp.asarray(1.0, F32), jnp.asarray(0.0, F32)
    counts_ref[...] += nt(low(jnp.where(bins == upper, one, zero)), low(jnp.where(bins == lower, one, zero)))


def count_codes(codes):
    parts, lanes = codes.shape
    return pl.pallas_call(
        count_kernel,
        grid=(parts,),
        in_specs=[pl.BlockSpec((1, 1, lanes), lambda s: (s, 0, 0))],
        out_specs=pl.BlockSpec((256, 256), lambda s: (0, 0)),
        out_shape=jax.ShapeDtypeStruct((256, 256), F32),
        cost_estimate=cost(5e5 * codes.size, 4 * codes.size),
        name="count",
    )(codes[:, None, :])


def frame_kernel(place_ref, clips_ref, bounds_ref, project, matrices, fsq_pair, gain_pair, first_conv, mid_conv, last_conv, head_map, lane_ref, slab_ref, turned_s):
    lanes = lane_ref.shape[1]
    clips = clips_ref[...]
    number = clips.shape[0]
    ahead = lax.broadcasted_iota(jnp.int32, (number, number), 1) < lax.broadcasted_iota(jnp.int32, (number, number), 0)
    starts = nn(low(jnp.where(ahead, 1.0, 0.0)), low(clips))
    frame = (place_ref[0] + lax.broadcasted_iota(jnp.int32, (1, lanes), 1) // 16).astype(F32)
    first, size = wide(starts, lanes), wide(clips, lanes)
    mine = (first <= frame) & (frame < first + size)
    weight = 1.0 / jnp.sum(jnp.where(mine, size, 0.0), axis=0, keepdims=True)
    height, width = bounds_ref[0:1, :], bounds_ref[1:2, :]
    lane_ref[0:1, :] = height
    lane_ref[1:2, :] = width
    lane_ref[2:3, :] = weight
    lane_ref[3:8, :] = jnp.zeros((5, lanes), F32)
    total = jnp.sum(height * width * weight * (3.0 / 16.0), axis=1, keepdims=True)
    for index in range(2):
        slab_ref[48 * index : 48 * index + 48, :] = low(project[index])
    for index in range(4):
        slab_ref[96 + 16 * index : 112 + 16 * index, :] = low(matrices[index])
    slab_ref[160:224, 0:128] = low(mid_conv[0:64, :])
    slab_ref[160:224, 128:256] = low(mid_conv[64:128, :])
    slab_ref[224:240, 0:128] = low(last_conv[...])
    turned_s[...] = jnp.zeros_like(turned_s)
    for index in range(2):
        turned_s[16 * index : 16 * index + 6, :] = fsq_pair[index]
    turned_s[32:33, :] = head_map[...]
    turned_s[33:35, :] = gain_pair[...]
    turned_s[48:96, 0:4] = first_conv[...].T
    upper = low(total).astype(F32)
    rest = total - upper
    middle = low(rest).astype(F32)
    for index, item in enumerate((upper, middle, rest - middle)):
        turned_s[96 + index : 97 + index, 0:1] = item
    slab_ref[224:240, 128:256] = low(turned_s[...].T)


def frame_lanes(first, clip_frames, frame_bounds, masters):
    lanes = frame_bounds.shape[0] * 16
    clips = jnp.broadcast_to(clip_frames.astype(F32)[:, None], (clip_frames.shape[0], 128))
    bounds = jnp.repeat(frame_bounds.T.astype(F32), 16, axis=1)
    operands = list(masters)
    operands[2] = operands[2].transpose(0, 2, 1)
    operands[4] = operands[4].T
    operands[6] = operands[6].T
    operands[7] = operands[7][None, :]
    return pl.pallas_call(
        frame_kernel,
        in_specs=[pl.BlockSpec(memory_space=pltpu.SMEM)] + [pl.BlockSpec(memory_space=pltpu.VMEM)] * 10,
        out_specs=[pl.BlockSpec(memory_space=pltpu.VMEM)] * 2,
        out_shape=[jax.ShapeDtypeStruct((8, lanes), F32), jax.ShapeDtypeStruct((SLAB_ROWS, 256), BF16)],
        scratch_shapes=[pltpu.VMEM((128, 16), F32)],
        name="frames",
    )(first.reshape(1), clips, bounds, *operands)


def passed_along(x, axis, by):
    size = lax.axis_size(axis)
    pairs = [(i, i + by) for i in range(size) if 0 <= i + by < size]
    return lax.ppermute(x, axis, pairs)


def swap(x, axis, bits):
    return lax.ppermute(x, axis, [(i, i ^ bits) for i in range(lax.axis_size(axis))])


def sum_all(x, axis):
    bits, size = 1, lax.axis_size(axis)
    while bits < size:
        x = x + swap(x, axis, bits)
        bits *= 2
    return x


def gather_slabs(slab, beside):
    gathered = slab[None]
    for bits, item in zip((8, 4, 2), beside):
        got = swap(gathered, "dp", bits)
        if item is not None:
            got, _ = lax.optimization_barrier((got, item))
        gathered = jnp.concatenate([gathered, got], axis=0)
    return gathered, swap(gathered, "dp", 1)


def hop_kernel(plans, *refs):
    refs = list(refs)
    inputs, outputs = refs[: 2 * len(plans)], refs[2 * len(plans) :]
    for number, (count, scalars, sent) in enumerate(plans):
        keep_ref, got_ref = inputs[2 * number : 2 * number + 2]
        half = count // 2
        for slab in range(count):
            place, cast, out_ref = slab, F32, outputs[0]
            if half and slab >= half:
                place, cast, out_ref = slab - half, sent, outputs[1]
            out_ref[place] = (keep_ref[slab] + got_ref[slab].astype(F32)).astype(cast)
            if scalars:
                got = got_ref[slab, 80:96, 128:256].astype(F32)
                exact = keep_ref[slab, 80:81, 128:256] + ((got[0:1] + got[1:2]) + got[2:3])
                out_ref[place, 80:96, 128:256] = scalar_rows(exact, cast == BF16).astype(cast)
        outputs = outputs[2 if half else 1 :]


def hop(*sums):
    plans, operands, outs = [], [], []
    for keep, got, scalars, sent in sums:
        count, rows = keep.shape[0], keep.shape[1]
        plans.append((count, scalars, sent))
        operands += [keep, got]
        outs.append(jax.ShapeDtypeStruct((max(count // 2, 1), rows, 256), F32))
        if count > 1:
            outs.append(jax.ShapeDtypeStruct((count // 2, rows, 256), sent))
    vmem = pl.BlockSpec(memory_space=pltpu.VMEM)
    return pl.pallas_call(
        lambda *refs: hop_kernel(plans, *refs),
        in_specs=[vmem] * len(operands),
        out_specs=[vmem] * len(outs),
        out_shape=outs,
        name="hop",
    )(*operands)


def reduce_both(auto_keep, auto_got, judge_send, judge_keep):
    judge_got = swap(judge_send, "dp", 1)
    auto_got, judge_got = lax.optimization_barrier((auto_got, judge_got))
    auto_keep, auto_send, judge_keep, judge_send = hop(
        (auto_keep, auto_got, False, BF16), (judge_keep, judge_got, True, BF16)
    )
    auto_got, judge_got = lax.optimization_barrier((swap(auto_send, "dp", 4), swap(judge_send, "dp", 2)))
    auto_keep, auto_send, judge_keep, judge_send = hop(
        (auto_keep, auto_got, False, F32), (judge_keep, judge_got, True, BF16)
    )
    auto_got, judge_got = lax.optimization_barrier((swap(auto_send, "dp", 8), swap(judge_send, "dp", 4)))
    auto_keep, judge_keep, judge_send = hop((auto_keep, auto_got, False, F32), (judge_keep, judge_got, True, F32))
    auto_got, judge_got = lax.optimization_barrier((swap(auto_keep, "grp", 1), swap(judge_send, "dp", 8)))
    (judge_keep,) = hop((judge_keep, judge_got, True, F32))
    judge_got = swap(judge_keep, "grp", 1)
    return auto_keep[0] + auto_got[0], judge_keep[0] + judge_got[0]


def unpack_auto(total):
    project = total[:96].reshape(2, 48, 256)
    matrices = total[96:160].reshape(4, 16, 256)
    fsq_pair = jnp.stack([total[160:176, 0:6], total[160:176, 128:134]])
    gain_pair = jnp.stack([jnp.sum(total[176:192, 0:128], axis=1), jnp.sum(total[176:192, 128:256], axis=1)])
    return project, matrices, fsq_pair, gain_pair


def unpack_judge_grads(total):
    mid = jnp.concatenate([total[:64, :128], total[:64, 128:]], axis=0)
    head = jnp.sum(total[64:80, 0:128], axis=1)
    last = total[64:80, 128:256].T
    first = total[80:84, 0:48].T
    return first, mid, last, head


def whole_slabs(first, clip_frames, frame_bounds, masters):
    gathered = [lax.all_gather(item, "dp", axis=axis, tiled=True) for item, axis in zip(masters, AXES)]

    def share(array, axis, number):
        size = array.shape[axis] // SLABS
        return lax.slice_in_dim(array, number * size, number * size + size, axis=axis)

    slabs = []
    for number in range(SLABS):
        shares = [share(item, axis, number) for item, axis in zip(gathered, AXES)]
        lane_info, slab = frame_lanes(first, clip_frames, frame_bounds, shares)
        slabs.append(slab)
    held = slabs[0][224, 224:227].astype(F32)
    total = lax.psum(held[0] + held[1] + held[2], "dp")
    upper = low(total)
    middle = low(total - upper.astype(F32))
    lower = low(total - upper.astype(F32) - middle.astype(F32))
    parts = jnp.stack([upper, middle, lower])
    slabs = [slab.at[224, 224:227].set(parts if number == 0 else 0) for number, slab in enumerate(slabs)]
    return lane_info, tuple(jnp.stack([slabs[value ^ core] for value in VALUES]) for core in range(2))


def whole_grads(auto, judge):
    def ordered(send, keep):
        pieces = [None] * SLABS
        for place, value in enumerate(VALUES):
            pieces[value] = keep[place]
            pieces[value ^ 1] = send[place].astype(F32)
        return pieces

    shares = [
        unpack_auto(left) + unpack_judge_grads(right) for left, right in zip(ordered(*auto), ordered(*judge))
    ]
    totals = []
    for index, axis in enumerate(AXES):
        whole = jnp.concatenate([share[index] for share in shares], axis=axis)
        totals.append(lax.psum_scatter(whole, "dp", scatter_dimension=axis, tiled=True))
    scalars = judge[1][0, 80, 128:131]
    totals.append(lax.psum(scalars, "dp"))
    return lax.psum(tuple(totals), "grp")


def adamw(master, moment, square, grad, rate, decay):
    new_moment = BETA_ONE * moment + (1.0 - BETA_ONE) * grad
    new_square = BETA_TWO * square + (1.0 - BETA_TWO) * grad * grad
    update = (
        new_moment
        / (1.0 - BETA_ONE**STEP)
        / (jnp.sqrt(new_square / (1.0 - BETA_TWO**STEP)) + ADAM_EPS)
    )
    return (new_moment, new_square, master - rate * (update + decay * master))


def constants():
    products = np.cumprod((1,) + LEVELS)[:6]
    rows = np.zeros((5, 16), np.float32)
    rows[1] = 1.0
    rows[2] = 1.0
    rows[0, :6] = 1.0 / products
    rows[1, :6] = LEVELS
    rows[2, :6] = 1.0 / np.array(LEVELS)
    rows[3, :6] = HALVES
    rows[4, :6] = 1.0 / np.array(HALVES)
    consts = np.broadcast_to(rows.reshape(80, 1), (80, 128)).astype(np.float32)
    places = np.arange(768)
    down = places // 48 // 4 * 4 + places % 48 // 12
    across = places // 48 % 4 * 4 + places % 48 % 12 // 3
    spots = np.broadcast_to(np.stack([down, across])[:, :, None], (2, 768, 128)).astype(np.float32)
    return jnp.asarray(consts), jnp.asarray(spots)


def on_device(pixels, frame_bounds, clip_frames, codes, *states):
    masters, moments, squares = states[:8], states[8:16], states[16:24]
    frames, band = pixels.shape[:2]
    grp, bands = lax.axis_index("grp"), lax.axis_size("grp")
    me, parts = lax.axis_index("dp"), lax.axis_size("dp")
    shared = parts == SLABS
    positions = frames * 16
    count_all = float(frames * parts * 256)

    code_halos = (passed_along(codes[:, 0], "grp", -1), passed_along(codes[:, band - 1], "grp", 1))
    code_rows = codes.transpose(1, 0, 2).reshape(band, positions).astype(F32)
    counts = count_codes(code_rows)
    xt = turn_pixels(pixels)
    if shared:
        lane_info, slab = frame_lanes(me * frames, clip_frames, frame_bounds, masters)
        slabs = gather_slabs(slab, (counts, None, xt))
    else:
        lane_info, slabs = whole_slabs(me * frames, clip_frames, frame_bounds, masters)
    counts = lax.psum(counts, ("dp", "grp"))
    halos = (passed_along(xt[0], "grp", -1), passed_along(xt[band - 1], "grp", 1))

    places = jnp.stack(
        [grp * band, (grp < bands - 1).astype(jnp.int32), (grp > 0).astype(jnp.int32), me if shared else jnp.int32(0)]
    ).astype(jnp.int32)
    above, under = (item.reshape(1, positions).astype(F32) for item in (code_halos[1], code_halos[0]))
    all_codes = jnp.concatenate([above, code_rows, under], axis=0)
    extra = (all_codes, lane_info, *constants())

    fake_outs = run_fake(xt, places, slabs, extra, count_all)
    halos, counts, fake_outs = lax.optimization_barrier((halos, counts, fake_outs))
    auto, starts = fake_outs[:2], fake_outs[2:7]
    if shared:
        auto_send, auto_keep = auto
        auto_keep, auto_send = hop((auto_keep, swap(auto_send, "dp", 1), False, BF16))
        got = swap(auto_send, "dp", 2)
    judge = run_real(xt, halos, places, slabs, starts, count_all)
    if shared:
        got, judge = lax.optimization_barrier((got, judge))
        auto_total, judge_total = reduce_both(auto_keep, got, *judge)
        totals = (*unpack_auto(auto_total), *unpack_judge_grads(judge_total))
        losses = judge_total[80, 128:131]
    else:
        *totals, losses = whole_grads(auto, judge)

    shares = counts * (1.0 / count_all)
    perplexity = jnp.exp(-jnp.sum(jax.scipy.special.xlogy(shares, shares)))
    results = [
        adamw(
            masters[number],
            moments[number],
            squares[number],
            totals[number],
            RATE_GAIN if number == 3 else RATE_MATRIX,
            0.0 if number == 3 else DECAY,
        )
        for number in range(8)
    ]
    return (
        *(result[0] for result in results),
        *(result[1] for result in results),
        *(result[2] for result in results),
        jnp.stack([losses[0], fake_outs[6][3, 0]]),
        losses[1:3],
        perplexity,
    )


def solution(mesh):
    states = (
        P(None, "dp", None),
        P(None, "dp", None),
        P(None, "dp", None),
        P(None, "dp"),
        P(None, "dp"),
        P("dp", None),
        P(None, "dp"),
        P("dp"),
    )
    return jax.shard_map(
        on_device,
        mesh=mesh,
        in_specs=(P("dp", "grp", None, None), P("dp", None), P(), P("dp", "grp", None)) + states * 3,
        out_specs=states * 3 + (P(), P(), P()),
        check_vma=False,
    )
```

```python
import jax
import jax.numpy as jnp
import numpy as np
from jax import lax
from jax.experimental import pallas as pl
from jax.experimental.pallas import tpu as pltpu
from jax.sharding import PartitionSpec as P

STEP = 10
EPS_NORM = 1e-06
BETA_ONE = 0.9
BETA_TWO = 0.95
ADAM_EPS = 1e-08
DECAY = 0.1
RATE_MATRIX = 0.04
RATE_GAIN = 0.25
GEN_WEIGHT = 0.02
HALVES = (3.5, 3.5, 3.5, 2.0, 2.0, 2.0)
LEVELS = (8, 8, 8, 5, 5, 5)

F32 = jnp.float32
BF16 = jnp.bfloat16
VMEM_LIMIT = 60 * 2**20
FAKE_LANES = 512
REAL_LANES = 1024
REAL_PART = 256
SLABS = 16
VALUES = (0, 8, 4, 12, 2, 10, 6, 14)
WINDOWS = (0, 128, 384, 512)
AUTO_ROWS = 160
SLAB_ROWS = 240
AXES = (1, 1, 1, 1, 1, 0, 1, 0)
HIGHEST = lax.Precision.HIGHEST


def nn(left, right):
    return jnp.dot(left, right, preferred_element_type=F32)


def nt(left, right):
    return lax.dot_general(left, right, (((1,), (1,)), ((), ())), preferred_element_type=F32)


def low(value):
    return value.astype(BF16)


def wide(columns, lanes):
    return jnp.concatenate([columns] * (lanes // 128), axis=1)


def fold(value):
    total = value[:, :128]
    for start in range(128, value.shape[1], 128):
        total = total + value[:, start : start + 128]
    return total


def silu_parts(half):
    turned = jnp.tanh(half)
    upper = 1.0 + turned
    acted = half * upper
    return acted, upper + acted * (1.0 - turned)


def norm_parts(stream):
    scaling = lax.rsqrt(jnp.mean(stream * stream, axis=0, keepdims=True) + EPS_NORM)
    return scaling, stream * scaling


def softplus(value):
    return jnp.maximum(value, 0.0) + jnp.log1p(jnp.exp(-jnp.abs(value)))


def cost(flops, moved):
    return pl.CostEstimate(flops=int(flops), bytes_accessed=int(moved), transcendentals=0)


def aligned(index, size):
    return pl.ds(pl.multiple_of(index * size, size), size)


def interleave(*streams):
    places = []
    for index, (stream, count, *span) in enumerate(streams):
        start, stop = span or (0.0, 1.0)
        places += [(start + (stop - start) * (piece + 0.5) / count, index) for piece in range(count)]
    for _, index in sorted(places):
        next(streams[index][0], None)
    for stream, *_ in streams:
        for _ in stream:
            pass


def slab_owners(me, slabs):
    for core, array in enumerate(slabs):
        for place, value in enumerate(VALUES):
            yield me ^ value ^ core, array.at[place]


def unpack_judge(me, slabs, pair_s, misc_s, first_row):
    for owner, slab in slab_owners(me, slabs):
        rows = pl.ds(pl.multiple_of(lax.rem(owner, 8) * 128, 128), 64)
        more = pl.ds(pl.multiple_of(lax.rem(owner, 8) * 128 + 64, 64), 64)
        side = owner // 8
        pair_s[side, rows, :] = slab[first_row : first_row + 64, 0:128]
        pair_s[side, more, :] = slab[first_row : first_row + 64, 128:256]
        misc_s[aligned(owner, 16), :] = slab[first_row + 64 : first_row + 80, :]


def slab_targets(me):
    for core in range(2):
        for place, value in enumerate(VALUES):
            yield me ^ value ^ core, core, place


def prepare_judge(pair_s, misc_s, judge):
    wmt_s, wmh_s, wlt_s, wlh_s, headw_s, headr_s, bdt_s, bd_s, windows_s = judge
    half = jnp.asarray(0.5, BF16)
    for side in range(2):
        columns = pl.ds(side * 128, 128)
        for part in range(4):
            rows = pl.ds(part * 256, 256)
            block = pair_s[side, rows, :] * half
            wmh_s[rows, columns] = block
            wmt_s[columns, rows] = block.T
    last_t = misc_s[:, 0:128]
    wlt_s[...] = last_t * half
    wlh_s[...] = last_t.T * half
    turned = misc_s[:, 128:256].T
    headr_s[...] = turned[32:48, :]
    headw_s[...] = jnp.broadcast_to(misc_s[:, 128:256].astype(F32)[:, 32:33] * 0.5, headw_s.shape)
    row = lax.broadcasted_iota(jnp.int32, (256, 256), 0) % 64
    column = lax.broadcasted_iota(jnp.int32, (256, 256), 1)
    pick = low(jnp.where(column == row // 4 * 16 + row % 4, 1.0, 0.0))
    picked = low(nn(pick, misc_s[...]))
    lane = lax.broadcasted_iota(jnp.int32, (256, 192), 0)
    place = lax.broadcasted_iota(jnp.int32, (256, 192), 1)
    spread = low(jnp.where(lane == 176 + place % 48, 1.0, 0.0))
    diagonal = (lane // 64) == (place // 48)
    band_t = jnp.where(diagonal, nn(picked, spread), 0.0)
    if bdt_s is not None:
        bdt_s[...] = low(band_t * 0.5)
        bd_s[...] = low(band_t).T
    if windows_s is not None:
        windows_s[...] = jnp.zeros_like(windows_s)
        windows_s[0, :, 0:192] = low(band_t * 0.5)
        lane = lax.broadcasted_iota(jnp.int32, (256, 256), 0)
        place = lax.broadcasted_iota(jnp.int32, (256, 256), 1)
        spread = low(jnp.where((lane == 176 + (place + 32) % 48) & (place >= 64), 1.0, 0.0))
        diagonal = (lane // 64) == (place - 64) // 48
        windows_s[1] = low(jnp.where(diagonal & (place >= 64), nn(picked, spread), 0.0) * 0.5)


def judge_scratch(fake):
    shapes = [((256, 1024), BF16), ((1024, 256), BF16), ((256, 128), BF16), ((128, 256), BF16)]
    shapes += [((256, 128), F32), ((16, 256), BF16)]
    if fake:
        shapes += [((256, 192), BF16), ((192, 256), BF16)]
    else:
        shapes += [((2, 256, 256), BF16)]
    return shapes


def judge_middle(part, act, q_s, judge, count_all, active, counted, kind, held, ghead_ref, loss_ref, new_g2):
    wmt_s, _, wlt_s, wlh_s, headw_s, headr_s = judge[:6]
    two_s, three_s = held
    fresh = nn(wmt_s[...], act[:, part])
    yield
    acted_two, slope_two = silu_parts(fresh[:128] + q_s[:, part])
    q_s[:, part] = fresh[128:]
    acted_two = low(acted_two)
    two_s[:, part] = acted_two * counted.astype(BF16)
    yield
    acted_three, slope_three = silu_parts(nn(wlt_s[...], acted_two))
    acted_three = low(acted_three)
    yield
    score = nn(headr_s[...], acted_three)[:1]
    shaped = wide(headw_s[...], score.shape[1]) * slope_three
    yield
    if kind == "real":
        grad_score = -jax.nn.sigmoid(1.0 - score) * (active / count_all)
        grad_three = low(grad_score * shaped)
        three_s[:, part] = grad_three
        loss_ref[0:1, part] += softplus(1.0 - score) * counted
        yield
        new_g2[0][:, part] = low(nn(wlh_s[...], grad_three) * slope_two)
    else:
        pull = jax.nn.sigmoid(1.0 + score)
        grad_score = pull * (active / count_all)
        three_s[:, part] = low(grad_score * shaped)
        grad_three_gen = low((-GEN_WEIGHT / count_all * active) * shaped)
        loss_ref[0:1, part] += softplus(1.0 + score) * counted
        loss_ref[1:2, part] -= score * counted
        yield
        grad_two_gen = nn(wlh_s[...], grad_three_gen) * slope_two
        new_g2[0][:, part] = low(grad_two_gen * (pull * (-1.0 / GEN_WEIGHT)))
        new_g2[1][:, part] = low(grad_two_gen)
    yield
    ghead_ref[...] += fold(acted_three.astype(F32) * (grad_score * counted))
    yield


def real_kernel(band, lanes, chunks, count_all):
    rows_n = band + 1
    total = chunks * rows_n

    def kernel(*refs):
        refs = list(refs)

        def take(number):
            taken = refs[:number]
            del refs[:number]
            return taken

        (places,) = take(1)
        slabs = take(2)
        xf, xe, xbelow, xabove = take(4)
        start_refs = take(4)
        (fake_loss,) = take(1)
        send_ref, keep_ref = take(2)
        judge = take(6) + [None, None] + take(1)
        pair_s, misc_s = take(2)
        gwm_ref, gwl_ref, gw1_ref, gwin_ref, ghead_ref = take(5)
        q_s, g2, g2_new, act_s, slope_s, small = take(6)
        first_s, lastt_s, loss_ref = take(3)
        held = take(2)
        wmt_s, wmh_s, windows_s = judge[0], judge[1], judge[8]
        stage = pl.program_id(0)
        has_below, has_above, me = places[1], places[2].astype(F32), places[3]
        step = lax.rem(stage, rows_n)
        row = band - 1 - step
        slot = lax.rem(stage, 2)
        back_ok = (stage >= 2) & (lax.rem(stage - 2, rows_n) != band)
        front_ok = stage < total
        act, slope = act_s.at[slot], slope_s.at[slot]
        halo = row < 0
        active = jnp.where(halo, has_above, 1.0)
        counted = jnp.where(halo, 0.0, 1.0)

        @pl.when(stage == 0)
        def prepare():
            unpack_judge(me, slabs, pair_s, misc_s, 0)
            prepare_judge(pair_s, misc_s, judge)
            for ref, start in zip((gwm_ref, gwl_ref, gw1_ref, ghead_ref), start_refs):
                ref[...] = start[...]
            loss_ref[...] = jnp.zeros_like(loss_ref)
            gwin_ref[...] = jnp.zeros_like(gwin_ref)

        @pl.when(front_ok & (step == 0) & (has_below > 0))
        def below():
            joined = jnp.zeros((128, lanes), F32)
            for group in range(4):
                x = xbelow[:, :, WINDOWS[group] : WINDOWS[group] + 256].reshape(lanes, 256)
                acted, _ = silu_parts(nt(windows_s[group % 2], x))
                joined = joined + nn(wmt_s[128:256, 256 * group : 256 * group + 256], low(acted))
            q_s[...] = joined

        @pl.when(front_ok & (step == 0) & (has_below == 0))
        def edge():
            q_s[...] = jnp.zeros_like(q_s)

        def back_small():
            for group in range(4):
                rows = slice(256 * group, 256 * group + 256)
                for start in range(0, lanes, 256):
                    part = slice(start, start + 256)
                    small[rows, part] = low(nn(wmh_s[rows, :], g2[:, part]) * slope[rows, part])
                    yield

        def back_middle():
            for group in range(4):
                rows = slice(256 * group, 256 * group + 256)
                gwm_ref[rows, :] += nt(act[rows, :], g2[...])
                yield

        def back_first():
            for group in range(4):
                x = xe[:, 0, :, WINDOWS[group] : WINDOWS[group] + 256].reshape(lanes, 256)
                gwin_ref[group % 2] += nn(small[256 * group : 256 * group + 256, :], x)
                yield

        def front_first():
            for group in range(4):
                for start in range(0, lanes, 256):
                    part = slice(start, start + 256)
                    some, window = slice(start // 16, start // 16 + 16), slice(WINDOWS[group], WINDOWS[group] + 256)
                    x = jnp.where(halo, xabove[some, :, window], xf[some, 0, :, window]).reshape(256, 256)
                    acted, slope_new = silu_parts(nt(windows_s[group % 2], x))
                    act[256 * group : 256 * group + 256, part] = low(acted)
                    slope[256 * group : 256 * group + 256, part] = slope_new
                    yield

        def front_middle(part):
            return judge_middle(
                part, act, q_s, judge, count_all, active, counted, "real", held, ghead_ref, loss_ref, (g2_new,)
            )

        def front_last():
            gwl_ref[...] += nt(held[0][...], held[1][...])
            yield

        def shift():
            g2[0:128, :] = g2[128:256, :]
            g2[128:256, :] = g2_new[...]

        parts = [slice(start, start + REAL_PART) for start in range(0, lanes, REAL_PART)]

        @pl.when(front_ok & back_ok)
        def both():
            interleave(
                (back_small(), lanes // 64, 0.0, 0.8),
                (back_middle(), 4, 0.0, 0.8),
                (front_first(), lanes // 64, 0.2, 1.0),
            )
            interleave(*((front_middle(part), 7) for part in parts), (back_first(), 4))
            interleave((front_last(), 1))
            shift()

        @pl.when(front_ok & jnp.logical_not(back_ok))
        def front_only():
            interleave((front_first(), 1))
            interleave(*((front_middle(part), 7) for part in parts))
            interleave((front_last(), 1))
            shift()

        @pl.when(jnp.logical_not(front_ok) & back_ok)
        def back_only():
            interleave((back_small(), 1))
            interleave((back_first(), 4), (back_middle(), 4))

        @pl.when(stage == total)
        def write():
            turned = gw1_ref[...].T
            lane = lax.broadcasted_iota(jnp.int32, (64, 192), 1)
            summed = jnp.zeros((64, 192), F32)
            for block in range(4):
                summed = summed + jnp.where(lane // 48 == block, turned[64 * block : 64 * block + 64, :], 0.0)
            place = lax.broadcasted_iota(jnp.int32, (192, 128), 0) % 48
            folding = jnp.where(place == lax.broadcasted_iota(jnp.int32, (192, 128), 1), 1.0, 0.0)
            first = jnp.dot(summed, folding, precision=HIGHEST, preferred_element_type=F32)
            lane = lax.broadcasted_iota(jnp.int32, (64, 256), 1)
            place = lax.broadcasted_iota(jnp.int32, (256, 128), 0)
            for odd in range(2):
                summed = jnp.zeros((64, 256), F32)
                for block in range(4):
                    start = 64 * odd + 48 * block
                    inside = (lane >= start) & (lane < start + 48)
                    summed = summed + jnp.where(inside, gwin_ref[odd, 64 * block : 64 * block + 64, :], 0.0)
                folding = jnp.where((place + 32 * odd) % 48 == lax.broadcasted_iota(jnp.int32, (256, 128), 1), 1.0, 0.0)
                first = first + jnp.dot(summed, folding, precision=HIGHEST, preferred_element_type=F32)
            for owner in range(SLABS):
                first_s[16 * owner : 16 * owner + 16, :] = jnp.zeros((16, 128), F32)
                first_s[16 * owner : 16 * owner + 4, :] = first[4 * owner : 4 * owner + 4, :]
            lastt_s[...] = gwl_ref[...].T
            scalars = jnp.zeros((1, 128), F32)
            sums = (jnp.sum(fake_loss[2:3, :]), jnp.sum(fake_loss[1:2, :]), jnp.sum(fake_loss[0:1, :]) + jnp.sum(loss_ref[0:1, :]))
            for number, item in enumerate(sums):
                scalars = jnp.where(lax.broadcasted_iota(jnp.int32, (1, 128), 1) == number, item, scalars)
            for owner, core, chip in slab_targets(me):
                side, rows = owner // 8, lax.rem(owner, 8) * 128
                upper = pl.ds(pl.multiple_of(rows, 64), 64)
                lower = pl.ds(pl.multiple_of(rows + 64, 64), 64)
                own = aligned(owner, 16)
                left = jnp.where(side == 0, gwm_ref[upper, 0:128], gwm_ref[upper, 128:256])
                right = jnp.where(side == 0, gwm_ref[lower, 0:128], gwm_ref[lower, 128:256])
                target = (keep_ref, send_ref)[core]
                target[chip, 0:64, 0:128] = left
                target[chip, 0:64, 128:256] = right
                target[chip, 64:80, 0:128] = ghead_ref[own, :]
                target[chip, 64:80, 128:256] = lastt_s[own, :]
                target[chip, 80:96, 0:128] = first_s[own, :]
                target[chip, 80:96, 128:256] = jnp.where(lax.broadcasted_iota(jnp.int32, (16, 128), 0) < 3, scalars, 0.0)

    return kernel


def run_real(pixels, halos, places, slabs, starts, count_all):
    frames, band = pixels.shape[:2]
    positions = frames * 16
    lanes = min(REAL_LANES, positions)
    chunks = positions // lanes
    rows_n = band + 1
    total = chunks * rows_n

    halo_spec = pl.BlockSpec((lanes // 16, 16, 768), lambda t: (jnp.minimum(t, total - 1) // rows_n, 0, 0))
    specs = [pl.BlockSpec(memory_space=pltpu.SMEM)]
    specs += [pl.BlockSpec((SLABS // 2, 80, 256), lambda t: (0, 2, 0))] * 2
    specs += stage_rows(band, lanes, chunks)
    specs += [halo_spec] * 2
    specs += [pl.BlockSpec(item.shape, lambda t: (0, 0)) for item in starts]
    outs = [
        jax.ShapeDtypeStruct((SLABS // 2, 96, 256), F32),
        jax.ShapeDtypeStruct((SLABS // 2, 96, 256), F32),
    ]
    scratch = judge_scratch(False) + [((2, 1024, 128), BF16), ((256, 256), BF16)]
    scratch += [((1024, 256), F32), ((128, 256), F32), ((192, 256), F32), ((2, 256, 256), F32), ((256, 128), F32)]
    scratch += [((128, lanes), F32), ((256, lanes), BF16), ((128, lanes), BF16)]
    scratch += [((2, 1024, lanes), BF16), ((2, 1024, lanes), F32), ((1024, lanes), BF16)]
    scratch += [((256, 128), F32), ((256, 128), F32), ((8, lanes), F32)]
    scratch += [((128, lanes), BF16), ((256, lanes), BF16)]
    return pl.pallas_call(
        real_kernel(band, lanes, chunks, count_all),
        grid=(total + 1,),
        in_specs=specs,
        out_specs=[pl.BlockSpec(item.shape, lambda t, n=len(item.shape): (0,) * n) for item in outs],
        out_shape=outs,
        scratch_shapes=[pltpu.VMEM(*item) for item in scratch],
        compiler_params=pltpu.CompilerParams(vmem_limit_bytes=VMEM_LIMIT),
        cost_estimate=cost(5.4e6 * band * positions, 3072 * band * positions),
        name="judge_real",
    )(places, *slabs, pixels, pixels, *halos, *starts)


def block_steps(stream, gain, first_half_t, second_t):
    scaling, normal = norm_parts(stream)
    normed = low(normal * gain)
    yield None
    acted, slope = silu_parts(nn(first_half_t[...], normed))
    acted = low(acted)
    yield None
    yield stream + nn(second_t[...], acted), (scaling, normal, normed, acted, slope)


def fake_kernel(band, lanes, chunks, count_all):
    rows_n = band + 1
    total = chunks * rows_n
    halves = [slice(start, start + 256) for start in range(0, lanes, 256)]

    def kernel(*refs):
        refs = list(refs)

        def take(number):
            taken = refs[:number]
            del refs[:number]
            return taken

        (places,) = take(1)
        slabs = take(2)
        xf_ref, xe_ref, codes_ref, lane_ref, consts_ref, spots_ref = take(6)
        send_ref, keep_ref, gwm_ref, gwl_ref, gw1_ref, ghead_ref, loss_ref = take(7)
        judge = take(8) + [None]
        pair_s, misc_s = take(2)
        proj_s, projt_s, block_s, blockt_s, blockh_s, fsq_s, fsqt_s, gains_s, total_s = take(9)
        gproj_ref, gprojt_ref, gblocks_ref, gfsq_ref, gfsqt_ref, ggains_ref = take(6)
        q_s, g2_disc, g2_gen, new_disc, new_gen, small_s, smallgen_s, gradlow_s, xt_s = take(9)
        fake_s, gl1_s, act_s, slope_s = take(4)
        saved_s = take(5)
        outlow_s, values_s = take(2)
        encoded_s = take(7)
        outer_s, inner_s, start_s, latent_s, stream_s = take(5)
        held = take(2)
        wmt_s, wmh_s, bdt_s, bd_s = judge[0], judge[1], judge[6], judge[7]
        stage = pl.program_id(0)
        row_start, has_below, me = places[0], places[1], places[3]
        has_above = places[2].astype(F32)
        step = lax.rem(stage, rows_n)
        row = band - 1 - step
        slot, slot_three, back_three = lax.rem(stage, 2), lax.rem(stage, 3), lax.rem(stage + 1, 3)
        back_ok = (stage >= 2) & (lax.rem(stage - 2, rows_n) != band)
        front_ok = stage < total
        gl1, act, slope = gl1_s.at[slot], act_s.at[slot], slope_s.at[slot]
        fake, fake_back = fake_s.at[slot_three], fake_s.at[back_three]
        counted = jnp.where(row >= 0, 1.0, 0.0)
        active = jnp.where(row >= 0, 1.0, has_above)

        @pl.when(stage == 0)
        def prepare():
            unpack_judge(me, slabs, pair_s, misc_s, AUTO_ROWS)
            prepare_judge(pair_s, misc_s, judge)
            for owner, slab in slab_owners(me, slabs):
                rows, some = aligned(owner, 48), aligned(owner, 16)
                proj_s[0, rows, :] = slab[0:48, :]
                proj_s[1, rows, :] = slab[48:96, :]
                for index in range(4):
                    block_s[index, some, :] = slab[96 + 16 * index : 112 + 16 * index, :]
            projt_s[0] = proj_s[0].T
            projt_s[1] = proj_s[1].T
            for index in range(4):
                scale = jnp.asarray(0.5 if index % 2 == 0 else 1.0, BF16)
                blockt_s[index] = (block_s[index] * scale).T
                if index % 2 == 1:
                    blockh_s[index // 2] = block_s[index] * jnp.asarray(0.5, BF16)
            tail = misc_s[:, 128:256]
            turned = tail.T
            fsqt_s[0] = turned[0:16, :]
            fsqt_s[1] = turned[16:32, :]
            for index in range(2):
                fsq_s[index] = fsqt_s[index].T
                gains_s[index] = jnp.broadcast_to(tail.astype(F32)[:, 33 + index : 34 + index], (256, 128))
            lane = lax.broadcasted_iota(jnp.int32, (256, 128), 1)
            held = (lane >= 96) & (lane < 99)
            total_s[...] = jnp.broadcast_to(jnp.sum(jnp.where(held, tail.astype(F32), 0.0)), (8, 128))
            for ref in (gwm_ref, gwl_ref, gw1_ref, ghead_ref, loss_ref, gproj_ref, gprojt_ref, gblocks_ref, gfsqt_ref, ggains_ref):
                ref[...] = jnp.zeros_like(ref)

        def latent_values(row):
            consts = consts_ref[...]
            code = codes_ref[pl.ds(row + 1, 1), :]
            turn = jnp.floor((code + 0.5) * wide(consts[0:16], lanes))
            level = wide(consts[16:32], lanes)
            digit = turn - level * jnp.floor((turn + 0.5) * wide(consts[32:48], lanes))
            return low((digit - wide(consts[48:64], lanes)) * wide(consts[64:80], lanes))

        @pl.when(front_ok & (step == 0) & (has_below > 0))
        def below():
            values = latent_values(jnp.int32(band))
            outputs = list(block_steps(nn(fsq_s[1], values), wide(gains_s[1], lanes), blockt_s.at[2], blockt_s.at[3]))
            outlow = low(outputs[-1][0])
            joined = jnp.zeros((128, lanes), F32)
            for group in range(4):
                recon = low(nn(proj_s[1, pl.ds(group * 192, 192), :], outlow))
                acted, _ = silu_parts(nn(bdt_s[...], recon))
                joined = joined + nn(wmt_s[128:256, 256 * group : 256 * group + 256], low(acted))
            q_s[...] = joined

        @pl.when(front_ok & (step == 0) & (has_below == 0))
        def edge():
            q_s[...] = jnp.zeros_like(q_s)

        def front_block(part):
            values = values_s[slot_three, :, part]
            width = values.shape[1]
            stream = nn(fsq_s[1], values)
            yield
            result = None
            for result in block_steps(stream, wide(gains_s[1], width), blockt_s.at[2], blockt_s.at[3]):
                yield
            output, saved = result
            outlow_s[slot_three, :, part] = low(output)
            for ref, item in zip(saved_s, saved):
                ref[slot_three, :, part] = item
            yield

        def front_turn():
            for part in halves:
                some = slice(part.start // 16, part.stop // 16)
                for column in range(0, 768, 256):
                    xt_s[column : column + 256, part] = xf_ref[some, 0, :, column : column + 256].reshape(256, 256).T
                    yield

        def front_recon():
            lane = lax.broadcasted_iota(jnp.int32, (1, lanes), 1)
            column = (lane % 16).astype(F32)
            place = (row_start + row).astype(F32)
            high = lane_ref[0:1, :] - 16.0 * place
            broad = lane_ref[1:2, :] - 16.0 * column
            weight = lane_ref[2:3, :] * counted
            weight_share = weight / wide(total_s[0:1, :], lanes)
            sums = [jnp.zeros((1, 256), F32) for _ in halves]
            for group in range(4):
                rows = slice(group * 192, group * 192 + 192)
                for index, part in enumerate(halves):
                    recon = nn(proj_s[1, rows, :], outlow_s[slot_three, :, part])
                    fake[rows, part] = low(recon)
                    diff = recon - xt_s[rows, part].astype(F32)
                    square = diff * diff + 1.0
                    inside = (wide(spots_ref[0, rows, :], 256) < high[:, part]) & (
                        wide(spots_ref[1, rows, :], 256) < broad[:, part]
                    )
                    share = lax.rsqrt(square) * jnp.where(inside, weight_share[:, part], 0.0)
                    gl1[rows, part] = diff * share
                    sums[index] = sums[index] + jnp.sum(square * share, axis=0, keepdims=True)
                    yield
            loss_ref[2:3, :] += jnp.concatenate(sums, axis=1) * wide(total_s[0:1, :], lanes)

        def front_first():
            for group in range(4):
                for part in halves:
                    acted, slope_new = silu_parts(nn(bdt_s[...], fake[192 * group : 192 * group + 192, part]))
                    act[256 * group : 256 * group + 256, part] = low(acted)
                    slope[256 * group : 256 * group + 256, part] = slope_new
                    yield

        def front_middle(part):
            return judge_middle(
                part, act, q_s, judge, count_all, active, counted, "fake", held, ghead_ref, loss_ref, (new_disc, new_gen)
            )

        def front_last():
            gwl_ref[...] += nt(held[0][...], held[1][...])
            yield

        def back_gen():
            for group in range(4):
                rows = slice(256 * group, 256 * group + 256)
                for part in halves:
                    smallgen_s[rows, part] = low(nn(wmh_s[rows, :], g2_gen[:, part]) * slope[rows, part])
                    yield

        def back_disc():
            for group in range(4):
                rows = slice(256 * group, 256 * group + 256)
                for part in halves:
                    small_s[rows, part] = low(nn(wmh_s[rows, :], g2_disc[:, part]) * slope[rows, part])
                    yield

        def back_recon():
            for group in range(4):
                rows = slice(group * 192, group * 192 + 192)
                gradlow_s[rows, :] = low(gl1[rows, :] + nn(bd_s[...], smallgen_s[256 * group : 256 * group + 256, :]))
                yield

        def back_first():
            for group in range(4):
                rows = slice(group * 192, group * 192 + 192)
                gw1_ref[...] += nt(fake_back[rows, :], small_s[256 * group : 256 * group + 256, :])
                yield

        def back_middle():
            for group in range(4):
                rows = slice(256 * group, 256 * group + 256)
                gwm_ref[rows, :] += nt(act[rows, :], g2_disc[...])
                yield

        def back_project():
            for group in range(4):
                rows = slice(group * 192, group * 192 + 192)
                gproj_ref[1, rows, :] += nt(gradlow_s[rows, :], outlow_s[back_three])
                yield

        def back_encode(part):
            some = slice(part.start // 16, part.stop // 16)
            stream = nt(projt_s[0], xe_ref[some].reshape(part.stop - part.start, 768))
            yield
            result = None
            for result in block_steps(
                stream, wide(gains_s[0], part.stop - part.start), blockt_s.at[0], blockt_s.at[1]
            ):
                yield
            middle, saved = result
            middle_low = low(middle)
            for ref, item in zip(encoded_s, (*saved, middle_low, nn(fsqt_s[0], middle_low))):
                ref[:, part] = item
            yield

        def back_block(grad_out, saved, index, part):
            scaling, normal, slope_in = saved
            gain = wide(gains_s[index], part.stop - part.start)
            outer = low(grad_out)
            outer_s[index, :, part] = outer
            grad_acted = nn(blockh_s[index], outer)
            yield None
            inner = low(grad_acted * slope_in)
            inner_s[index, :, part] = inner
            grad_normed = nn(block_s[2 * index], inner)
            yield None
            along = grad_normed * normal
            ggains_ref[index] += fold(along)
            mean = jnp.mean(along * gain, axis=0, keepdims=True)
            yield grad_out + scaling * (grad_normed * gain - normal * mean)

        def back_chain(part):
            grad_out = nn(projt_s[1], gradlow_s[:, part])
            yield
            saved = tuple(saved_s[n][back_three, :, part] for n in (0, 1, 4))
            grad_start = None
            for grad_start in back_block(grad_out, saved, 1, part):
                yield
            start_low = low(grad_start)
            start_s[:, part] = start_low
            grad_values = nn(fsqt_s[1], start_low)
            yield
            tangent = jnp.tanh(encoded_s[6][:, part])
            grad_latent = low(grad_values * (1.0 - tangent * tangent))
            latent_s[:, part] = grad_latent
            grad_middle = nn(fsq_s[0], grad_latent)
            yield
            saved = tuple(encoded_s[n][:, part] for n in (0, 1, 4))
            grad_stream = None
            for grad_stream in back_block(grad_middle, saved, 0, part):
                yield
            stream_s[:, part] = low(grad_stream)
            yield

        def back_weights():
            gblocks_ref[3] += nt(saved_s[3][back_three], outer_s[1])
            yield
            gblocks_ref[2] += nt(saved_s[2][back_three], inner_s[1])
            yield
            gfsqt_ref[1] += nt(values_s[back_three], start_s[...])
            gfsqt_ref[0] += nt(latent_s[...], encoded_s[5][...])
            yield
            gblocks_ref[1] += nt(encoded_s[3][...], outer_s[0])
            yield
            gblocks_ref[0] += nt(encoded_s[2][...], inner_s[0])
            yield
            for start in range(0, 768, 256):
                x = xe_ref[:, 0, :, start : start + 256].reshape(lanes, 256)
                gprojt_ref[:, start : start + 256] += nn(stream_s[...], x)
                yield

        def shift():
            for ref, new in ((g2_disc, new_disc), (g2_gen, new_gen)):
                ref[0:128, :] = ref[128:256, :]
                ref[128:256, :] = new[...]

        @pl.when(front_ok & back_ok)
        def both():
            values_s[slot_three] = latent_values(row)
            interleave(
                (back_gen(), 4 * len(halves)),
                *((front_block(part), 5) for part in halves),
                *((back_encode(part), 5) for part in halves),
                (front_turn(), 6),
            )
            interleave(
                (back_recon(), 4, 0.0, 0.8), (back_disc(), 4 * len(halves)), (front_recon(), 4 * len(halves), 0.2, 1.0)
            )
            interleave(
                *((back_chain(part), 10) for part in halves),
                (back_middle(), 4, 0.0, 0.8),
                (front_first(), 4 * len(halves), 0.2, 1.0),
                (back_first(), 4),
                (back_project(), 4),
            )
            interleave(*((front_middle(part), 7) for part in halves), (back_weights(), 8))
            interleave((front_last(), 1))
            shift()

        @pl.when(front_ok & jnp.logical_not(back_ok))
        def front_only():
            values_s[slot_three] = latent_values(row)
            interleave(*((front_block(part), 5) for part in halves), (front_turn(), 6))
            interleave((front_recon(), 1))
            interleave((front_first(), 1))
            interleave(*((front_middle(part), 7) for part in halves))
            interleave((front_last(), 1))
            shift()

        @pl.when(jnp.logical_not(front_ok) & back_ok)
        def back_only():
            interleave((back_gen(), 4 * len(halves)), *((back_encode(part), 5) for part in halves))
            interleave((back_recon(), 4), (back_disc(), 4 * len(halves)))
            interleave(
                *((back_chain(part), 10) for part in halves), (back_middle(), 4), (back_first(), 4), (back_project(), 4)
            )
            interleave((back_weights(), 1))

        @pl.when(stage == total)
        def write():
            loss_ref[3:4, 0:128] = total_s[0:1, :]
            gproj_ref[0] = gprojt_ref[...].T
            for index in range(2):
                gfsq_ref[index] = gfsqt_ref[index].T
            for owner, core, chip in slab_targets(me):
                rows, own = aligned(owner, 48), aligned(owner, 16)
                target = (keep_ref, send_ref)[core]
                target[chip, 0:48, :] = gproj_ref[0, rows, :]
                target[chip, 48:96, :] = gproj_ref[1, rows, :]
                for index in range(4):
                    target[chip, 96 + 16 * index : 112 + 16 * index, :] = gblocks_ref[index, own, :]
                target[chip, 160:192, :] = jnp.zeros((32, 256), F32)
                target[chip, 160:176, 0:16] = gfsq_ref[0, own, :]
                target[chip, 160:176, 128:144] = gfsq_ref[1, own, :]
                target[chip, 176:192, 0:128] = ggains_ref[0, own, :]
                target[chip, 176:192, 128:256] = ggains_ref[1, own, :]

    return kernel


def stage_rows(band, lanes, chunks):
    rows_n = band + 1
    total = chunks * rows_n

    def front(t):
        t = jnp.minimum(t, total - 1)
        return (t // rows_n, jnp.maximum(band - 1 - lax.rem(t, rows_n), 0), 0, 0)

    def back(t):
        t = jnp.maximum(t - 2, 0)
        return (t // rows_n, jnp.maximum(band - 1 - lax.rem(t, rows_n), 0), 0, 0)

    block = (lanes // 16, 1, 16, 768)
    return pl.BlockSpec(block, front), pl.BlockSpec(block, back)


def run_fake(pixels, places, slabs, extra, count_all):
    frames, band = pixels.shape[:2]
    positions = frames * 16
    lanes = min(FAKE_LANES, positions)
    chunks = positions // lanes
    total = chunks * (band + 1)
    codes, lane_info, consts, spots = extra

    def whole(array):
        return pl.BlockSpec(array.shape, lambda t: (0,) * array.ndim)

    def chunk_spec(array):
        return pl.BlockSpec((array.shape[0], lanes), lambda t: (0, jnp.minimum(t, total - 1) // (band + 1)))

    specs = [pl.BlockSpec(memory_space=pltpu.SMEM)]
    specs += [whole(item) for item in slabs]
    specs += stage_rows(band, lanes, chunks)
    specs += [chunk_spec(codes), chunk_spec(lane_info), whole(consts), whole(spots)]
    outs = [
        jax.ShapeDtypeStruct((SLABS // 2, 192, 256), F32),
        jax.ShapeDtypeStruct((SLABS // 2, 192, 256), F32),
        *(jax.ShapeDtypeStruct(shape, F32) for shape in [(1024, 256), (128, 256), (192, 256), (256, 128), (8, lanes)]),
    ]
    scratch = judge_scratch(True) + [((2, 1024, 128), BF16), ((256, 256), BF16)]
    scratch += [((2, 768, 256), BF16), ((2, 256, 768), BF16), ((4, 256, 256), BF16), ((4, 256, 256), BF16)]
    scratch += [((2, 256, 256), BF16), ((2, 256, 16), BF16), ((2, 16, 256), BF16), ((2, 256, 128), F32), ((8, 128), F32)]
    scratch += [((2, 768, 256), F32), ((256, 768), F32), ((4, 256, 256), F32), ((2, 256, 16), F32), ((2, 16, 256), F32), ((2, 256, 128), F32)]
    scratch += [((128, lanes), F32)] + [((256, lanes), BF16)] * 2 + [((128, lanes), BF16)] * 2
    scratch += [((1024, lanes), BF16)] * 2 + [((768, lanes), BF16)] * 2
    scratch += [((3, 768, lanes), BF16), ((2, 768, lanes), F32), ((2, 1024, lanes), BF16), ((2, 1024, lanes), F32)]
    scratch += [((3, 1, lanes), F32), ((3, 256, lanes), F32), ((3, 256, lanes), BF16), ((3, 256, lanes), BF16)]
    scratch += [((3, 256, lanes), F32), ((3, 256, lanes), BF16), ((3, 16, lanes), BF16)]
    scratch += [((1, lanes), F32), ((256, lanes), F32), ((256, lanes), BF16), ((256, lanes), BF16)]
    scratch += [((256, lanes), F32), ((256, lanes), BF16), ((16, lanes), F32)]
    scratch += [((2, 256, lanes), BF16)] * 2 + [((256, lanes), BF16), ((16, lanes), BF16), ((256, lanes), BF16)]
    scratch += [((128, lanes), BF16), ((256, lanes), BF16)]
    return pl.pallas_call(
        fake_kernel(band, lanes, chunks, count_all),
        grid=(total + 1,),
        in_specs=specs,
        out_specs=[pl.BlockSpec(item.shape, lambda t, n=len(item.shape): (0,) * n) for item in outs],
        out_shape=outs,
        scratch_shapes=[pltpu.VMEM(*item) for item in scratch],
        compiler_params=pltpu.CompilerParams(vmem_limit_bytes=VMEM_LIMIT),
        cost_estimate=cost(1.6e7 * band * positions, 3072 * band * positions),
        name="judge_fake",
    )(places, *slabs, pixels, pixels, codes, lane_info, consts, spots)


def count_kernel(codes_ref, counts_ref):
    @pl.when(pl.program_id(0) == 0)
    def clear():
        counts_ref[...] = jnp.zeros_like(counts_ref)

    code = codes_ref[0]
    upper = jnp.floor(code * (1.0 / 256.0))
    lower = code - 256.0 * upper
    bins = lax.broadcasted_iota(jnp.int32, (256, code.shape[1]), 0).astype(F32)
    one, zero = jnp.asarray(1.0, F32), jnp.asarray(0.0, F32)
    counts_ref[...] += nt(low(jnp.where(bins == upper, one, zero)), low(jnp.where(bins == lower, one, zero)))


def count_codes(codes):
    parts, lanes = codes.shape
    return pl.pallas_call(
        count_kernel,
        grid=(parts,),
        in_specs=[pl.BlockSpec((1, 1, lanes), lambda s: (s, 0, 0))],
        out_specs=pl.BlockSpec((256, 256), lambda s: (0, 0)),
        out_shape=jax.ShapeDtypeStruct((256, 256), F32),
        cost_estimate=cost(5e5 * codes.size, 4 * codes.size),
        name="count",
    )(codes[:, None, :])


def frame_kernel(place_ref, clips_ref, bounds_ref, project, matrices, fsq_pair, gain_pair, first_conv, mid_conv, last_conv, head_map, lane_ref, slab_ref, turned_s):
    lanes = lane_ref.shape[1]
    clips = clips_ref[...]
    number = clips.shape[0]
    ahead = lax.broadcasted_iota(jnp.int32, (number, number), 1) < lax.broadcasted_iota(jnp.int32, (number, number), 0)
    starts = nn(low(jnp.where(ahead, 1.0, 0.0)), low(clips))
    frame = (place_ref[0] + lax.broadcasted_iota(jnp.int32, (1, lanes), 1) // 16).astype(F32)
    first, size = wide(starts, lanes), wide(clips, lanes)
    mine = (first <= frame) & (frame < first + size)
    weight = 1.0 / jnp.sum(jnp.where(mine, size, 0.0), axis=0, keepdims=True)
    height, width = bounds_ref[0:1, :], bounds_ref[1:2, :]
    lane_ref[0:1, :] = height
    lane_ref[1:2, :] = width
    lane_ref[2:3, :] = weight
    lane_ref[3:8, :] = jnp.zeros((5, lanes), F32)
    total = jnp.sum(height * width * weight * (3.0 / 16.0), axis=1, keepdims=True)
    for index in range(2):
        slab_ref[48 * index : 48 * index + 48, :] = low(project[index])
    for index in range(4):
        slab_ref[96 + 16 * index : 112 + 16 * index, :] = low(matrices[index])
    slab_ref[160:224, 0:128] = low(mid_conv[0:64, :])
    slab_ref[160:224, 128:256] = low(mid_conv[64:128, :])
    slab_ref[224:240, 0:128] = low(last_conv[...])
    turned_s[...] = jnp.zeros_like(turned_s)
    for index in range(2):
        turned_s[16 * index : 16 * index + 6, :] = fsq_pair[index]
    turned_s[32:33, :] = head_map[...]
    turned_s[33:35, :] = gain_pair[...]
    turned_s[48:96, 0:4] = first_conv[...].T
    upper = low(total).astype(F32)
    rest = total - upper
    middle = low(rest).astype(F32)
    for index, item in enumerate((upper, middle, rest - middle)):
        turned_s[96 + index : 97 + index, 0:1] = item
    slab_ref[224:240, 128:256] = low(turned_s[...].T)


def frame_lanes(first, clip_frames, frame_bounds, masters):
    lanes = frame_bounds.shape[0] * 16
    clips = jnp.broadcast_to(clip_frames.astype(F32)[:, None], (clip_frames.shape[0], 128))
    bounds = jnp.repeat(frame_bounds.T.astype(F32), 16, axis=1)
    operands = list(masters)
    operands[2] = operands[2].transpose(0, 2, 1)
    operands[4] = operands[4].T
    operands[6] = operands[6].T
    operands[7] = operands[7][None, :]
    return pl.pallas_call(
        frame_kernel,
        in_specs=[pl.BlockSpec(memory_space=pltpu.SMEM)] + [pl.BlockSpec(memory_space=pltpu.VMEM)] * 10,
        out_specs=[pl.BlockSpec(memory_space=pltpu.VMEM)] * 2,
        out_shape=[jax.ShapeDtypeStruct((8, lanes), F32), jax.ShapeDtypeStruct((SLAB_ROWS, 256), BF16)],
        scratch_shapes=[pltpu.VMEM((128, 16), F32)],
        name="frames",
    )(first.reshape(1), clips, bounds, *operands)


def passed_along(x, axis, by):
    size = lax.axis_size(axis)
    pairs = [(i, i + by) for i in range(size) if 0 <= i + by < size]
    return lax.ppermute(x, axis, pairs)


def neighbours(rows, grp, bands):
    last = rows.shape[1] - 1
    if bands == 2:
        got = swap(lax.dynamic_index_in_dim(rows, jnp.where(grp == 0, last, 0), 1, keepdims=False), "grp", 1)
        return got, got
    return passed_along(rows[:, 0], "grp", -1), passed_along(rows[:, last], "grp", 1)


def swap(x, axis, bits):
    return lax.ppermute(x, axis, [(i, i ^ bits) for i in range(lax.axis_size(axis))])


def sum_all(x, axis):
    bits, size = 1, lax.axis_size(axis)
    while bits < size:
        x = x + swap(x, axis, bits)
        bits *= 2
    return x


def gather_slabs(slab, beside):
    gathered = slab[None]
    for bits, item in zip((8, 4, 2), beside):
        got = swap(gathered, "dp", bits)
        if item is not None:
            got, _ = lax.optimization_barrier((got, item))
        gathered = jnp.concatenate([gathered, got], axis=0)
    return gathered, swap(gathered, "dp", 1)


def scalar_places(shape):
    row = lax.broadcasted_iota(jnp.int32, shape, 1)
    lane = lax.broadcasted_iota(jnp.int32, shape, 2)
    return row, (row >= 80) & (row < 83) & (lane >= 128)


def going(summed, scalars):
    if scalars:
        row, held = scalar_places(summed.shape)
        upper = lax.reduce_precision(summed, 8, 7)
        middle = lax.reduce_precision(summed - upper, 8, 7)
        parts = jnp.where(row == 81, summed - upper, jnp.where(row == 82, (summed - upper) - middle, summed))
        summed = jnp.where(held, parts, summed)
    return low(summed)


def coming(got, scalars):
    got = got.astype(F32)
    if scalars:
        _, held = scalar_places(got.shape)
        whole = (got[:, 80:81] + got[:, 81:82]) + got[:, 82:83]
        got = jnp.where(held, jnp.broadcast_to(whole, got.shape), got)
    return got


def split(summed):
    half = summed.shape[0] // 2
    return summed[:half], summed[half:]


def reduce_both(auto_keep, auto_got, judge_send, judge_keep):
    judge_got = swap(judge_send, "dp", 1)
    auto_got, judge_got = lax.optimization_barrier((auto_got, judge_got))
    auto_keep, auto_send = split(auto_keep + coming(auto_got, False))
    judge_keep, judge_send = split(judge_keep + judge_got)
    auto_got = swap(going(auto_send, False), "dp", 4)
    judge_got = swap(going(judge_send, True), "dp", 2)
    auto_got, judge_got = lax.optimization_barrier((auto_got, judge_got))
    auto_keep, auto_send = split(auto_keep + coming(auto_got, False))
    judge_keep, judge_send = split(judge_keep + coming(judge_got, True))
    auto_got = swap(auto_send, "dp", 8)
    judge_got = swap(going(judge_send, True), "dp", 4)
    auto_got, judge_got = lax.optimization_barrier((auto_got, judge_got))
    auto_keep = auto_keep + auto_got
    judge_keep, judge_send = split(judge_keep + coming(judge_got, True))
    auto_got = swap(auto_keep, "grp", 1)
    judge_got = swap(judge_send, "dp", 8)
    auto_got, judge_got = lax.optimization_barrier((auto_got, judge_got))
    judge_keep = judge_keep + judge_got
    judge_got = swap(judge_keep, "grp", 1)
    return auto_keep[0] + auto_got[0], judge_keep[0] + judge_got[0]


def unpack_auto(total):
    project = total[:96].reshape(2, 48, 256)
    matrices = total[96:160].reshape(4, 16, 256)
    fsq_pair = jnp.stack([total[160:176, 0:6], total[160:176, 128:134]])
    gain_pair = jnp.stack([jnp.sum(total[176:192, 0:128], axis=1), jnp.sum(total[176:192, 128:256], axis=1)])
    return project, matrices, fsq_pair, gain_pair


def unpack_judge_grads(total):
    mid = jnp.concatenate([total[:64, :128], total[:64, 128:]], axis=0)
    head = jnp.sum(total[64:80, 0:128], axis=1)
    last = total[64:80, 128:256].T
    first = total[80:84, 0:48].T
    return first, mid, last, head


def whole_slabs(first, clip_frames, frame_bounds, masters):
    gathered = [lax.all_gather(item, "dp", axis=axis, tiled=True) for item, axis in zip(masters, AXES)]

    def share(array, axis, number):
        size = array.shape[axis] // SLABS
        return lax.slice_in_dim(array, number * size, number * size + size, axis=axis)

    slabs = []
    for number in range(SLABS):
        shares = [share(item, axis, number) for item, axis in zip(gathered, AXES)]
        lane_info, slab = frame_lanes(first, clip_frames, frame_bounds, shares)
        slabs.append(slab)
    held = slabs[0][224, 224:227].astype(F32)
    total = lax.psum(held[0] + held[1] + held[2], "dp")
    upper = low(total)
    middle = low(total - upper.astype(F32))
    lower = low(total - upper.astype(F32) - middle.astype(F32))
    parts = jnp.stack([upper, middle, lower])
    slabs = [slab.at[224, 224:227].set(parts if number == 0 else 0) for number, slab in enumerate(slabs)]
    return lane_info, tuple(jnp.stack([slabs[value ^ core] for value in VALUES]) for core in range(2))


def whole_grads(auto, judge):
    def ordered(send, keep):
        pieces = [None] * SLABS
        for place, value in enumerate(VALUES):
            pieces[value] = keep[place]
            pieces[value ^ 1] = send[place].astype(F32)
        return pieces

    shares = [
        unpack_auto(left) + unpack_judge_grads(right) for left, right in zip(ordered(*auto), ordered(*judge))
    ]
    totals = []
    for index, axis in enumerate(AXES):
        whole = jnp.concatenate([share[index] for share in shares], axis=axis)
        totals.append(lax.psum_scatter(whole, "dp", scatter_dimension=axis, tiled=True))
    scalars = judge[1][0, 80, 128:131]
    totals.append(lax.psum(scalars, "dp"))
    return lax.psum(tuple(totals), "grp")


def adamw(master, moment, square, grad, rate, decay):
    new_moment = BETA_ONE * moment + (1.0 - BETA_ONE) * grad
    new_square = BETA_TWO * square + (1.0 - BETA_TWO) * grad * grad
    update = (
        new_moment
        / (1.0 - BETA_ONE**STEP)
        / (jnp.sqrt(new_square / (1.0 - BETA_TWO**STEP)) + ADAM_EPS)
    )
    return (new_moment, new_square, master - rate * (update + decay * master))


def constants():
    products = np.cumprod((1,) + LEVELS)[:6]
    rows = np.zeros((5, 16), np.float32)
    rows[1] = 1.0
    rows[2] = 1.0
    rows[0, :6] = 1.0 / products
    rows[1, :6] = LEVELS
    rows[2, :6] = 1.0 / np.array(LEVELS)
    rows[3, :6] = HALVES
    rows[4, :6] = 1.0 / np.array(HALVES)
    consts = np.broadcast_to(rows.reshape(80, 1), (80, 128)).astype(np.float32)
    places = np.arange(768)
    down = places // 48 // 4 * 4 + places % 48 // 12
    across = places // 48 % 4 * 4 + places % 48 % 12 // 3
    spots = np.broadcast_to(np.stack([down, across])[:, :, None], (2, 768, 128)).astype(np.float32)
    return jnp.asarray(consts), jnp.asarray(spots)


def on_device(pixels, frame_bounds, clip_frames, codes, *states):
    masters, moments, squares = states[:8], states[8:16], states[16:24]
    frames, band = pixels.shape[:2]
    grp, bands = lax.axis_index("grp"), lax.axis_size("grp")
    me, parts = lax.axis_index("dp"), lax.axis_size("dp")
    shared = parts == SLABS
    positions = frames * 16
    count_all = float(frames * parts * 256)

    code_halos = neighbours(codes, grp, bands)
    code_rows = codes.transpose(1, 0, 2).reshape(band, positions).astype(F32)
    counts = count_codes(code_rows)
    halos = neighbours(pixels, grp, bands)
    if shared:
        lane_info, slab = frame_lanes(me * frames, clip_frames, frame_bounds, masters)
        slabs = gather_slabs(slab, (counts, None, code_halos))
    else:
        lane_info, slabs = whole_slabs(me * frames, clip_frames, frame_bounds, masters)
    counts = lax.psum(counts, ("dp", "grp"))

    places = jnp.stack(
        [grp * band, (grp < bands - 1).astype(jnp.int32), (grp > 0).astype(jnp.int32), me if shared else jnp.int32(0)]
    ).astype(jnp.int32)
    above, under = (item.reshape(1, positions).astype(F32) for item in (code_halos[1], code_halos[0]))
    all_codes = jnp.concatenate([above, code_rows, under], axis=0)
    extra = (all_codes, lane_info, *constants())

    fake_outs = run_fake(pixels, places, slabs, extra, count_all)
    halos, counts, fake_outs = lax.optimization_barrier((halos, counts, fake_outs))
    auto, starts = fake_outs[:2], fake_outs[2:7]
    if shared:
        auto_send, auto_keep = auto
        auto_keep, auto_send = split(auto_keep + swap(auto_send, "dp", 1))
        got = swap(going(auto_send, False), "dp", 2)
    judge = run_real(pixels, halos, places, slabs, starts, count_all)
    if shared:
        got, judge = lax.optimization_barrier((got, judge))
        auto_total, judge_total = reduce_both(auto_keep, got, *judge)
        totals = (*unpack_auto(auto_total), *unpack_judge_grads(judge_total))
        losses = judge_total[80, 128:131]
    else:
        *totals, losses = whole_grads(auto, judge)

    shares = counts * (1.0 / count_all)
    perplexity = jnp.exp(-jnp.sum(jax.scipy.special.xlogy(shares, shares)))
    results = [
        adamw(
            masters[number],
            moments[number],
            squares[number],
            totals[number],
            RATE_GAIN if number == 3 else RATE_MATRIX,
            0.0 if number == 3 else DECAY,
        )
        for number in range(8)
    ]
    return (
        *(result[0] for result in results),
        *(result[1] for result in results),
        *(result[2] for result in results),
        jnp.stack([losses[0], fake_outs[6][3, 0]]),
        losses[1:3],
        perplexity,
    )


def solution(mesh):
    states = (
        P(None, "dp", None),
        P(None, "dp", None),
        P(None, "dp", None),
        P(None, "dp"),
        P(None, "dp"),
        P("dp", None),
        P(None, "dp"),
        P("dp"),
    )
    return jax.shard_map(
        on_device,
        mesh=mesh,
        in_specs=(P("dp", "grp", None, None), P("dp", None), P(), P("dp", "grp", None)) + states * 3,
        out_specs=states * 3 + (P(), P(), P()),
        check_vma=False,
    )
```

```python
import jax
import jax.numpy as jnp
import numpy as np
from jax import lax
from jax.experimental import pallas as pl
from jax.experimental.pallas import tpu as pltpu
from jax.sharding import PartitionSpec as P

STEP = 10
EPS_NORM = 1e-06
BETA_ONE = 0.9
BETA_TWO = 0.95
ADAM_EPS = 1e-08
DECAY = 0.1
RATE_MATRIX = 0.04
RATE_GAIN = 0.25
GEN_WEIGHT = 0.02
HALVES = (3.5, 3.5, 3.5, 2.0, 2.0, 2.0)
LEVELS = (8, 8, 8, 5, 5, 5)

F32 = jnp.float32
BF16 = jnp.bfloat16
VMEM_LIMIT = 60 * 2**20
FAKE_LANES = 512
REAL_LANES = 1024
REAL_PART = 256
SLABS = 16
VALUES = (0, 8, 4, 12, 2, 10, 6, 14)
WINDOWS = (0, 128, 384, 512)
AUTO_ROWS = 160
SLAB_ROWS = 240
AXES = (1, 1, 1, 1, 1, 0, 1, 0)
HIGHEST = lax.Precision.HIGHEST


def nn(left, right):
    return jnp.dot(left, right, preferred_element_type=F32)


def nt(left, right):
    return lax.dot_general(left, right, (((1,), (1,)), ((), ())), preferred_element_type=F32)


def low(value):
    return value.astype(BF16)


def wide(columns, lanes):
    return jnp.concatenate([columns] * (lanes // 128), axis=1)


def fold(value):
    total = value[:, :128]
    for start in range(128, value.shape[1], 128):
        total = total + value[:, start : start + 128]
    return total


def silu_parts(half):
    turned = jnp.tanh(half)
    upper = 1.0 + turned
    acted = half * upper
    return acted, upper + acted * (1.0 - turned)


def norm_parts(stream):
    scaling = lax.rsqrt(jnp.mean(stream * stream, axis=0, keepdims=True) + EPS_NORM)
    return scaling, stream * scaling


def softplus(value):
    return jnp.maximum(value, 0.0) + jnp.log1p(jnp.exp(-jnp.abs(value)))


def cost(flops, moved):
    return pl.CostEstimate(flops=int(flops), bytes_accessed=int(moved), transcendentals=0)


def aligned(index, size):
    return pl.ds(pl.multiple_of(index * size, size), size)


def interleave(*streams):
    places = []
    for index, (stream, count, *span) in enumerate(streams):
        start, stop = span or (0.0, 1.0)
        places += [(start + (stop - start) * (piece + 0.5) / count, index) for piece in range(count)]
    for _, index in sorted(places):
        next(streams[index][0], None)
    for stream, *_ in streams:
        for _ in stream:
            pass


def slab_owners(me, slabs):
    for core, array in enumerate(slabs):
        for place, value in enumerate(VALUES):
            yield me ^ value ^ core, array.at[place]


def unpack_judge(me, slabs, pair_s, misc_s, first_row):
    for owner, slab in slab_owners(me, slabs):
        rows = pl.ds(pl.multiple_of(lax.rem(owner, 8) * 128, 128), 64)
        more = pl.ds(pl.multiple_of(lax.rem(owner, 8) * 128 + 64, 64), 64)
        side = owner // 8
        pair_s[side, rows, :] = slab[first_row : first_row + 64, 0:128]
        pair_s[side, more, :] = slab[first_row : first_row + 64, 128:256]
        misc_s[aligned(owner, 16), :] = slab[first_row + 64 : first_row + 80, :]


def slab_targets(me):
    for core in range(2):
        for place, value in enumerate(VALUES):
            yield me ^ value ^ core, core, place


def prepare_judge(pair_s, misc_s, judge):
    wmt_s, wmh_s, wlt_s, wlh_s, headw_s, headr_s, bdt_s, bd_s, windows_s = judge
    half = jnp.asarray(0.5, BF16)
    for side in range(2):
        columns = pl.ds(side * 128, 128)
        for part in range(4):
            rows = pl.ds(part * 256, 256)
            block = pair_s[side, rows, :] * half
            wmh_s[rows, columns] = block
            wmt_s[columns, rows] = block.T
    last_t = misc_s[:, 0:128]
    wlt_s[...] = last_t * half
    wlh_s[...] = last_t.T * half
    turned = misc_s[:, 128:256].T
    headr_s[...] = turned[32:48, :]
    headw_s[...] = jnp.broadcast_to(misc_s[:, 128:256].astype(F32)[:, 32:33] * 0.5, headw_s.shape)
    row = lax.broadcasted_iota(jnp.int32, (256, 256), 0) % 64
    column = lax.broadcasted_iota(jnp.int32, (256, 256), 1)
    pick = low(jnp.where(column == row // 4 * 16 + row % 4, 1.0, 0.0))
    picked = low(nn(pick, misc_s[...]))
    lane = lax.broadcasted_iota(jnp.int32, (256, 192), 0)
    place = lax.broadcasted_iota(jnp.int32, (256, 192), 1)
    spread = low(jnp.where(lane == 176 + place % 48, 1.0, 0.0))
    diagonal = (lane // 64) == (place // 48)
    band_t = jnp.where(diagonal, nn(picked, spread), 0.0)
    if bdt_s is not None:
        bdt_s[...] = low(band_t * 0.5)
        bd_s[...] = low(band_t).T
    if windows_s is not None:
        windows_s[...] = jnp.zeros_like(windows_s)
        windows_s[0, :, 0:192] = low(band_t * 0.5)
        lane = lax.broadcasted_iota(jnp.int32, (256, 256), 0)
        place = lax.broadcasted_iota(jnp.int32, (256, 256), 1)
        spread = low(jnp.where((lane == 176 + (place + 32) % 48) & (place >= 64), 1.0, 0.0))
        diagonal = (lane // 64) == (place - 64) // 48
        windows_s[1] = low(jnp.where(diagonal & (place >= 64), nn(picked, spread), 0.0) * 0.5)


def judge_scratch(fake):
    shapes = [((256, 1024), BF16), ((1024, 256), BF16), ((256, 128), BF16), ((128, 256), BF16)]
    shapes += [((256, 128), F32), ((16, 256), BF16)]
    if fake:
        shapes += [((256, 192), BF16), ((192, 256), BF16)]
    else:
        shapes += [((2, 256, 256), BF16)]
    return shapes


def judge_middle(part, act, q_s, judge, count_all, active, counted, kind, held, ghead_ref, loss_ref, new_g2):
    wmt_s, _, wlt_s, wlh_s, headw_s, headr_s = judge[:6]
    two_s, three_s = held
    fresh = nn(wmt_s[...], act[:, part])
    yield
    acted_two, slope_two = silu_parts(fresh[:128] + q_s[:, part])
    q_s[:, part] = fresh[128:]
    acted_two = low(acted_two)
    two_s[:, part] = acted_two * counted.astype(BF16)
    yield
    acted_three, slope_three = silu_parts(nn(wlt_s[...], acted_two))
    acted_three = low(acted_three)
    yield
    score = nn(headr_s[...], acted_three)[:1]
    shaped = wide(headw_s[...], score.shape[1]) * slope_three
    yield
    if kind == "real":
        grad_score = -jax.nn.sigmoid(1.0 - score) * (active / count_all)
        grad_three = low(grad_score * shaped)
        three_s[:, part] = grad_three
        loss_ref[0:1, part] += softplus(1.0 - score) * counted
        yield
        new_g2[0][:, part] = low(nn(wlh_s[...], grad_three) * slope_two)
    else:
        pull = jax.nn.sigmoid(1.0 + score)
        grad_score = pull * (active / count_all)
        three_s[:, part] = low(grad_score * shaped)
        grad_three_gen = low((-GEN_WEIGHT / count_all * active) * shaped)
        loss_ref[0:1, part] += softplus(1.0 + score) * counted
        loss_ref[1:2, part] -= score * counted
        yield
        grad_two_gen = nn(wlh_s[...], grad_three_gen) * slope_two
        new_g2[0][:, part] = low(grad_two_gen * (pull * (-1.0 / GEN_WEIGHT)))
        new_g2[1][:, part] = low(grad_two_gen)
    yield
    ghead_ref[...] += fold(acted_three.astype(F32) * (grad_score * counted))
    yield


def real_kernel(band, lanes, chunks, count_all):
    rows_n = band + 1
    total = chunks * rows_n

    def kernel(*refs):
        refs = list(refs)

        def take(number):
            taken = refs[:number]
            del refs[:number]
            return taken

        (places,) = take(1)
        slabs = take(2)
        xf, xe, xbelow, xabove = take(4)
        start_refs = take(4)
        (fake_loss,) = take(1)
        send_ref, keep_ref = take(2)
        judge = take(6) + [None, None] + take(1)
        pair_s, misc_s = take(2)
        gwm_ref, gwl_ref, gw1_ref, gwin_ref, ghead_ref = take(5)
        q_s, g2, g2_new, act_s, slope_s, small = take(6)
        first_s, lastt_s, loss_ref = take(3)
        held = take(2)
        wmt_s, wmh_s, windows_s = judge[0], judge[1], judge[8]
        stage = pl.program_id(0)
        has_below, has_above, me = places[1], places[2].astype(F32), places[3]
        step = lax.rem(stage, rows_n)
        row = band - 1 - step
        slot = lax.rem(stage, 2)
        back_ok = (stage >= 2) & (lax.rem(stage - 2, rows_n) != band)
        front_ok = stage < total
        act, slope = act_s.at[slot], slope_s.at[slot]
        halo = row < 0
        active = jnp.where(halo, has_above, 1.0)
        counted = jnp.where(halo, 0.0, 1.0)

        @pl.when(stage == 0)
        def prepare():
            unpack_judge(me, slabs, pair_s, misc_s, 0)
            prepare_judge(pair_s, misc_s, judge)
            for ref, start in zip((gwm_ref, gwl_ref, gw1_ref, ghead_ref), start_refs):
                ref[...] = start[...]
            loss_ref[...] = jnp.zeros_like(loss_ref)
            gwin_ref[...] = jnp.zeros_like(gwin_ref)

        @pl.when(front_ok & (step == 0) & (has_below > 0))
        def below():
            joined = jnp.zeros((128, lanes), F32)
            for group in range(4):
                x = xbelow[:, :, WINDOWS[group] : WINDOWS[group] + 256].reshape(lanes, 256)
                acted, _ = silu_parts(nt(windows_s[group % 2], x))
                joined = joined + nn(wmt_s[128:256, 256 * group : 256 * group + 256], low(acted))
            q_s[...] = joined

        @pl.when(front_ok & (step == 0) & (has_below == 0))
        def edge():
            q_s[...] = jnp.zeros_like(q_s)

        def back_small():
            for group in range(4):
                rows = slice(256 * group, 256 * group + 256)
                for start in range(0, lanes, 256):
                    part = slice(start, start + 256)
                    small[rows, part] = low(nn(wmh_s[rows, :], g2[:, part]) * slope[rows, part])
                    yield

        def back_middle():
            for group in range(4):
                rows = slice(256 * group, 256 * group + 256)
                gwm_ref[rows, :] += nt(act[rows, :], g2[...])
                yield

        def back_first():
            for group in range(4):
                x = xe[:, 0, :, WINDOWS[group] : WINDOWS[group] + 256].reshape(lanes, 256)
                gwin_ref[group % 2] += nn(small[256 * group : 256 * group + 256, :], x)
                yield

        def front_first():
            for group in range(4):
                for start in range(0, lanes, 256):
                    part = slice(start, start + 256)
                    some, window = slice(start // 16, start // 16 + 16), slice(WINDOWS[group], WINDOWS[group] + 256)
                    x = jnp.where(halo, xabove[some, :, window], xf[some, 0, :, window]).reshape(256, 256)
                    acted, slope_new = silu_parts(nt(windows_s[group % 2], x))
                    act[256 * group : 256 * group + 256, part] = low(acted)
                    slope[256 * group : 256 * group + 256, part] = slope_new
                    yield

        def front_middle(part):
            return judge_middle(
                part, act, q_s, judge, count_all, active, counted, "real", held, ghead_ref, loss_ref, (g2_new,)
            )

        def front_last():
            gwl_ref[...] += nt(held[0][...], held[1][...])
            yield

        def shift():
            g2[0:128, :] = g2[128:256, :]
            g2[128:256, :] = g2_new[...]

        parts = [slice(start, start + REAL_PART) for start in range(0, lanes, REAL_PART)]

        @pl.when(front_ok & back_ok)
        def both():
            interleave(
                (back_small(), lanes // 64, 0.0, 0.8),
                (back_middle(), 4, 0.0, 0.8),
                (front_first(), lanes // 64, 0.2, 1.0),
            )
            interleave(*((front_middle(part), 7) for part in parts), (back_first(), 4))
            interleave((front_last(), 1))
            shift()

        @pl.when(front_ok & jnp.logical_not(back_ok))
        def front_only():
            interleave((front_first(), 1))
            interleave(*((front_middle(part), 7) for part in parts))
            interleave((front_last(), 1))
            shift()

        @pl.when(jnp.logical_not(front_ok) & back_ok)
        def back_only():
            interleave((back_small(), 1))
            interleave((back_first(), 4), (back_middle(), 4))

        @pl.when(stage == total)
        def write():
            turned = gw1_ref[...].T
            lane = lax.broadcasted_iota(jnp.int32, (64, 192), 1)
            summed = jnp.zeros((64, 192), F32)
            for block in range(4):
                summed = summed + jnp.where(lane // 48 == block, turned[64 * block : 64 * block + 64, :], 0.0)
            place = lax.broadcasted_iota(jnp.int32, (192, 128), 0) % 48
            folding = jnp.where(place == lax.broadcasted_iota(jnp.int32, (192, 128), 1), 1.0, 0.0)
            first = jnp.dot(summed, folding, precision=HIGHEST, preferred_element_type=F32)
            lane = lax.broadcasted_iota(jnp.int32, (64, 256), 1)
            place = lax.broadcasted_iota(jnp.int32, (256, 128), 0)
            for odd in range(2):
                summed = jnp.zeros((64, 256), F32)
                for block in range(4):
                    start = 64 * odd + 48 * block
                    inside = (lane >= start) & (lane < start + 48)
                    summed = summed + jnp.where(inside, gwin_ref[odd, 64 * block : 64 * block + 64, :], 0.0)
                folding = jnp.where((place + 32 * odd) % 48 == lax.broadcasted_iota(jnp.int32, (256, 128), 1), 1.0, 0.0)
                first = first + jnp.dot(summed, folding, precision=HIGHEST, preferred_element_type=F32)
            for owner in range(SLABS):
                first_s[16 * owner : 16 * owner + 16, :] = jnp.zeros((16, 128), F32)
                first_s[16 * owner : 16 * owner + 4, :] = first[4 * owner : 4 * owner + 4, :]
            lastt_s[...] = gwl_ref[...].T
            scalars = jnp.zeros((1, 128), F32)
            sums = (jnp.sum(fake_loss[2:3, :]), jnp.sum(fake_loss[1:2, :]), jnp.sum(fake_loss[0:1, :]) + jnp.sum(loss_ref[0:1, :]))
            for number, item in enumerate(sums):
                scalars = jnp.where(lax.broadcasted_iota(jnp.int32, (1, 128), 1) == number, item, scalars)
            for owner, core, chip in slab_targets(me):
                side, rows = owner // 8, lax.rem(owner, 8) * 128
                upper = pl.ds(pl.multiple_of(rows, 64), 64)
                lower = pl.ds(pl.multiple_of(rows + 64, 64), 64)
                own = aligned(owner, 16)
                left = jnp.where(side == 0, gwm_ref[upper, 0:128], gwm_ref[upper, 128:256])
                right = jnp.where(side == 0, gwm_ref[lower, 0:128], gwm_ref[lower, 128:256])
                target = (keep_ref, send_ref)[core]
                target[chip, 0:64, 0:128] = left
                target[chip, 0:64, 128:256] = right
                target[chip, 64:80, 0:128] = ghead_ref[own, :]
                target[chip, 64:80, 128:256] = lastt_s[own, :]
                target[chip, 80:96, 0:128] = first_s[own, :]
                target[chip, 80:96, 128:256] = jnp.where(lax.broadcasted_iota(jnp.int32, (16, 128), 0) < 3, scalars, 0.0)

    return kernel


def run_real(pixels, halos, places, slabs, starts, count_all):
    frames, band = pixels.shape[:2]
    positions = frames * 16
    lanes = min(REAL_LANES, positions)
    chunks = positions // lanes
    rows_n = band + 1
    total = chunks * rows_n

    halo_spec = pl.BlockSpec((lanes // 16, 16, 768), lambda t: (jnp.minimum(t, total - 1) // rows_n, 0, 0))
    specs = [pl.BlockSpec(memory_space=pltpu.SMEM)]
    specs += [pl.BlockSpec((SLABS // 2, 80, 256), lambda t: (0, 2, 0))] * 2
    specs += stage_rows(band, lanes, chunks)
    specs += [halo_spec] * 2
    specs += [pl.BlockSpec(item.shape, lambda t: (0, 0)) for item in starts]
    outs = [
        jax.ShapeDtypeStruct((SLABS // 2, 96, 256), F32),
        jax.ShapeDtypeStruct((SLABS // 2, 96, 256), F32),
    ]
    scratch = judge_scratch(False) + [((2, 1024, 128), BF16), ((256, 256), BF16)]
    scratch += [((1024, 256), F32), ((128, 256), F32), ((192, 256), F32), ((2, 256, 256), F32), ((256, 128), F32)]
    scratch += [((128, lanes), F32), ((256, lanes), BF16), ((128, lanes), BF16)]
    scratch += [((2, 1024, lanes), BF16), ((2, 1024, lanes), F32), ((1024, lanes), BF16)]
    scratch += [((256, 128), F32), ((256, 128), F32), ((8, lanes), F32)]
    scratch += [((128, lanes), BF16), ((256, lanes), BF16)]
    return pl.pallas_call(
        real_kernel(band, lanes, chunks, count_all),
        grid=(total + 1,),
        in_specs=specs,
        out_specs=[pl.BlockSpec(item.shape, lambda t, n=len(item.shape): (0,) * n) for item in outs],
        out_shape=outs,
        scratch_shapes=[pltpu.VMEM(*item) for item in scratch],
        compiler_params=pltpu.CompilerParams(vmem_limit_bytes=VMEM_LIMIT),
        cost_estimate=cost(5.4e6 * band * positions, 3072 * band * positions),
        name="judge_real",
    )(places, *slabs, pixels, pixels, *halos, *starts)


def block_steps(stream, gain, first_half_t, second_t):
    scaling, normal = norm_parts(stream)
    normed = low(normal * gain)
    yield None
    acted, slope = silu_parts(nn(first_half_t[...], normed))
    acted = low(acted)
    yield None
    yield stream + nn(second_t[...], acted), (scaling, normal, normed, acted, slope)


def fake_kernel(band, lanes, chunks, count_all):
    rows_n = band + 1
    total = chunks * rows_n
    halves = [slice(start, start + 256) for start in range(0, lanes, 256)]

    def kernel(*refs):
        refs = list(refs)

        def take(number):
            taken = refs[:number]
            del refs[:number]
            return taken

        (places,) = take(1)
        slabs = take(2)
        xf_ref, xe_ref, codes_ref, lane_ref, consts_ref, spots_ref = take(6)
        send_ref, keep_ref, gwm_ref, gwl_ref, gw1_ref, ghead_ref, loss_ref = take(7)
        judge = take(8) + [None]
        pair_s, misc_s = take(2)
        proj_s, projt_s, block_s, blockt_s, blockh_s, fsq_s, fsqt_s, gains_s, total_s = take(9)
        gproj_ref, gprojt_ref, gblocks_ref, gfsq_ref, gfsqt_ref, ggains_ref = take(6)
        q_s, g2_disc, g2_gen, new_disc, new_gen, small_s, smallgen_s, gradlow_s, xt_s = take(9)
        fake_s, gl1_s, act_s, slope_s = take(4)
        saved_s = take(5)
        outlow_s, values_s = take(2)
        encoded_s = take(7)
        outer_s, inner_s, start_s, latent_s, stream_s = take(5)
        held = take(2)
        wmt_s, wmh_s, bdt_s, bd_s = judge[0], judge[1], judge[6], judge[7]
        stage = pl.program_id(0)
        row_start, has_below, me = places[0], places[1], places[3]
        has_above = places[2].astype(F32)
        step = lax.rem(stage, rows_n)
        row = band - 1 - step
        slot, slot_three, back_three = lax.rem(stage, 2), lax.rem(stage, 3), lax.rem(stage + 1, 3)
        back_ok = (stage >= 2) & (lax.rem(stage - 2, rows_n) != band)
        front_ok = stage < total
        gl1, act, slope = gl1_s.at[slot], act_s.at[slot], slope_s.at[slot]
        fake, fake_back = fake_s.at[slot_three], fake_s.at[back_three]
        counted = jnp.where(row >= 0, 1.0, 0.0)
        active = jnp.where(row >= 0, 1.0, has_above)

        @pl.when(stage == 0)
        def prepare():
            unpack_judge(me, slabs, pair_s, misc_s, AUTO_ROWS)
            prepare_judge(pair_s, misc_s, judge)
            for owner, slab in slab_owners(me, slabs):
                rows, some = aligned(owner, 48), aligned(owner, 16)
                proj_s[0, rows, :] = slab[0:48, :]
                proj_s[1, rows, :] = slab[48:96, :]
                for index in range(4):
                    block_s[index, some, :] = slab[96 + 16 * index : 112 + 16 * index, :]
            projt_s[0] = proj_s[0].T
            projt_s[1] = proj_s[1].T
            for index in range(4):
                scale = jnp.asarray(0.5 if index % 2 == 0 else 1.0, BF16)
                blockt_s[index] = (block_s[index] * scale).T
                if index % 2 == 1:
                    blockh_s[index // 2] = block_s[index] * jnp.asarray(0.5, BF16)
            tail = misc_s[:, 128:256]
            turned = tail.T
            fsqt_s[0] = turned[0:16, :]
            fsqt_s[1] = turned[16:32, :]
            for index in range(2):
                fsq_s[index] = fsqt_s[index].T
                gains_s[index] = jnp.broadcast_to(tail.astype(F32)[:, 33 + index : 34 + index], (256, 128))
            lane = lax.broadcasted_iota(jnp.int32, (256, 128), 1)
            held = (lane >= 96) & (lane < 99)
            total_s[...] = jnp.broadcast_to(jnp.sum(jnp.where(held, tail.astype(F32), 0.0)), (8, 128))
            for ref in (gwm_ref, gwl_ref, gw1_ref, ghead_ref, loss_ref, gproj_ref, gprojt_ref, gblocks_ref, gfsqt_ref, ggains_ref):
                ref[...] = jnp.zeros_like(ref)

        def latent_values(row):
            consts = consts_ref[...]
            code = codes_ref[pl.ds(row + 1, 1), :]
            turn = jnp.floor((code + 0.5) * wide(consts[0:16], lanes))
            level = wide(consts[16:32], lanes)
            digit = turn - level * jnp.floor((turn + 0.5) * wide(consts[32:48], lanes))
            return low((digit - wide(consts[48:64], lanes)) * wide(consts[64:80], lanes))

        @pl.when(front_ok & (step == 0) & (has_below > 0))
        def below():
            values = latent_values(jnp.int32(band))
            outputs = list(block_steps(nn(fsq_s[1], values), wide(gains_s[1], lanes), blockt_s.at[2], blockt_s.at[3]))
            outlow = low(outputs[-1][0])
            joined = jnp.zeros((128, lanes), F32)
            for group in range(4):
                recon = low(nn(proj_s[1, pl.ds(group * 192, 192), :], outlow))
                acted, _ = silu_parts(nn(bdt_s[...], recon))
                joined = joined + nn(wmt_s[128:256, 256 * group : 256 * group + 256], low(acted))
            q_s[...] = joined

        @pl.when(front_ok & (step == 0) & (has_below == 0))
        def edge():
            q_s[...] = jnp.zeros_like(q_s)

        def front_block(part):
            values = values_s[slot_three, :, part]
            width = values.shape[1]
            stream = nn(fsq_s[1], values)
            yield
            result = None
            for result in block_steps(stream, wide(gains_s[1], width), blockt_s.at[2], blockt_s.at[3]):
                yield
            output, saved = result
            outlow_s[slot_three, :, part] = low(output)
            for ref, item in zip(saved_s, saved):
                ref[slot_three, :, part] = item
            yield

        def front_turn():
            for part in halves:
                some = slice(part.start // 16, part.stop // 16)
                for column in range(0, 768, 256):
                    xt_s[column : column + 256, part] = xf_ref[some, 0, :, column : column + 256].reshape(256, 256).T
                    yield

        def front_recon():
            lane = lax.broadcasted_iota(jnp.int32, (1, lanes), 1)
            column = (lane % 16).astype(F32)
            place = (row_start + row).astype(F32)
            high = lane_ref[0:1, :] - 16.0 * place
            broad = lane_ref[1:2, :] - 16.0 * column
            weight = lane_ref[2:3, :] * counted
            weight_share = weight / wide(total_s[0:1, :], lanes)
            sums = [jnp.zeros((1, 256), F32) for _ in halves]
            for group in range(4):
                rows = slice(group * 192, group * 192 + 192)
                for index, part in enumerate(halves):
                    recon = nn(proj_s[1, rows, :], outlow_s[slot_three, :, part])
                    fake[rows, part] = low(recon)
                    diff = recon - xt_s[rows, part].astype(F32)
                    square = diff * diff + 1.0
                    inside = (wide(spots_ref[0, rows, :], 256) < high[:, part]) & (
                        wide(spots_ref[1, rows, :], 256) < broad[:, part]
                    )
                    share = lax.rsqrt(square) * jnp.where(inside, weight_share[:, part], 0.0)
                    gl1[rows, part] = diff * share
                    sums[index] = sums[index] + jnp.sum(square * share, axis=0, keepdims=True)
                    yield
            loss_ref[2:3, :] += jnp.concatenate(sums, axis=1) * wide(total_s[0:1, :], lanes)

        def front_first():
            for group in range(4):
                for part in halves:
                    acted, slope_new = silu_parts(nn(bdt_s[...], fake[192 * group : 192 * group + 192, part]))
                    act[256 * group : 256 * group + 256, part] = low(acted)
                    slope[256 * group : 256 * group + 256, part] = slope_new
                    yield

        def front_middle(part):
            return judge_middle(
                part, act, q_s, judge, count_all, active, counted, "fake", held, ghead_ref, loss_ref, (new_disc, new_gen)
            )

        def front_last():
            gwl_ref[...] += nt(held[0][...], held[1][...])
            yield

        def back_gen():
            for group in range(4):
                rows = slice(256 * group, 256 * group + 256)
                for part in halves:
                    smallgen_s[rows, part] = low(nn(wmh_s[rows, :], g2_gen[:, part]) * slope[rows, part])
                    yield

        def back_disc():
            for group in range(4):
                rows = slice(256 * group, 256 * group + 256)
                for part in halves:
                    small_s[rows, part] = low(nn(wmh_s[rows, :], g2_disc[:, part]) * slope[rows, part])
                    yield

        def back_recon():
            for group in range(4):
                rows = slice(group * 192, group * 192 + 192)
                gradlow_s[rows, :] = low(gl1[rows, :] + nn(bd_s[...], smallgen_s[256 * group : 256 * group + 256, :]))
                yield

        def back_first():
            for group in range(4):
                rows = slice(group * 192, group * 192 + 192)
                gw1_ref[...] += nt(fake_back[rows, :], small_s[256 * group : 256 * group + 256, :])
                yield

        def back_middle():
            for group in range(2):
                rows = slice(512 * group, 512 * group + 512)
                gwm_ref[rows, :] += nt(act[rows, :], g2_disc[...])
                yield

        def back_project():
            for group in range(2):
                rows = slice(group * 384, group * 384 + 384)
                gproj_ref[1, rows, :] += nt(gradlow_s[rows, :], outlow_s[back_three])
                yield

        def back_encode(part):
            some = slice(part.start // 16, part.stop // 16)
            stream = nt(projt_s[0], xe_ref[some].reshape(part.stop - part.start, 768))
            yield
            result = None
            for result in block_steps(
                stream, wide(gains_s[0], part.stop - part.start), blockt_s.at[0], blockt_s.at[1]
            ):
                yield
            middle, saved = result
            middle_low = low(middle)
            for ref, item in zip(encoded_s, (*saved, middle_low, nn(fsqt_s[0], middle_low))):
                ref[:, part] = item
            yield

        def back_block(grad_out, saved, index, part):
            scaling, normal, slope_in = saved
            gain = wide(gains_s[index], part.stop - part.start)
            outer = low(grad_out)
            outer_s[index, :, part] = outer
            grad_acted = nn(blockh_s[index], outer)
            yield None
            inner = low(grad_acted * slope_in)
            inner_s[index, :, part] = inner
            grad_normed = nn(block_s[2 * index], inner)
            yield None
            along = grad_normed * normal
            ggains_ref[index] += fold(along)
            mean = jnp.mean(along * gain, axis=0, keepdims=True)
            yield grad_out + scaling * (grad_normed * gain - normal * mean)

        def back_chain(part):
            grad_out = nn(projt_s[1], gradlow_s[:, part])
            yield
            saved = tuple(saved_s[n][back_three, :, part] for n in (0, 1, 4))
            grad_start = None
            for grad_start in back_block(grad_out, saved, 1, part):
                yield
            start_low = low(grad_start)
            start_s[:, part] = start_low
            grad_values = nn(fsqt_s[1], start_low)
            yield
            tangent = jnp.tanh(encoded_s[6][:, part])
            grad_latent = low(grad_values * (1.0 - tangent * tangent))
            latent_s[:, part] = grad_latent
            grad_middle = nn(fsq_s[0], grad_latent)
            yield
            saved = tuple(encoded_s[n][:, part] for n in (0, 1, 4))
            grad_stream = None
            for grad_stream in back_block(grad_middle, saved, 0, part):
                yield
            stream_s[:, part] = low(grad_stream)
            yield

        def back_fill():
            first, project, weights = back_first(), back_project(), back_weights()
            for piece in (first, project, first, weights, first, weights, project, first, weights, weights, weights):
                next(piece)
                yield

        def back_stream():
            gprojt_ref[...] += nn(stream_s[...], xe_ref[...].reshape(lanes, 768))
            yield

        def back_weights():
            gblocks_ref[3] += nt(saved_s[3][back_three], outer_s[1])
            yield
            gblocks_ref[2] += nt(saved_s[2][back_three], inner_s[1])
            yield
            gfsqt_ref[1] += nt(values_s[back_three], start_s[...])
            gfsqt_ref[0] += nt(latent_s[...], encoded_s[5][...])
            yield
            gblocks_ref[1] += nt(encoded_s[3][...], outer_s[0])
            yield
            gblocks_ref[0] += nt(encoded_s[2][...], inner_s[0])
            yield
        def shift():
            for ref, new in ((g2_disc, new_disc), (g2_gen, new_gen)):
                ref[0:128, :] = ref[128:256, :]
                ref[128:256, :] = new[...]

        @pl.when(front_ok & back_ok)
        def both():
            values_s[slot_three] = latent_values(row)
            interleave(
                (back_gen(), 4 * len(halves)),
                *((front_block(part), 5) for part in halves),
                *((back_encode(part), 5) for part in halves),
                (front_turn(), 6),
                (back_middle(), 2),
            )
            interleave(
                (back_recon(), 4, 0.0, 0.6),
                (back_disc(), 4 * len(halves), 0.0, 0.6),
                (front_recon(), 4 * len(halves), 0.1, 0.8),
                (front_first(), 4 * len(halves), 0.3, 1.0),
            )
            interleave(
                *((back_chain(part), 10, 0.0, 0.9 + 0.1 * number) for number, part in enumerate(halves)),
                *((front_middle(part), 7, 0.1, 1.0) for part in halves),
                (back_fill(), 11, 0.05, 1.0),
            )
            interleave((front_last(), 1), (back_stream(), 1))
            shift()

        @pl.when(front_ok & jnp.logical_not(back_ok))
        def front_only():
            values_s[slot_three] = latent_values(row)
            interleave(*((front_block(part), 5) for part in halves), (front_turn(), 6))
            interleave((front_recon(), 1))
            interleave((front_first(), 1))
            interleave(*((front_middle(part), 7) for part in halves))
            interleave((front_last(), 1))
            shift()

        @pl.when(jnp.logical_not(front_ok) & back_ok)
        def back_only():
            interleave((back_gen(), 4 * len(halves)), *((back_encode(part), 5) for part in halves))
            interleave((back_recon(), 4), (back_disc(), 4 * len(halves)))
            interleave(
                *((back_chain(part), 10) for part in halves), (back_middle(), 2), (back_first(), 4), (back_project(), 2)
            )
            interleave((back_weights(), 1), (back_stream(), 1))

        @pl.when(stage == total)
        def write():
            loss_ref[3:4, 0:128] = total_s[0:1, :]
            gproj_ref[0] = gprojt_ref[...].T
            for index in range(2):
                gfsq_ref[index] = gfsqt_ref[index].T
            for owner, core, chip in slab_targets(me):
                rows, own = aligned(owner, 48), aligned(owner, 16)
                target = (keep_ref, send_ref)[core]
                target[chip, 0:48, :] = gproj_ref[0, rows, :]
                target[chip, 48:96, :] = gproj_ref[1, rows, :]
                for index in range(4):
                    target[chip, 96 + 16 * index : 112 + 16 * index, :] = gblocks_ref[index, own, :]
                target[chip, 160:192, :] = jnp.zeros((32, 256), F32)
                target[chip, 160:176, 0:16] = gfsq_ref[0, own, :]
                target[chip, 160:176, 128:144] = gfsq_ref[1, own, :]
                target[chip, 176:192, 0:128] = ggains_ref[0, own, :]
                target[chip, 176:192, 128:256] = ggains_ref[1, own, :]

    return kernel


def stage_rows(band, lanes, chunks):
    rows_n = band + 1
    total = chunks * rows_n

    def front(t):
        t = jnp.minimum(t, total - 1)
        return (t // rows_n, jnp.maximum(band - 1 - lax.rem(t, rows_n), 0), 0, 0)

    def back(t):
        t = jnp.maximum(t - 2, 0)
        return (t // rows_n, jnp.maximum(band - 1 - lax.rem(t, rows_n), 0), 0, 0)

    block = (lanes // 16, 1, 16, 768)
    return pl.BlockSpec(block, front), pl.BlockSpec(block, back)


def run_fake(pixels, places, slabs, extra, count_all):
    frames, band = pixels.shape[:2]
    positions = frames * 16
    lanes = min(FAKE_LANES, positions)
    chunks = positions // lanes
    total = chunks * (band + 1)
    codes, lane_info, consts, spots = extra

    def whole(array):
        return pl.BlockSpec(array.shape, lambda t: (0,) * array.ndim)

    def chunk_spec(array):
        return pl.BlockSpec((array.shape[0], lanes), lambda t: (0, jnp.minimum(t, total - 1) // (band + 1)))

    specs = [pl.BlockSpec(memory_space=pltpu.SMEM)]
    specs += [whole(item) for item in slabs]
    specs += stage_rows(band, lanes, chunks)
    specs += [chunk_spec(codes), chunk_spec(lane_info), whole(consts), whole(spots)]
    outs = [
        jax.ShapeDtypeStruct((SLABS // 2, 192, 256), F32),
        jax.ShapeDtypeStruct((SLABS // 2, 192, 256), F32),
        *(jax.ShapeDtypeStruct(shape, F32) for shape in [(1024, 256), (128, 256), (192, 256), (256, 128), (8, lanes)]),
    ]
    scratch = judge_scratch(True) + [((2, 1024, 128), BF16), ((256, 256), BF16)]
    scratch += [((2, 768, 256), BF16), ((2, 256, 768), BF16), ((4, 256, 256), BF16), ((4, 256, 256), BF16)]
    scratch += [((2, 256, 256), BF16), ((2, 256, 16), BF16), ((2, 16, 256), BF16), ((2, 256, 128), F32), ((8, 128), F32)]
    scratch += [((2, 768, 256), F32), ((256, 768), F32), ((4, 256, 256), F32), ((2, 256, 16), F32), ((2, 16, 256), F32), ((2, 256, 128), F32)]
    scratch += [((128, lanes), F32)] + [((256, lanes), BF16)] * 2 + [((128, lanes), BF16)] * 2
    scratch += [((1024, lanes), BF16)] * 2 + [((768, lanes), BF16)] * 2
    scratch += [((3, 768, lanes), BF16), ((2, 768, lanes), F32), ((2, 1024, lanes), BF16), ((2, 1024, lanes), F32)]
    scratch += [((3, 1, lanes), F32), ((3, 256, lanes), F32), ((3, 256, lanes), BF16), ((3, 256, lanes), BF16)]
    scratch += [((3, 256, lanes), F32), ((3, 256, lanes), BF16), ((3, 16, lanes), BF16)]
    scratch += [((1, lanes), F32), ((256, lanes), F32), ((256, lanes), BF16), ((256, lanes), BF16)]
    scratch += [((256, lanes), F32), ((256, lanes), BF16), ((16, lanes), F32)]
    scratch += [((2, 256, lanes), BF16)] * 2 + [((256, lanes), BF16), ((16, lanes), BF16), ((256, lanes), BF16)]
    scratch += [((128, lanes), BF16), ((256, lanes), BF16)]
    return pl.pallas_call(
        fake_kernel(band, lanes, chunks, count_all),
        grid=(total + 1,),
        in_specs=specs,
        out_specs=[pl.BlockSpec(item.shape, lambda t, n=len(item.shape): (0,) * n) for item in outs],
        out_shape=outs,
        scratch_shapes=[pltpu.VMEM(*item) for item in scratch],
        compiler_params=pltpu.CompilerParams(vmem_limit_bytes=VMEM_LIMIT),
        cost_estimate=cost(1.6e7 * band * positions, 3072 * band * positions),
        name="judge_fake",
    )(places, *slabs, pixels, pixels, codes, lane_info, consts, spots)


def count_kernel(codes_ref, counts_ref):
    @pl.when(pl.program_id(0) == 0)
    def clear():
        counts_ref[...] = jnp.zeros_like(counts_ref)

    code = codes_ref[0]
    upper = jnp.floor(code * (1.0 / 256.0))
    lower = code - 256.0 * upper
    bins = lax.broadcasted_iota(jnp.int32, (256, code.shape[1]), 0).astype(F32)
    one, zero = jnp.asarray(1.0, F32), jnp.asarray(0.0, F32)
    counts_ref[...] += nt(low(jnp.where(bins == upper, one, zero)), low(jnp.where(bins == lower, one, zero)))


def count_codes(codes):
    parts, lanes = codes.shape
    return pl.pallas_call(
        count_kernel,
        grid=(parts,),
        in_specs=[pl.BlockSpec((1, 1, lanes), lambda s: (s, 0, 0))],
        out_specs=pl.BlockSpec((256, 256), lambda s: (0, 0)),
        out_shape=jax.ShapeDtypeStruct((256, 256), F32),
        cost_estimate=cost(5e5 * codes.size, 4 * codes.size),
        name="count",
    )(codes[:, None, :])


def frame_kernel(place_ref, clips_ref, bounds_ref, project, matrices, fsq_pair, gain_pair, first_conv, mid_conv, last_conv, head_map, lane_ref, slab_ref, turned_s):
    lanes = lane_ref.shape[1]
    clips = clips_ref[...].astype(F32)
    number = clips.shape[1]
    column = lax.broadcasted_iota(jnp.int32, (number, number), 1)
    row = lax.broadcasted_iota(jnp.int32, (number, number), 0)
    first = jnp.sum(jnp.where(column < row, clips, 0.0), axis=1, keepdims=True)
    size = jnp.sum(jnp.where(column == row, clips, 0.0), axis=1, keepdims=True)
    frame = (place_ref[0] + lax.broadcasted_iota(jnp.int32, (1, lanes), 1) // 16).astype(F32)
    mine = (first <= frame) & (frame < first + size)
    weight = 1.0 / jnp.sum(jnp.where(mine, size, 0.0), axis=0, keepdims=True)
    frames = bounds_ref.shape[1]
    spread = lax.broadcasted_iota(jnp.int32, (frames, lanes), 1) // 16
    spread = low(jnp.where(spread == lax.broadcasted_iota(jnp.int32, (frames, lanes), 0), 1.0, 0.0))
    extents = nn(low(bounds_ref[...].astype(F32)), spread)
    height, width = extents[0:1, :], extents[1:2, :]
    lane_ref[0:1, :] = height
    lane_ref[1:2, :] = width
    lane_ref[2:3, :] = weight
    lane_ref[3:8, :] = jnp.zeros((5, lanes), F32)
    total = jnp.sum(height * width * weight * (3.0 / 16.0), axis=1, keepdims=True)
    for index in range(2):
        slab_ref[48 * index : 48 * index + 48, :] = low(project[index])
    for index in range(4):
        slab_ref[96 + 16 * index : 112 + 16 * index, :] = low(matrices[index])
    slab_ref[160:224, 0:128] = low(mid_conv[0:64, :])
    slab_ref[160:224, 128:256] = low(mid_conv[64:128, :])
    slab_ref[224:240, 0:128] = low(last_conv[...])
    turned_s[...] = jnp.zeros_like(turned_s)
    for index in range(2):
        for digit in range(6):
            turned_s[16 * index + digit : 16 * index + digit + 1, :] = fsq_pair[digit, index : index + 1, :]
    turned_s[32:33, :] = head_map[...]
    turned_s[33:35, :] = gain_pair[...]
    turned_s[48:96, 0:4] = first_conv[...].T
    upper = low(total).astype(F32)
    rest = total - upper
    middle = low(rest).astype(F32)
    for index, item in enumerate((upper, middle, rest - middle)):
        turned_s[96 + index : 97 + index, 0:1] = item
    slab_ref[224:240, 128:256] = low(turned_s[...].T)


def frame_lanes(first, clip_frames, frame_bounds, masters):
    lanes = frame_bounds.shape[0] * 16
    clips = clip_frames.reshape(1, -1)
    bounds = frame_bounds.T
    operands = list(masters)
    operands[2] = operands[2].transpose(2, 0, 1)
    operands[4] = operands[4].T
    operands[6] = operands[6].T
    operands[7] = operands[7][None, :]
    return pl.pallas_call(
        frame_kernel,
        in_specs=[pl.BlockSpec(memory_space=pltpu.SMEM)] + [pl.BlockSpec(memory_space=pltpu.VMEM)] * 10,
        out_specs=[pl.BlockSpec(memory_space=pltpu.VMEM)] * 2,
        out_shape=[jax.ShapeDtypeStruct((8, lanes), F32), jax.ShapeDtypeStruct((SLAB_ROWS, 256), BF16)],
        scratch_shapes=[pltpu.VMEM((128, 16), F32)],
        name="frames",
    )(first.reshape(1), clips, bounds, *operands)


def passed_along(x, axis, by):
    size = lax.axis_size(axis)
    pairs = [(i, i + by) for i in range(size) if 0 <= i + by < size]
    return lax.ppermute(x, axis, pairs)


def neighbours(rows, grp, bands):
    last = rows.shape[1] - 1
    if bands == 2:
        got = swap(lax.dynamic_index_in_dim(rows, jnp.where(grp == 0, last, 0), 1, keepdims=False), "grp", 1)
        return got, got
    return passed_along(rows[:, 0], "grp", -1), passed_along(rows[:, last], "grp", 1)


def swap(x, axis, bits):
    return lax.ppermute(x, axis, [(i, i ^ bits) for i in range(lax.axis_size(axis))])


def sum_all(x, axis):
    bits, size = 1, lax.axis_size(axis)
    while bits < size:
        x = x + swap(x, axis, bits)
        bits *= 2
    return x


def gather_slabs(slab, beside):
    gathered = slab[None]
    for bits, item in zip((8, 4, 2), beside):
        got = swap(gathered, "dp", bits)
        if item is not None:
            got, _ = lax.optimization_barrier((got, item))
        gathered = jnp.concatenate([gathered, got], axis=0)
    return gathered, swap(gathered, "dp", 1)


def scalar_places(shape):
    row = lax.broadcasted_iota(jnp.int32, shape, 1)
    lane = lax.broadcasted_iota(jnp.int32, shape, 2)
    return row, (row >= 80) & (row < 83) & (lane >= 128)


def going(summed, scalars):
    if scalars:
        row, held = scalar_places(summed.shape)
        upper = lax.reduce_precision(summed, 8, 7)
        middle = lax.reduce_precision(summed - upper, 8, 7)
        parts = jnp.where(row == 81, summed - upper, jnp.where(row == 82, (summed - upper) - middle, summed))
        summed = jnp.where(held, parts, summed)
    return low(summed)


def coming(got, scalars):
    got = got.astype(F32)
    if scalars:
        _, held = scalar_places(got.shape)
        whole = (got[:, 80:81] + got[:, 81:82]) + got[:, 82:83]
        got = jnp.where(held, jnp.broadcast_to(whole, got.shape), got)
    return got


def split(summed):
    half = summed.shape[0] // 2
    return summed[:half], summed[half:]


def reduce_both(auto_keep, auto_got, judge_send, judge_keep):
    judge_got = swap(judge_send, "dp", 1)
    auto_got, judge_got = lax.optimization_barrier((auto_got, judge_got))
    auto_keep, auto_send = split(auto_keep + coming(auto_got, False))
    judge_keep, judge_send = split(judge_keep + judge_got)
    auto_got = swap(going(auto_send, False), "dp", 4)
    judge_got = swap(going(judge_send, True), "dp", 2)
    auto_got, judge_got = lax.optimization_barrier((auto_got, judge_got))
    auto_keep, auto_send = split(auto_keep + coming(auto_got, False))
    judge_keep, judge_send = split(judge_keep + coming(judge_got, True))
    auto_got = swap(auto_send, "dp", 8)
    judge_got = swap(going(judge_send, True), "dp", 4)
    auto_got, judge_got = lax.optimization_barrier((auto_got, judge_got))
    auto_keep = auto_keep + auto_got
    judge_keep, judge_send = split(judge_keep + coming(judge_got, True))
    auto_got = swap(auto_keep, "grp", 1)
    judge_got = swap(judge_send, "dp", 8)
    auto_got, judge_got = lax.optimization_barrier((auto_got, judge_got))
    judge_keep = judge_keep + judge_got
    judge_got = swap(judge_keep, "grp", 1)
    return auto_keep[0] + auto_got[0], judge_keep[0] + judge_got[0]


def unpack_auto(total):
    project = total[:96].reshape(2, 48, 256)
    matrices = total[96:160].reshape(4, 16, 256)
    fsq_pair = jnp.stack([total[160:176, 0:6], total[160:176, 128:134]])
    gain_pair = jnp.stack([jnp.sum(total[176:192, 0:128], axis=1), jnp.sum(total[176:192, 128:256], axis=1)])
    return project, matrices, fsq_pair, gain_pair


def unpack_judge_grads(total):
    mid = jnp.concatenate([total[:64, :128], total[:64, 128:]], axis=0)
    head = jnp.sum(total[64:80, 0:128], axis=1)
    last = total[64:80, 128:256].T
    first = total[80:84, 0:48].T
    return first, mid, last, head


def whole_slabs(first, clip_frames, frame_bounds, masters):
    gathered = [lax.all_gather(item, "dp", axis=axis, tiled=True) for item, axis in zip(masters, AXES)]

    def share(array, axis, number):
        size = array.shape[axis] // SLABS
        return lax.slice_in_dim(array, number * size, number * size + size, axis=axis)

    slabs = []
    for number in range(SLABS):
        shares = [share(item, axis, number) for item, axis in zip(gathered, AXES)]
        lane_info, slab = frame_lanes(first, clip_frames, frame_bounds, shares)
        slabs.append(slab)
    held = slabs[0][224, 224:227].astype(F32)
    total = lax.psum(held[0] + held[1] + held[2], "dp")
    upper = low(total)
    middle = low(total - upper.astype(F32))
    lower = low(total - upper.astype(F32) - middle.astype(F32))
    parts = jnp.stack([upper, middle, lower])
    slabs = [slab.at[224, 224:227].set(parts if number == 0 else 0) for number, slab in enumerate(slabs)]
    return lane_info, tuple(jnp.stack([slabs[value ^ core] for value in VALUES]) for core in range(2))


def whole_grads(auto, judge):
    def ordered(send, keep):
        pieces = [None] * SLABS
        for place, value in enumerate(VALUES):
            pieces[value] = keep[place]
            pieces[value ^ 1] = send[place].astype(F32)
        return pieces

    shares = [
        unpack_auto(left) + unpack_judge_grads(right) for left, right in zip(ordered(*auto), ordered(*judge))
    ]
    totals = []
    for index, axis in enumerate(AXES):
        whole = jnp.concatenate([share[index] for share in shares], axis=axis)
        totals.append(lax.psum_scatter(whole, "dp", scatter_dimension=axis, tiled=True))
    scalars = judge[1][0, 80, 128:131]
    totals.append(lax.psum(scalars, "dp"))
    return lax.psum(tuple(totals), "grp")


def adamw(master, moment, square, grad, rate, decay):
    new_moment = BETA_ONE * moment + (1.0 - BETA_ONE) * grad
    new_square = BETA_TWO * square + (1.0 - BETA_TWO) * grad * grad
    update = (
        new_moment
        / (1.0 - BETA_ONE**STEP)
        / (jnp.sqrt(new_square / (1.0 - BETA_TWO**STEP)) + ADAM_EPS)
    )
    return (new_moment, new_square, master - rate * (update + decay * master))


def constants():
    products = np.cumprod((1,) + LEVELS)[:6]
    rows = np.zeros((5, 16), np.float32)
    rows[1] = 1.0
    rows[2] = 1.0
    rows[0, :6] = 1.0 / products
    rows[1, :6] = LEVELS
    rows[2, :6] = 1.0 / np.array(LEVELS)
    rows[3, :6] = HALVES
    rows[4, :6] = 1.0 / np.array(HALVES)
    consts = np.broadcast_to(rows.reshape(80, 1), (80, 128)).astype(np.float32)
    places = np.arange(768)
    down = places // 48 // 4 * 4 + places % 48 // 12
    across = places // 48 % 4 * 4 + places % 48 % 12 // 3
    spots = np.broadcast_to(np.stack([down, across])[:, :, None], (2, 768, 128)).astype(np.float32)
    return jnp.asarray(consts), jnp.asarray(spots)


def on_device(pixels, frame_bounds, clip_frames, codes, *states):
    masters, moments, squares = states[:8], states[8:16], states[16:24]
    frames, band = pixels.shape[:2]
    grp, bands = lax.axis_index("grp"), lax.axis_size("grp")
    me, parts = lax.axis_index("dp"), lax.axis_size("dp")
    shared = parts == SLABS
    positions = frames * 16
    count_all = float(frames * parts * 256)

    code_halos = neighbours(codes, grp, bands)
    code_rows = codes.transpose(1, 0, 2).reshape(band, positions).astype(F32)
    counts = count_codes(code_rows)
    both_counts = counts + swap(counts, "grp", 1) if bands == 2 else lax.psum(counts, "grp")
    halos = neighbours(pixels, grp, bands)
    if shared:
        lane_info, slab = frame_lanes(me * frames, clip_frames, frame_bounds, masters)
        slabs = gather_slabs(slab, (counts, None, (code_halos, both_counts)))
    else:
        lane_info, slabs = whole_slabs(me * frames, clip_frames, frame_bounds, masters)
    counts = lax.psum(both_counts, "dp")

    places = jnp.stack(
        [grp * band, (grp < bands - 1).astype(jnp.int32), (grp > 0).astype(jnp.int32), me if shared else jnp.int32(0)]
    ).astype(jnp.int32)
    above, under = (item.reshape(1, positions).astype(F32) for item in (code_halos[1], code_halos[0]))
    all_codes = jnp.concatenate([above, code_rows, under], axis=0)
    extra = (all_codes, lane_info, *constants())

    fake_outs = run_fake(pixels, places, slabs, extra, count_all)
    halos, counts, fake_outs = lax.optimization_barrier((halos, counts, fake_outs))
    auto, starts = fake_outs[:2], fake_outs[2:7]
    if shared:
        auto_send, auto_keep = auto
        auto_keep, auto_send = split(auto_keep + swap(auto_send, "dp", 1))
        got = swap(going(auto_send, False), "dp", 2)
    judge = run_real(pixels, halos, places, slabs, starts, count_all)
    if shared:
        got, judge = lax.optimization_barrier((got, judge))
        auto_total, judge_total = reduce_both(auto_keep, got, *judge)
        totals = (*unpack_auto(auto_total), *unpack_judge_grads(judge_total))
        losses = judge_total[80, 128:131]
    else:
        *totals, losses = whole_grads(auto, judge)

    shares = counts * (1.0 / count_all)
    perplexity = jnp.exp(-jnp.sum(jax.scipy.special.xlogy(shares, shares)))
    results = [
        adamw(
            masters[number],
            moments[number],
            squares[number],
            totals[number],
            RATE_GAIN if number == 3 else RATE_MATRIX,
            0.0 if number == 3 else DECAY,
        )
        for number in range(8)
    ]
    return (
        *(result[0] for result in results),
        *(result[1] for result in results),
        *(result[2] for result in results),
        jnp.where(jnp.arange(2) == 0, losses[0], fake_outs[6][3, 0]),
        losses[1:3],
        perplexity,
    )


def solution(mesh):
    states = (
        P(None, "dp", None),
        P(None, "dp", None),
        P(None, "dp", None),
        P(None, "dp"),
        P(None, "dp"),
        P("dp", None),
        P(None, "dp"),
        P("dp"),
    )
    return jax.shard_map(
        on_device,
        mesh=mesh,
        in_specs=(P("dp", "grp", None, None), P("dp", None), P(), P("dp", "grp", None)) + states * 3,
        out_specs=states * 3 + (P(), P(), P()),
        check_vma=False,
    )
```

```python
import jax
import jax.numpy as jnp
import numpy as np
from jax import lax
from jax.experimental import pallas as pl
from jax.experimental.pallas import tpu as pltpu
from jax.sharding import PartitionSpec as P

STEP = 10
EPS_NORM = 1e-06
BETA_ONE = 0.9
BETA_TWO = 0.95
ADAM_EPS = 1e-08
DECAY = 0.1
RATE_MATRIX = 0.04
RATE_GAIN = 0.25
GEN_WEIGHT = 0.02
HALVES = (3.5, 3.5, 3.5, 2.0, 2.0, 2.0)
LEVELS = (8, 8, 8, 5, 5, 5)

F32 = jnp.float32
BF16 = jnp.bfloat16
VMEM_LIMIT = 60 * 2**20
FAKE_LANES = 512
REAL_LANES = 1024
REAL_PART = 256
SLABS = 16
VALUES = (0, 8, 4, 12, 2, 10, 6, 14)
WINDOWS = (0, 128, 384, 512)
AUTO_ROWS = 160
SLAB_ROWS = 240
AXES = (1, 1, 1, 1, 1, 0, 1, 0)
HIGHEST = lax.Precision.HIGHEST


def nn(left, right):
    return jnp.dot(left, right, preferred_element_type=F32)


def nt(left, right):
    return lax.dot_general(left, right, (((1,), (1,)), ((), ())), preferred_element_type=F32)


def low(value):
    return value.astype(BF16)


def wide(columns, lanes):
    return jnp.concatenate([columns] * (lanes // 128), axis=1)


def fold(value):
    total = value[:, :128]
    for start in range(128, value.shape[1], 128):
        total = total + value[:, start : start + 128]
    return total


def silu_parts(half):
    turned = jnp.tanh(half)
    upper = 1.0 + turned
    acted = half * upper
    return acted, upper + acted * (1.0 - turned)


def norm_parts(stream):
    scaling = lax.rsqrt(jnp.mean(stream * stream, axis=0, keepdims=True) + EPS_NORM)
    return scaling, stream * scaling


def softplus(value):
    return jnp.maximum(value, 0.0) + jnp.log1p(jnp.exp(-jnp.abs(value)))


def cost(flops, moved):
    return pl.CostEstimate(flops=int(flops), bytes_accessed=int(moved), transcendentals=0)


def aligned(index, size):
    return pl.ds(pl.multiple_of(index * size, size), size)


def interleave(*streams):
    places = []
    for index, (stream, count, *span) in enumerate(streams):
        start, stop = span or (0.0, 1.0)
        places += [(start + (stop - start) * (piece + 0.5) / count, index) for piece in range(count)]
    for _, index in sorted(places):
        next(streams[index][0], None)
    for stream, *_ in streams:
        for _ in stream:
            pass


def slab_owners(me, slabs):
    for core, array in enumerate(slabs):
        for place, value in enumerate(VALUES):
            yield me ^ value ^ core, array.at[place]


def unpack_judge(me, slabs, pair_s, misc_s, first_row):
    for owner, slab in slab_owners(me, slabs):
        rows = pl.ds(pl.multiple_of(lax.rem(owner, 8) * 128, 128), 64)
        more = pl.ds(pl.multiple_of(lax.rem(owner, 8) * 128 + 64, 64), 64)
        side = owner // 8
        pair_s[side, rows, :] = slab[first_row : first_row + 64, 0:128]
        pair_s[side, more, :] = slab[first_row : first_row + 64, 128:256]
        misc_s[aligned(owner, 16), :] = slab[first_row + 64 : first_row + 80, :]


def slab_targets(me):
    for core in range(2):
        for place, value in enumerate(VALUES):
            yield me ^ value ^ core, core, place


def prepare_judge(pair_s, misc_s, judge):
    wmt_s, wmh_s, wlt_s, wlh_s, headw_s, headr_s, bdt_s, bd_s, windows_s = judge
    half = jnp.asarray(0.5, BF16)
    for side in range(2):
        columns = pl.ds(side * 128, 128)
        for part in range(4):
            rows = pl.ds(part * 256, 256)
            block = pair_s[side, rows, :] * half
            wmh_s[rows, columns] = block
            wmt_s[columns, rows] = block.T
    last_t = misc_s[:, 0:128]
    wlt_s[...] = last_t * half
    wlh_s[...] = last_t.T * half
    turned = misc_s[:, 128:256].T
    headr_s[...] = turned[32:48, :]
    headw_s[...] = jnp.broadcast_to(misc_s[:, 128:256].astype(F32)[:, 32:33] * 0.5, headw_s.shape)
    row = lax.broadcasted_iota(jnp.int32, (256, 256), 0) % 64
    column = lax.broadcasted_iota(jnp.int32, (256, 256), 1)
    pick = low(jnp.where(column == row // 4 * 16 + row % 4, 1.0, 0.0))
    picked = low(nn(pick, misc_s[...]))
    lane = lax.broadcasted_iota(jnp.int32, (256, 192), 0)
    place = lax.broadcasted_iota(jnp.int32, (256, 192), 1)
    spread = low(jnp.where(lane == 176 + place % 48, 1.0, 0.0))
    diagonal = (lane // 64) == (place // 48)
    band_t = jnp.where(diagonal, nn(picked, spread), 0.0)
    if bdt_s is not None:
        bdt_s[...] = low(band_t * 0.5)
        bd_s[...] = low(band_t).T
    if windows_s is not None:
        windows_s[...] = jnp.zeros_like(windows_s)
        windows_s[0, :, 0:192] = low(band_t * 0.5)
        lane = lax.broadcasted_iota(jnp.int32, (256, 256), 0)
        place = lax.broadcasted_iota(jnp.int32, (256, 256), 1)
        spread = low(jnp.where((lane == 176 + (place + 32) % 48) & (place >= 64), 1.0, 0.0))
        diagonal = (lane // 64) == (place - 64) // 48
        windows_s[1] = low(jnp.where(diagonal & (place >= 64), nn(picked, spread), 0.0) * 0.5)


def judge_scratch(fake):
    shapes = [((256, 1024), BF16), ((1024, 256), BF16), ((256, 128), BF16), ((128, 256), BF16)]
    shapes += [((256, 128), F32), ((16, 256), BF16)]
    if fake:
        shapes += [((256, 192), BF16), ((192, 256), BF16)]
    else:
        shapes += [((2, 256, 256), BF16)]
    return shapes


def judge_middle(part, act, q_s, judge, count_all, active, counted, kind, held, ghead_ref, loss_ref, new_g2):
    wmt_s, _, wlt_s, wlh_s, headw_s, headr_s = judge[:6]
    two_s, three_s = held
    fresh = nn(wmt_s[...], act[:, part])
    yield
    acted_two, slope_two = silu_parts(fresh[:128] + q_s[:, part])
    q_s[:, part] = fresh[128:]
    acted_two = low(acted_two)
    two_s[:, part] = acted_two * counted.astype(BF16)
    yield
    acted_three, slope_three = silu_parts(nn(wlt_s[...], acted_two))
    acted_three = low(acted_three)
    yield
    score = nn(headr_s[...], acted_three)[:1]
    shaped = wide(headw_s[...], score.shape[1]) * slope_three
    yield
    if kind == "real":
        grad_score = -jax.nn.sigmoid(1.0 - score) * (active / count_all)
        grad_three = low(grad_score * shaped)
        three_s[:, part] = grad_three
        loss_ref[0:1, part] += softplus(1.0 - score) * counted
        yield
        new_g2[0][:, part] = low(nn(wlh_s[...], grad_three) * slope_two)
    else:
        pull = jax.nn.sigmoid(1.0 + score)
        grad_score = pull * (active / count_all)
        three_s[:, part] = low(grad_score * shaped)
        grad_three_gen = low((-GEN_WEIGHT / count_all * active) * shaped)
        loss_ref[0:1, part] += softplus(1.0 + score) * counted
        loss_ref[1:2, part] -= score * counted
        yield
        grad_two_gen = nn(wlh_s[...], grad_three_gen) * slope_two
        new_g2[0][:, part] = low(grad_two_gen * (pull * (-1.0 / GEN_WEIGHT)))
        new_g2[1][:, part] = low(grad_two_gen)
    yield
    ghead_ref[...] += fold(acted_three.astype(F32) * (grad_score * counted))
    yield


def real_kernel(band, lanes, chunks, count_all, share):
    rows_n = band + 1
    total = chunks * rows_n

    def kernel(*refs):
        refs = list(refs)

        def take(number):
            taken = refs[:number]
            del refs[:number]
            return taken

        (places,) = take(1)
        slabs = take(2)
        xf, xe, xbelow, xabove = take(4)
        start_refs = take(4)
        (fake_loss,) = take(1)
        send_ref, keep_ref = take(2)
        judge = take(6) + [None, None] + take(1)
        pair_s, misc_s = take(2)
        gwm_ref, gwl_ref, gw1_ref, gwin_ref, ghead_ref = take(5)
        q_s, g2, g2_new, act_s, slope_s, small = take(6)
        first_s, lastt_s, loss_ref = take(3)
        held = take(2)
        wmt_s, wmh_s, windows_s = judge[0], judge[1], judge[8]
        stage = pl.program_id(0)
        has_below, has_above, me = places[1], places[2].astype(F32), places[3]
        step = lax.rem(stage, rows_n)
        row = band - 1 - step
        slot = lax.rem(stage, 2)
        back_ok = (stage >= 2) & (lax.rem(stage - 2, rows_n) != band)
        front_ok = stage < total
        act, slope = act_s.at[slot], slope_s.at[slot]
        halo = row < 0
        active = jnp.where(halo, has_above, 1.0)
        counted = jnp.where(halo, 0.0, 1.0)

        @pl.when(stage == 0)
        def prepare():
            unpack_judge(me, slabs, pair_s, misc_s, 0)
            prepare_judge(pair_s, misc_s, judge)
            for ref, start in zip((gwm_ref, gwl_ref, gw1_ref, ghead_ref), start_refs):
                ref[...] = start[...]
            loss_ref[...] = jnp.zeros_like(loss_ref)
            gwin_ref[...] = jnp.zeros_like(gwin_ref)

        @pl.when(front_ok & (step == 0) & (has_below > 0))
        def below():
            joined = jnp.zeros((128, lanes), F32)
            for group in range(4):
                x = xbelow[:, :, WINDOWS[group] : WINDOWS[group] + 256].reshape(lanes, 256)
                acted, _ = silu_parts(nt(windows_s[group % 2], x))
                joined = joined + nn(wmt_s[128:256, 256 * group : 256 * group + 256], low(acted))
            q_s[...] = joined

        @pl.when(front_ok & (step == 0) & (has_below == 0))
        def edge():
            q_s[...] = jnp.zeros_like(q_s)

        def back_small():
            for group in range(4):
                rows = slice(256 * group, 256 * group + 256)
                for start in range(0, lanes, 256):
                    part = slice(start, start + 256)
                    small[rows, part] = low(nn(wmh_s[rows, :], g2[:, part]) * slope[rows, part])
                    yield

        def back_middle():
            for group in range(4):
                rows = slice(256 * group, 256 * group + 256)
                gwm_ref[rows, :] += nt(act[rows, :], g2[...])
                yield

        def back_first():
            for group in range(4):
                x = xe[:, 0, :, WINDOWS[group] : WINDOWS[group] + 256].reshape(lanes, 256)
                gwin_ref[group % 2] += nn(small[256 * group : 256 * group + 256, :], x)
                yield

        def front_first():
            for group in range(4):
                for start in range(0, lanes, 256):
                    part = slice(start, start + 256)
                    some, window = slice(start // 16, start // 16 + 16), slice(WINDOWS[group], WINDOWS[group] + 256)
                    x = jnp.where(halo, xabove[some, :, window], xf[some, 0, :, window]).reshape(256, 256)
                    acted, slope_new = silu_parts(nt(windows_s[group % 2], x))
                    act[256 * group : 256 * group + 256, part] = low(acted)
                    slope[256 * group : 256 * group + 256, part] = slope_new
                    yield

        def front_middle(part):
            return judge_middle(
                part, act, q_s, judge, count_all, active, counted, "real", held, ghead_ref, loss_ref, (g2_new,)
            )

        def front_last():
            gwl_ref[...] += nt(held[0][...], held[1][...])
            yield

        def shift():
            g2[0:128, :] = g2[128:256, :]
            g2[128:256, :] = g2_new[...]

        parts = [slice(start, start + REAL_PART) for start in range(0, lanes, REAL_PART)]

        @pl.when(front_ok & back_ok)
        def both():
            interleave(
                (back_small(), lanes // 64, 0.0, 0.8),
                (back_middle(), 4, 0.0, 0.8),
                (front_first(), lanes // 64, 0.2, 1.0),
            )
            interleave(*((front_middle(part), 7) for part in parts), (back_first(), 4))
            interleave((front_last(), 1))
            shift()

        @pl.when(front_ok & jnp.logical_not(back_ok))
        def front_only():
            interleave((front_first(), 1))
            interleave(*((front_middle(part), 7) for part in parts))
            interleave((front_last(), 1))
            shift()

        @pl.when(jnp.logical_not(front_ok) & back_ok)
        def back_only():
            interleave((back_small(), 1))
            interleave((back_first(), 4), (back_middle(), 4))

        @pl.when(stage == total)
        def write():
            turned = gw1_ref[...].T
            lane = lax.broadcasted_iota(jnp.int32, (64, 192), 1)
            summed = jnp.zeros((64, 192), F32)
            for block in range(4):
                summed = summed + jnp.where(lane // 48 == block, turned[64 * block : 64 * block + 64, :], 0.0)
            place = lax.broadcasted_iota(jnp.int32, (192, 128), 0) % 48
            folding = jnp.where(place == lax.broadcasted_iota(jnp.int32, (192, 128), 1), 1.0, 0.0)
            first = jnp.dot(summed, folding, precision=HIGHEST, preferred_element_type=F32)
            lane = lax.broadcasted_iota(jnp.int32, (64, 256), 1)
            place = lax.broadcasted_iota(jnp.int32, (256, 128), 0)
            for odd in range(2):
                summed = jnp.zeros((64, 256), F32)
                for block in range(4):
                    start = 64 * odd + 48 * block
                    inside = (lane >= start) & (lane < start + 48)
                    summed = summed + jnp.where(inside, gwin_ref[odd, 64 * block : 64 * block + 64, :], 0.0)
                folding = jnp.where((place + 32 * odd) % 48 == lax.broadcasted_iota(jnp.int32, (256, 128), 1), 1.0, 0.0)
                first = first + jnp.dot(summed, folding, precision=HIGHEST, preferred_element_type=F32)
            for owner in range(SLABS):
                first_s[16 * owner : 16 * owner + 16, :] = jnp.zeros((16, 128), F32)
                first_s[16 * owner : 16 * owner + 4, :] = first[4 * owner : 4 * owner + 4, :]
            lastt_s[...] = gwl_ref[...].T
            scalars = jnp.zeros((1, 128), F32)
            sums = (
                jnp.sum(fake_loss[2:3, :]),
                jnp.sum(fake_loss[3:4, 0:1]) * share,
                jnp.sum(fake_loss[1:2, :]),
                jnp.sum(fake_loss[0:1, :]) + jnp.sum(loss_ref[0:1, :]),
            )
            for number, item in enumerate(sums):
                scalars = jnp.where(lax.broadcasted_iota(jnp.int32, (1, 128), 1) == number, item, scalars)
            for owner, core, chip in slab_targets(me):
                side, rows = owner // 8, lax.rem(owner, 8) * 128
                upper = pl.ds(pl.multiple_of(rows, 64), 64)
                lower = pl.ds(pl.multiple_of(rows + 64, 64), 64)
                own = aligned(owner, 16)
                left = jnp.where(side == 0, gwm_ref[upper, 0:128], gwm_ref[upper, 128:256])
                right = jnp.where(side == 0, gwm_ref[lower, 0:128], gwm_ref[lower, 128:256])
                target = (keep_ref, send_ref)[core]
                target[chip, 0:64, 0:128] = left
                target[chip, 0:64, 128:256] = right
                target[chip, 64:80, 0:128] = ghead_ref[own, :]
                target[chip, 64:80, 128:256] = lastt_s[own, :]
                target[chip, 80:96, 0:128] = first_s[own, :]
                target[chip, 80:96, 128:256] = jnp.where(lax.broadcasted_iota(jnp.int32, (16, 128), 0) < 3, scalars, 0.0)

    return kernel


def run_real(pixels, halos, places, slabs, starts, count_all):
    frames, band = pixels.shape[:2]
    positions = frames * 16
    lanes = min(REAL_LANES, positions)
    chunks = positions // lanes
    rows_n = band + 1
    total = chunks * rows_n

    halo_spec = pl.BlockSpec((lanes // 16, 16, 768), lambda t: (jnp.minimum(t, total - 1) // rows_n, 0, 0))
    specs = [pl.BlockSpec(memory_space=pltpu.SMEM)]
    specs += [pl.BlockSpec((SLABS // 2, 80, 256), lambda t: (0, 2, 0))] * 2
    specs += stage_rows(band, lanes, chunks)
    specs += [halo_spec] * 2
    specs += [pl.BlockSpec(item.shape, lambda t: (0, 0)) for item in starts]
    outs = [
        jax.ShapeDtypeStruct((SLABS // 2, 96, 256), F32),
        jax.ShapeDtypeStruct((SLABS // 2, 96, 256), F32),
    ]
    scratch = judge_scratch(False) + [((2, 1024, 128), BF16), ((256, 256), BF16)]
    scratch += [((1024, 256), F32), ((128, 256), F32), ((192, 256), F32), ((2, 256, 256), F32), ((256, 128), F32)]
    scratch += [((128, lanes), F32), ((256, lanes), BF16), ((128, lanes), BF16)]
    scratch += [((2, 1024, lanes), BF16), ((2, 1024, lanes), F32), ((1024, lanes), BF16)]
    scratch += [((256, 128), F32), ((256, 128), F32), ((8, lanes), F32)]
    scratch += [((128, lanes), BF16), ((256, lanes), BF16)]
    return pl.pallas_call(
        real_kernel(band, lanes, chunks, count_all, 1.0 / (lax.axis_size("dp") * lax.axis_size("grp"))),
        grid=(total + 1,),
        in_specs=specs,
        out_specs=[pl.BlockSpec(item.shape, lambda t, n=len(item.shape): (0,) * n) for item in outs],
        out_shape=outs,
        scratch_shapes=[pltpu.VMEM(*item) for item in scratch],
        compiler_params=pltpu.CompilerParams(vmem_limit_bytes=VMEM_LIMIT),
        cost_estimate=cost(5.4e6 * band * positions, 3072 * band * positions),
        name="judge_real",
    )(places, *slabs, pixels, pixels, *halos, *starts)


def block_steps(stream, gain, first_half_t, second_t):
    scaling, normal = norm_parts(stream)
    normed = low(normal * gain)
    yield None
    acted, slope = silu_parts(nn(first_half_t[...], normed))
    acted = low(acted)
    yield None
    yield stream + nn(second_t[...], acted), (scaling, normal, normed, acted, slope)


def fake_kernel(band, lanes, chunks, count_all):
    rows_n = band + 1
    total = chunks * rows_n
    halves = [slice(start, start + 256) for start in range(0, lanes, 256)]

    def kernel(*refs):
        refs = list(refs)

        def take(number):
            taken = refs[:number]
            del refs[:number]
            return taken

        (places,) = take(1)
        slabs = take(2)
        xf_ref, xe_ref, codes_ref, lane_ref, consts_ref, spots_ref = take(6)
        send_ref, keep_ref, gwm_ref, gwl_ref, gw1_ref, ghead_ref, loss_ref = take(7)
        judge = take(8) + [None]
        pair_s, misc_s = take(2)
        proj_s, projt_s, block_s, blockt_s, blockh_s, fsq_s, fsqt_s, gains_s, total_s = take(9)
        gproj_ref, gprojt_ref, gblocks_ref, gfsq_ref, gfsqt_ref, ggains_ref = take(6)
        q_s, g2_disc, g2_gen, new_disc, new_gen, small_s, smallgen_s, gradlow_s, xt_s = take(9)
        fake_s, gl1_s, act_s, slope_s = take(4)
        saved_s = take(5)
        outlow_s, values_s = take(2)
        encoded_s = take(7)
        outer_s, inner_s, start_s, latent_s, stream_s = take(5)
        held = take(2)
        wmt_s, wmh_s, bdt_s, bd_s = judge[0], judge[1], judge[6], judge[7]
        stage = pl.program_id(0)
        row_start, has_below, me = places[0], places[1], places[3]
        has_above = places[2].astype(F32)
        step = lax.rem(stage, rows_n)
        row = band - 1 - step
        slot, slot_three, back_three = lax.rem(stage, 2), lax.rem(stage, 3), lax.rem(stage + 1, 3)
        back_ok = (stage >= 2) & (lax.rem(stage - 2, rows_n) != band)
        front_ok = stage < total
        gl1, act, slope = gl1_s.at[slot], act_s.at[slot], slope_s.at[slot]
        fake, fake_back = fake_s.at[slot_three], fake_s.at[back_three]
        counted = jnp.where(row >= 0, 1.0, 0.0)
        active = jnp.where(row >= 0, 1.0, has_above)

        @pl.when(stage == 0)
        def prepare():
            unpack_judge(me, slabs, pair_s, misc_s, AUTO_ROWS)
            prepare_judge(pair_s, misc_s, judge)
            for owner, slab in slab_owners(me, slabs):
                rows, some = aligned(owner, 48), aligned(owner, 16)
                proj_s[0, rows, :] = slab[0:48, :]
                proj_s[1, rows, :] = slab[48:96, :]
                for index in range(4):
                    block_s[index, some, :] = slab[96 + 16 * index : 112 + 16 * index, :]
            projt_s[0] = proj_s[0].T
            projt_s[1] = proj_s[1].T
            for index in range(4):
                scale = jnp.asarray(0.5 if index % 2 == 0 else 1.0, BF16)
                blockt_s[index] = (block_s[index] * scale).T
                if index % 2 == 1:
                    blockh_s[index // 2] = block_s[index] * jnp.asarray(0.5, BF16)
            tail = misc_s[:, 128:256]
            turned = tail.T
            fsqt_s[0] = turned[0:16, :]
            fsqt_s[1] = turned[16:32, :]
            for index in range(2):
                fsq_s[index] = fsqt_s[index].T
                gains_s[index] = jnp.broadcast_to(tail.astype(F32)[:, 33 + index : 34 + index], (256, 128))
            lane = lax.broadcasted_iota(jnp.int32, (256, 128), 1)
            held = (lane >= 96) & (lane < 99)
            total_s[...] = jnp.broadcast_to(jnp.sum(jnp.where(held, tail.astype(F32), 0.0)), (8, 128))
            for ref in (gwm_ref, gwl_ref, gw1_ref, ghead_ref, loss_ref, gproj_ref, gprojt_ref, gblocks_ref, gfsqt_ref, ggains_ref):
                ref[...] = jnp.zeros_like(ref)

        def latent_values(row):
            consts = consts_ref[...]
            code = codes_ref[pl.ds(row + 1, 1), :]
            turn = jnp.floor((code + 0.5) * wide(consts[0:16], lanes))
            level = wide(consts[16:32], lanes)
            digit = turn - level * jnp.floor((turn + 0.5) * wide(consts[32:48], lanes))
            return low((digit - wide(consts[48:64], lanes)) * wide(consts[64:80], lanes))

        @pl.when(front_ok & (step == 0) & (has_below > 0))
        def below():
            values = latent_values(jnp.int32(band))
            outputs = list(block_steps(nn(fsq_s[1], values), wide(gains_s[1], lanes), blockt_s.at[2], blockt_s.at[3]))
            outlow = low(outputs[-1][0])
            joined = jnp.zeros((128, lanes), F32)
            for group in range(4):
                recon = low(nn(proj_s[1, pl.ds(group * 192, 192), :], outlow))
                acted, _ = silu_parts(nn(bdt_s[...], recon))
                joined = joined + nn(wmt_s[128:256, 256 * group : 256 * group + 256], low(acted))
            q_s[...] = joined

        @pl.when(front_ok & (step == 0) & (has_below == 0))
        def edge():
            q_s[...] = jnp.zeros_like(q_s)

        def front_block(part):
            values = values_s[slot_three, :, part]
            width = values.shape[1]
            stream = nn(fsq_s[1], values)
            yield
            result = None
            for result in block_steps(stream, wide(gains_s[1], width), blockt_s.at[2], blockt_s.at[3]):
                yield
            output, saved = result
            outlow_s[slot_three, :, part] = low(output)
            for ref, item in zip(saved_s, saved):
                ref[slot_three, :, part] = item
            yield

        def front_turn():
            for part in halves:
                some = slice(part.start // 16, part.stop // 16)
                for column in range(0, 768, 256):
                    xt_s[column : column + 256, part] = xf_ref[some, 0, :, column : column + 256].reshape(256, 256).T
                    yield

        def front_recon():
            lane = lax.broadcasted_iota(jnp.int32, (1, lanes), 1)
            column = (lane % 16).astype(F32)
            place = (row_start + row).astype(F32)
            high = lane_ref[0:1, :] - 16.0 * place
            broad = lane_ref[1:2, :] - 16.0 * column
            weight = lane_ref[2:3, :] * counted
            weight_share = weight / wide(total_s[0:1, :], lanes)
            sums = [jnp.zeros((1, 256), F32) for _ in halves]
            for group in range(4):
                rows = slice(group * 192, group * 192 + 192)
                for index, part in enumerate(halves):
                    recon = nn(proj_s[1, rows, :], outlow_s[slot_three, :, part])
                    fake[rows, part] = low(recon)
                    diff = recon - xt_s[rows, part].astype(F32)
                    square = diff * diff + 1.0
                    inside = (wide(spots_ref[0, rows, :], 256) < high[:, part]) & (
                        wide(spots_ref[1, rows, :], 256) < broad[:, part]
                    )
                    share = lax.rsqrt(square) * jnp.where(inside, weight_share[:, part], 0.0)
                    gl1[rows, part] = diff * share
                    sums[index] = sums[index] + jnp.sum(square * share, axis=0, keepdims=True)
                    yield
            loss_ref[2:3, :] += jnp.concatenate(sums, axis=1) * wide(total_s[0:1, :], lanes)

        def front_first():
            for group in range(4):
                for part in halves:
                    acted, slope_new = silu_parts(nn(bdt_s[...], fake[192 * group : 192 * group + 192, part]))
                    act[256 * group : 256 * group + 256, part] = low(acted)
                    slope[256 * group : 256 * group + 256, part] = slope_new
                    yield

        def front_middle(part):
            return judge_middle(
                part, act, q_s, judge, count_all, active, counted, "fake", held, ghead_ref, loss_ref, (new_disc, new_gen)
            )

        def front_last():
            gwl_ref[...] += nt(held[0][...], held[1][...])
            yield

        def back_gen():
            for group in range(4):
                rows = slice(256 * group, 256 * group + 256)
                for part in halves:
                    smallgen_s[rows, part] = low(nn(wmh_s[rows, :], g2_gen[:, part]) * slope[rows, part])
                    yield

        def back_disc():
            for group in range(4):
                rows = slice(256 * group, 256 * group + 256)
                for part in halves:
                    small_s[rows, part] = low(nn(wmh_s[rows, :], g2_disc[:, part]) * slope[rows, part])
                    yield

        def back_recon():
            for group in range(4):
                rows = slice(group * 192, group * 192 + 192)
                gradlow_s[rows, :] = low(gl1[rows, :] + nn(bd_s[...], smallgen_s[256 * group : 256 * group + 256, :]))
                yield

        def back_first():
            for group in range(4):
                rows = slice(group * 192, group * 192 + 192)
                gw1_ref[...] += nt(fake_back[rows, :], small_s[256 * group : 256 * group + 256, :])
                yield

        def back_middle():
            for group in range(2):
                rows = slice(512 * group, 512 * group + 512)
                gwm_ref[rows, :] += nt(act[rows, :], g2_disc[...])
                yield

        def back_project():
            for group in range(2):
                rows = slice(group * 384, group * 384 + 384)
                gproj_ref[1, rows, :] += nt(gradlow_s[rows, :], outlow_s[back_three])
                yield

        def back_encode(part):
            some = slice(part.start // 16, part.stop // 16)
            stream = nt(projt_s[0], xe_ref[some].reshape(part.stop - part.start, 768))
            yield
            result = None
            for result in block_steps(
                stream, wide(gains_s[0], part.stop - part.start), blockt_s.at[0], blockt_s.at[1]
            ):
                yield
            middle, saved = result
            middle_low = low(middle)
            for ref, item in zip(encoded_s, (*saved, middle_low, nn(fsqt_s[0], middle_low))):
                ref[:, part] = item
            yield

        def back_block(grad_out, saved, index, part):
            scaling, normal, slope_in = saved
            gain = wide(gains_s[index], part.stop - part.start)
            outer = low(grad_out)
            outer_s[index, :, part] = outer
            grad_acted = nn(blockh_s[index], outer)
            yield None
            inner = low(grad_acted * slope_in)
            inner_s[index, :, part] = inner
            grad_normed = nn(block_s[2 * index], inner)
            yield None
            along = grad_normed * normal
            ggains_ref[index] += fold(along)
            mean = jnp.mean(along * gain, axis=0, keepdims=True)
            yield grad_out + scaling * (grad_normed * gain - normal * mean)

        def back_chain(part):
            grad_out = nn(projt_s[1], gradlow_s[:, part])
            yield
            saved = tuple(saved_s[n][back_three, :, part] for n in (0, 1, 4))
            grad_start = None
            for grad_start in back_block(grad_out, saved, 1, part):
                yield
            start_low = low(grad_start)
            start_s[:, part] = start_low
            grad_values = nn(fsqt_s[1], start_low)
            yield
            tangent = jnp.tanh(encoded_s[6][:, part])
            grad_latent = low(grad_values * (1.0 - tangent * tangent))
            latent_s[:, part] = grad_latent
            grad_middle = nn(fsq_s[0], grad_latent)
            yield
            saved = tuple(encoded_s[n][:, part] for n in (0, 1, 4))
            grad_stream = None
            for grad_stream in back_block(grad_middle, saved, 0, part):
                yield
            stream_s[:, part] = low(grad_stream)
            yield

        def back_fill():
            first, project, weights = back_first(), back_project(), back_weights()
            for piece in (first, project, first, weights, first, weights, project, first, weights, weights, weights):
                next(piece)
                yield

        def back_stream():
            gprojt_ref[...] += nn(stream_s[...], xe_ref[...].reshape(lanes, 768))
            yield

        def back_weights():
            gblocks_ref[3] += nt(saved_s[3][back_three], outer_s[1])
            yield
            gblocks_ref[2] += nt(saved_s[2][back_three], inner_s[1])
            yield
            gfsqt_ref[1] += nt(values_s[back_three], start_s[...])
            gfsqt_ref[0] += nt(latent_s[...], encoded_s[5][...])
            yield
            gblocks_ref[1] += nt(encoded_s[3][...], outer_s[0])
            yield
            gblocks_ref[0] += nt(encoded_s[2][...], inner_s[0])
            yield
        def shift():
            for ref, new in ((g2_disc, new_disc), (g2_gen, new_gen)):
                ref[0:128, :] = ref[128:256, :]
                ref[128:256, :] = new[...]

        @pl.when(front_ok & back_ok)
        def both():
            values_s[slot_three] = latent_values(row)
            interleave(
                (back_gen(), 4 * len(halves)),
                *((front_block(part), 5) for part in halves),
                (front_turn(), 6),
                (back_middle(), 2),
            )
            interleave(
                (back_recon(), 4, 0.0, 0.2),
                (back_disc(), 4 * len(halves), 0.0, 0.25),
                (front_recon(), 4 * len(halves), 0.02, 0.42),
                (front_first(), 4 * len(halves), 0.12, 0.53),
                *((back_encode(part), 5, 0.0, 0.45) for part in halves),
                *((back_chain(part), 10, 0.22, 0.95) for part in halves),
                *((front_middle(part), 7, 0.54, 1.0) for part in halves),
                (back_fill(), 11, 0.3, 1.0),
            )
            interleave((front_last(), 1), (back_stream(), 1))
            shift()

        @pl.when(front_ok & jnp.logical_not(back_ok))
        def front_only():
            values_s[slot_three] = latent_values(row)
            interleave(*((front_block(part), 5) for part in halves), (front_turn(), 6))
            interleave((front_recon(), 1))
            interleave((front_first(), 1))
            interleave(*((front_middle(part), 7) for part in halves))
            interleave((front_last(), 1))
            shift()

        @pl.when(jnp.logical_not(front_ok) & back_ok)
        def back_only():
            interleave((back_gen(), 4 * len(halves)), *((back_encode(part), 5) for part in halves))
            interleave((back_recon(), 4), (back_disc(), 4 * len(halves)))
            interleave(
                *((back_chain(part), 10) for part in halves), (back_middle(), 2), (back_first(), 4), (back_project(), 2)
            )
            interleave((back_weights(), 1), (back_stream(), 1))

        @pl.when(stage == total)
        def write():
            loss_ref[3:4, 0:128] = total_s[0:1, :]
            gproj_ref[0] = gprojt_ref[...].T
            for index in range(2):
                gfsq_ref[index] = gfsqt_ref[index].T
            for owner, core, chip in slab_targets(me):
                rows, own = aligned(owner, 48), aligned(owner, 16)
                target = (keep_ref, send_ref)[core]
                target[chip, 0:48, :] = gproj_ref[0, rows, :]
                target[chip, 48:96, :] = gproj_ref[1, rows, :]
                for index in range(4):
                    target[chip, 96 + 16 * index : 112 + 16 * index, :] = gblocks_ref[index, own, :]
                target[chip, 160:192, :] = jnp.zeros((32, 256), F32)
                target[chip, 160:176, 0:16] = gfsq_ref[0, own, :]
                target[chip, 160:176, 128:144] = gfsq_ref[1, own, :]
                target[chip, 176:192, 0:128] = ggains_ref[0, own, :]
                target[chip, 176:192, 128:256] = ggains_ref[1, own, :]

    return kernel


def stage_rows(band, lanes, chunks):
    rows_n = band + 1
    total = chunks * rows_n

    def front(t):
        t = jnp.minimum(t, total - 1)
        return (t // rows_n, jnp.maximum(band - 1 - lax.rem(t, rows_n), 0), 0, 0)

    def back(t):
        t = jnp.maximum(t - 2, 0)
        return (t // rows_n, jnp.maximum(band - 1 - lax.rem(t, rows_n), 0), 0, 0)

    block = (lanes // 16, 1, 16, 768)
    return pl.BlockSpec(block, front), pl.BlockSpec(block, back)


def run_fake(pixels, places, slabs, extra, count_all):
    frames, band = pixels.shape[:2]
    positions = frames * 16
    lanes = min(FAKE_LANES, positions)
    chunks = positions // lanes
    total = chunks * (band + 1)
    codes, lane_info, consts, spots = extra

    def whole(array):
        return pl.BlockSpec(array.shape, lambda t: (0,) * array.ndim)

    def chunk_spec(array):
        return pl.BlockSpec((array.shape[0], lanes), lambda t: (0, jnp.minimum(t, total - 1) // (band + 1)))

    specs = [pl.BlockSpec(memory_space=pltpu.SMEM)]
    specs += [whole(item) for item in slabs]
    specs += stage_rows(band, lanes, chunks)
    specs += [chunk_spec(codes), chunk_spec(lane_info), whole(consts), whole(spots)]
    outs = [
        jax.ShapeDtypeStruct((SLABS // 2, 192, 256), F32),
        jax.ShapeDtypeStruct((SLABS // 2, 192, 256), F32),
        *(jax.ShapeDtypeStruct(shape, F32) for shape in [(1024, 256), (128, 256), (192, 256), (256, 128), (8, lanes)]),
    ]
    scratch = judge_scratch(True) + [((2, 1024, 128), BF16), ((256, 256), BF16)]
    scratch += [((2, 768, 256), BF16), ((2, 256, 768), BF16), ((4, 256, 256), BF16), ((4, 256, 256), BF16)]
    scratch += [((2, 256, 256), BF16), ((2, 256, 16), BF16), ((2, 16, 256), BF16), ((2, 256, 128), F32), ((8, 128), F32)]
    scratch += [((2, 768, 256), F32), ((256, 768), F32), ((4, 256, 256), F32), ((2, 256, 16), F32), ((2, 16, 256), F32), ((2, 256, 128), F32)]
    scratch += [((128, lanes), F32)] + [((256, lanes), BF16)] * 2 + [((128, lanes), BF16)] * 2
    scratch += [((1024, lanes), BF16)] * 2 + [((768, lanes), BF16)] * 2
    scratch += [((3, 768, lanes), BF16), ((2, 768, lanes), F32), ((2, 1024, lanes), BF16), ((2, 1024, lanes), F32)]
    scratch += [((3, 1, lanes), F32), ((3, 256, lanes), F32), ((3, 256, lanes), BF16), ((3, 256, lanes), BF16)]
    scratch += [((3, 256, lanes), F32), ((3, 256, lanes), BF16), ((3, 16, lanes), BF16)]
    scratch += [((1, lanes), F32), ((256, lanes), F32), ((256, lanes), BF16), ((256, lanes), BF16)]
    scratch += [((256, lanes), F32), ((256, lanes), BF16), ((16, lanes), F32)]
    scratch += [((2, 256, lanes), BF16)] * 2 + [((256, lanes), BF16), ((16, lanes), BF16), ((256, lanes), BF16)]
    scratch += [((128, lanes), BF16), ((256, lanes), BF16)]
    return pl.pallas_call(
        fake_kernel(band, lanes, chunks, count_all),
        grid=(total + 1,),
        in_specs=specs,
        out_specs=[pl.BlockSpec(item.shape, lambda t, n=len(item.shape): (0,) * n) for item in outs],
        out_shape=outs,
        scratch_shapes=[pltpu.VMEM(*item) for item in scratch],
        compiler_params=pltpu.CompilerParams(vmem_limit_bytes=VMEM_LIMIT),
        cost_estimate=cost(1.6e7 * band * positions, 3072 * band * positions),
        name="judge_fake",
    )(places, *slabs, pixels, pixels, codes, lane_info, consts, spots)


def count_kernel(codes_ref, counts_ref):
    @pl.when(pl.program_id(0) == 0)
    def clear():
        counts_ref[...] = jnp.zeros_like(counts_ref)

    code = codes_ref[0]
    upper = jnp.floor(code * (1.0 / 256.0))
    lower = code - 256.0 * upper
    bins = lax.broadcasted_iota(jnp.int32, (256, code.shape[1]), 0).astype(F32)
    one, zero = jnp.asarray(1.0, F32), jnp.asarray(0.0, F32)
    counts_ref[...] += nt(low(jnp.where(bins == upper, one, zero)), low(jnp.where(bins == lower, one, zero)))


def count_codes(codes):
    parts, lanes = codes.shape
    return pl.pallas_call(
        count_kernel,
        grid=(parts,),
        in_specs=[pl.BlockSpec((1, 1, lanes), lambda s: (s, 0, 0))],
        out_specs=pl.BlockSpec((256, 256), lambda s: (0, 0)),
        out_shape=jax.ShapeDtypeStruct((256, 256), F32),
        cost_estimate=cost(5e5 * codes.size, 4 * codes.size),
        name="count",
    )(codes[:, None, :])


def frame_kernel(place_ref, clips_ref, bounds_ref, project, matrices, fsq_pair, gain_pair, first_conv, mid_conv, last_conv, head_map, lane_ref, slab_ref, turned_s):
    lanes = lane_ref.shape[1]
    clips = clips_ref[...].astype(F32)
    number = clips.shape[1]
    column = lax.broadcasted_iota(jnp.int32, (number, number), 1)
    row = lax.broadcasted_iota(jnp.int32, (number, number), 0)
    first = jnp.sum(jnp.where(column < row, clips, 0.0), axis=1, keepdims=True)
    size = jnp.sum(jnp.where(column == row, clips, 0.0), axis=1, keepdims=True)
    frame = (place_ref[0] + lax.broadcasted_iota(jnp.int32, (1, lanes), 1) // 16).astype(F32)
    mine = (first <= frame) & (frame < first + size)
    weight = 1.0 / jnp.sum(jnp.where(mine, size, 0.0), axis=0, keepdims=True)
    frames = bounds_ref.shape[1]
    spread = lax.broadcasted_iota(jnp.int32, (frames, lanes), 1) // 16
    spread = low(jnp.where(spread == lax.broadcasted_iota(jnp.int32, (frames, lanes), 0), 1.0, 0.0))
    extents = nn(low(bounds_ref[...].astype(F32)), spread)
    height, width = extents[0:1, :], extents[1:2, :]
    lane_ref[0:1, :] = height
    lane_ref[1:2, :] = width
    lane_ref[2:3, :] = weight
    lane_ref[3:8, :] = jnp.zeros((5, lanes), F32)
    total = jnp.sum(height * width * weight * (3.0 / 16.0), axis=1, keepdims=True)
    for index in range(2):
        slab_ref[48 * index : 48 * index + 48, :] = low(project[index])
    for index in range(4):
        slab_ref[96 + 16 * index : 112 + 16 * index, :] = low(matrices[index])
    slab_ref[160:224, 0:128] = low(mid_conv[0:64, :])
    slab_ref[160:224, 128:256] = low(mid_conv[64:128, :])
    slab_ref[224:240, 0:128] = low(last_conv[...])
    turned_s[...] = jnp.zeros_like(turned_s)
    for index in range(2):
        for digit in range(6):
            turned_s[16 * index + digit : 16 * index + digit + 1, :] = fsq_pair[digit, index : index + 1, :]
    turned_s[32:33, :] = head_map[...]
    turned_s[33:35, :] = gain_pair[...]
    turned_s[48:96, 0:4] = first_conv[...].T
    upper = low(total).astype(F32)
    rest = total - upper
    middle = low(rest).astype(F32)
    for index, item in enumerate((upper, middle, rest - middle)):
        turned_s[96 + index : 97 + index, 0:1] = item
    slab_ref[224:240, 128:256] = low(turned_s[...].T)


def frame_lanes(first, clip_frames, frame_bounds, masters):
    lanes = frame_bounds.shape[0] * 16
    clips = clip_frames.reshape(1, -1)
    bounds = frame_bounds.T
    operands = list(masters)
    operands[2] = operands[2].transpose(2, 0, 1)
    operands[4] = operands[4].T
    operands[6] = operands[6].T
    operands[7] = operands[7][None, :]
    return pl.pallas_call(
        frame_kernel,
        in_specs=[pl.BlockSpec(memory_space=pltpu.SMEM)] + [pl.BlockSpec(memory_space=pltpu.VMEM)] * 10,
        out_specs=[pl.BlockSpec(memory_space=pltpu.VMEM)] * 2,
        out_shape=[jax.ShapeDtypeStruct((8, lanes), F32), jax.ShapeDtypeStruct((SLAB_ROWS, 256), BF16)],
        scratch_shapes=[pltpu.VMEM((128, 16), F32)],
        name="frames",
    )(first.reshape(1), clips, bounds, *operands)


def passed_along(x, axis, by):
    size = lax.axis_size(axis)
    pairs = [(i, i + by) for i in range(size) if 0 <= i + by < size]
    return lax.ppermute(x, axis, pairs)


def neighbours(rows, grp, bands):
    last = rows.shape[1] - 1
    if bands == 2:
        got = swap(lax.dynamic_index_in_dim(rows, jnp.where(grp == 0, last, 0), 1, keepdims=False), "grp", 1)
        return got, got
    return passed_along(rows[:, 0], "grp", -1), passed_along(rows[:, last], "grp", 1)


def swap(x, axis, bits):
    return lax.ppermute(x, axis, [(i, i ^ bits) for i in range(lax.axis_size(axis))])


def sum_all(x, axis):
    bits, size = 1, lax.axis_size(axis)
    while bits < size:
        x = x + swap(x, axis, bits)
        bits *= 2
    return x


def gather_slabs(slab, beside):
    gathered = slab[None]
    for bits, item in zip((8, 4, 2), beside):
        got = swap(gathered, "dp", bits)
        if item is not None:
            got, _ = lax.optimization_barrier((got, item))
        gathered = jnp.concatenate([gathered, got], axis=0)
    return gathered, swap(gathered, "dp", 1)


def scalar_places(shape):
    row = lax.broadcasted_iota(jnp.int32, shape, 1)
    lane = lax.broadcasted_iota(jnp.int32, shape, 2)
    return row, (row >= 80) & (row < 83) & (lane >= 128)


def going(summed, scalars):
    if scalars:
        row, held = scalar_places(summed.shape)
        upper = lax.reduce_precision(summed, 8, 7)
        middle = lax.reduce_precision(summed - upper, 8, 7)
        parts = jnp.where(row == 81, summed - upper, jnp.where(row == 82, (summed - upper) - middle, summed))
        summed = jnp.where(held, parts, summed)
    return low(summed)


def coming(got, scalars):
    got = got.astype(F32)
    if scalars:
        _, held = scalar_places(got.shape)
        whole = (got[:, 80:81] + got[:, 81:82]) + got[:, 82:83]
        got = jnp.where(held, jnp.broadcast_to(whole, got.shape), got)
    return got


def split(summed):
    half = summed.shape[0] // 2
    return summed[:half], summed[half:]


def reduce_both(auto_keep, auto_got, judge_send, judge_keep):
    judge_got = swap(judge_send, "dp", 1)
    auto_got, judge_got = lax.optimization_barrier((auto_got, judge_got))
    auto_keep, auto_send = split(auto_keep + coming(auto_got, False))
    judge_keep, judge_send = split(judge_keep + judge_got)
    auto_got = swap(going(auto_send, False), "dp", 4)
    judge_got = swap(going(judge_send, True), "dp", 2)
    auto_got, judge_got = lax.optimization_barrier((auto_got, judge_got))
    auto_keep, auto_send = split(auto_keep + coming(auto_got, False))
    judge_keep, judge_send = split(judge_keep + coming(judge_got, True))
    auto_got = swap(auto_send, "dp", 8)
    judge_got = swap(going(judge_send, True), "dp", 4)
    auto_got, judge_got = lax.optimization_barrier((auto_got, judge_got))
    auto_keep = auto_keep + auto_got
    judge_keep, judge_send = split(judge_keep + coming(judge_got, True))
    auto_got = swap(auto_keep, "grp", 1)
    judge_got = swap(judge_send, "dp", 8)
    auto_got, judge_got = lax.optimization_barrier((auto_got, judge_got))
    judge_keep = judge_keep + judge_got
    judge_got = swap(judge_keep, "grp", 1)
    return auto_keep[0] + auto_got[0], judge_keep[0] + judge_got[0]


def unpack_auto(total):
    project = total[:96].reshape(2, 48, 256)
    matrices = total[96:160].reshape(4, 16, 256)
    fsq_pair = jnp.stack([total[160:176, 0:6], total[160:176, 128:134]])
    gain_pair = jnp.stack([jnp.sum(total[176:192, 0:128], axis=1), jnp.sum(total[176:192, 128:256], axis=1)])
    return project, matrices, fsq_pair, gain_pair


def unpack_judge_grads(total):
    mid = jnp.concatenate([total[:64, :128], total[:64, 128:]], axis=0)
    head = jnp.sum(total[64:80, 0:128], axis=1)
    last = total[64:80, 128:256].T
    first = total[80:84, 0:48].T
    return first, mid, last, head


def whole_slabs(first, clip_frames, frame_bounds, masters):
    gathered = [lax.all_gather(item, "dp", axis=axis, tiled=True) for item, axis in zip(masters, AXES)]

    def share(array, axis, number):
        size = array.shape[axis] // SLABS
        return lax.slice_in_dim(array, number * size, number * size + size, axis=axis)

    slabs = []
    for number in range(SLABS):
        shares = [share(item, axis, number) for item, axis in zip(gathered, AXES)]
        lane_info, slab = frame_lanes(first, clip_frames, frame_bounds, shares)
        slabs.append(slab)
    held = slabs[0][224, 224:227].astype(F32)
    total = lax.psum(held[0] + held[1] + held[2], "dp")
    upper = low(total)
    middle = low(total - upper.astype(F32))
    lower = low(total - upper.astype(F32) - middle.astype(F32))
    parts = jnp.stack([upper, middle, lower])
    slabs = [slab.at[224, 224:227].set(parts if number == 0 else 0) for number, slab in enumerate(slabs)]
    return lane_info, tuple(jnp.stack([slabs[value ^ core] for value in VALUES]) for core in range(2))


def whole_grads(auto, judge):
    def ordered(send, keep):
        pieces = [None] * SLABS
        for place, value in enumerate(VALUES):
            pieces[value] = keep[place]
            pieces[value ^ 1] = send[place].astype(F32)
        return pieces

    shares = [
        unpack_auto(left) + unpack_judge_grads(right) for left, right in zip(ordered(*auto), ordered(*judge))
    ]
    totals = []
    for index, axis in enumerate(AXES):
        whole = jnp.concatenate([share[index] for share in shares], axis=axis)
        totals.append(lax.psum_scatter(whole, "dp", scatter_dimension=axis, tiled=True))
    scalars = judge[1][0, 80, 128:132]
    totals.append(lax.psum(scalars, "dp"))
    return lax.psum(tuple(totals), "grp")


def adamw(master, moment, square, grad, rate, decay):
    new_moment = BETA_ONE * moment + (1.0 - BETA_ONE) * grad
    new_square = BETA_TWO * square + (1.0 - BETA_TWO) * grad * grad
    update = (
        new_moment
        / (1.0 - BETA_ONE**STEP)
        / (jnp.sqrt(new_square / (1.0 - BETA_TWO**STEP)) + ADAM_EPS)
    )
    return (new_moment, new_square, master - rate * (update + decay * master))


def constants():
    products = np.cumprod((1,) + LEVELS)[:6]
    rows = np.zeros((5, 16), np.float32)
    rows[1] = 1.0
    rows[2] = 1.0
    rows[0, :6] = 1.0 / products
    rows[1, :6] = LEVELS
    rows[2, :6] = 1.0 / np.array(LEVELS)
    rows[3, :6] = HALVES
    rows[4, :6] = 1.0 / np.array(HALVES)
    consts = np.broadcast_to(rows.reshape(80, 1), (80, 128)).astype(np.float32)
    places = np.arange(768)
    down = places // 48 // 4 * 4 + places % 48 // 12
    across = places // 48 % 4 * 4 + places % 48 % 12 // 3
    spots = np.broadcast_to(np.stack([down, across])[:, :, None], (2, 768, 128)).astype(np.float32)
    return jnp.asarray(consts), jnp.asarray(spots)


def on_device(pixels, frame_bounds, clip_frames, codes, *states):
    masters, moments, squares = states[:8], states[8:16], states[16:24]
    frames, band = pixels.shape[:2]
    grp, bands = lax.axis_index("grp"), lax.axis_size("grp")
    me, parts = lax.axis_index("dp"), lax.axis_size("dp")
    shared = parts == SLABS
    positions = frames * 16
    count_all = float(frames * parts * 256)

    code_halos = neighbours(codes, grp, bands)
    code_rows = codes.transpose(1, 0, 2).reshape(band, positions).astype(F32)
    counts = count_codes(code_rows)
    both_counts = counts + swap(counts, "grp", 1) if bands == 2 else lax.psum(counts, "grp")
    halos = neighbours(pixels, grp, bands)
    if shared:
        lane_info, slab = frame_lanes(me * frames, clip_frames, frame_bounds, masters)
        slabs = gather_slabs(slab, (counts, None, (code_halos, both_counts)))
    else:
        lane_info, slabs = whole_slabs(me * frames, clip_frames, frame_bounds, masters)
    counts = lax.psum(both_counts, "dp")

    places = jnp.stack(
        [grp * band, (grp < bands - 1).astype(jnp.int32), (grp > 0).astype(jnp.int32), me if shared else jnp.int32(0)]
    ).astype(jnp.int32)
    above, under = (item.reshape(1, positions).astype(F32) for item in (code_halos[1], code_halos[0]))
    all_codes = jnp.concatenate([above, code_rows, under], axis=0)
    extra = (all_codes, lane_info, *constants())

    fake_outs = run_fake(pixels, places, slabs, extra, count_all)
    halos, counts, fake_outs = lax.optimization_barrier((halos, counts, fake_outs))
    auto, starts = fake_outs[:2], fake_outs[2:7]
    if shared:
        auto_send, auto_keep = auto
        auto_keep, auto_send = split(auto_keep + swap(auto_send, "dp", 1))
        got = swap(going(auto_send, False), "dp", 2)
    judge = run_real(pixels, halos, places, slabs, starts, count_all)
    if shared:
        got, judge = lax.optimization_barrier((got, judge))
        auto_total, judge_total = reduce_both(auto_keep, got, *judge)
        totals = (*unpack_auto(auto_total), *unpack_judge_grads(judge_total))
        losses = judge_total[80, 128:132]
    else:
        *totals, losses = whole_grads(auto, judge)

    shares = counts * (1.0 / count_all)
    perplexity = jnp.exp(-jnp.sum(jax.scipy.special.xlogy(shares, shares)))
    results = [
        adamw(
            masters[number],
            moments[number],
            squares[number],
            totals[number],
            RATE_GAIN if number == 3 else RATE_MATRIX,
            0.0 if number == 3 else DECAY,
        )
        for number in range(8)
    ]
    return (
        *(result[0] for result in results),
        *(result[1] for result in results),
        *(result[2] for result in results),
        losses[0:2],
        losses[2:4],
        perplexity,
    )


def solution(mesh):
    states = (
        P(None, "dp", None),
        P(None, "dp", None),
        P(None, "dp", None),
        P(None, "dp"),
        P(None, "dp"),
        P("dp", None),
        P(None, "dp"),
        P("dp"),
    )
    return jax.shard_map(
        on_device,
        mesh=mesh,
        in_specs=(P("dp", "grp", None, None), P("dp", None), P(), P("dp", "grp", None)) + states * 3,
        out_specs=states * 3 + (P(), P(), P()),
        check_vma=False,
    )
```
